32 devices in a mesh: dp: 4 (over z), fsdp: 8 (over y, x, core).
Axes of the slice: x: 2, y: 2, z: 4, core: 2. Of those that a mesh axis runs over, the one named last changes fastest.
Arguments:
- layer_input: bfloat16 [8192, 8192], P('dp', 'fsdp'), may hold values from -6 to 6
- cotangent: bfloat16 [2, 8192, 1024], P(None, ('dp', 'fsdp')), may hold values from -6 to 6
- candidates: bfloat16 [2, 4, 1024, 512], P(None, 'dp', None, 'fsdp'), may hold values from -0.1875 to 0.1875
- moment_first: float32 [2, 512, 8192], P(None, 'dp', 'fsdp'), may hold values from -0.6 to 0.6
- moment_second: float32 [2, 512, 8192], P(None, 'dp', 'fsdp'), may hold values from 0.0001 to 0.01
- owners: int32 [2], replicated, may hold values from 0 to 3
Outputs:
- update: bfloat16 [2, 1024, 8192], P(None, 'dp', 'fsdp')
- first_next: float32 [2, 512, 8192], P(None, 'dp', 'fsdp')
- second_next: float32 [2, 512, 8192], P(None, 'dp', 'fsdp')
The draws below stay inside these ranges and needn't reach their ends.
Inputs may be any that keep to these rules, and one draw needn't show every extreme that they name: owners[m] names a data-parallel replica.
All inputs are finite; a program needn't handle non-finite values.
Results may differ from the reference program's by a relative error of at most 0.0056.
Values may be sent and summed in bfloat16 or wider, within the bound.
No kernel may reach another device: no remote copies, remote signals or barrier semaphores. Data moves between devices by JAX's collectives and lax.ppermute only.
A program may use at most 64 MiB of HBM per device.

```python
import math
import jax
import jax.numpy as jnp
from jax import lax

D = 8192
KV = 1024
RANK = 512
MATS = 2
STEP = 10
TOKENS = 8192
N_DP = 4


def shard_levels(stream_key, shape, pieces, least, high):
    level = 1.0
    for axis_at, blocks in pieces:
        steps = jax.random.uniform(jax.random.fold_in(jax.random.fold_in(stream_key, 6), axis_at), (blocks,), jnp.float32, least / len(pieces), high / len(pieces))
        level = level * jnp.repeat(jnp.exp(steps), shape[axis_at] // blocks).reshape((-1,) + (1,) * (len(shape) - 1 - axis_at))
    return level


def centred(own_key, dims, scale, bound, shards=(), dtype=jnp.bfloat16):
    result = scale * jax.random.normal(own_key, dims, jnp.float32)
    if shards:
        result = result * shard_levels(own_key, dims, shards, -0.22, 0.18)
    return jnp.clip(result, -bound, bound).astype(dtype)


def setup_inputs(seed: int = 0) -> dict:
    splits = jax.random.split(jax.random.key(seed), 7)
    return {
        "layer_input": centred(splits[0], (TOKENS, D), 1.0, 6.0, ((0, 4), (1, 8))),
        "cotangent": centred(splits[1], (MATS, TOKENS, KV), 1.0, 6.0, ((1, 32),)),
        "candidates": centred(splits[2], (MATS, N_DP, KV, RANK), KV ** -0.5, 0.1875, ((1, 4), (3, 8))),
        "moment_first": centred(splits[3], (MATS, RANK, D), 0.1, 0.6, ((1, 4), (2, 8)), jnp.float32),
        "moment_second": jnp.clip(jnp.exp(math.log(0.01) - 4.6051702 * jax.random.uniform(splits[4], (MATS, RANK, D), jnp.float32) ** shard_levels(splits[4], (MATS, RANK, D), ((1, 4), (2, 8)), -0.2, 0.2)), 0.0001, 0.01),
        "owners": jax.random.randint(splits[5], (MATS,), 0, N_DP).astype(jnp.int32),
    }


beta_first = 0.9
beta_second = 0.999
epsilon = 1e-08

def reference(layer_input, cotangent, candidates, moment_first, moment_second, owners):
    inverse_root = 1.0 / jnp.sqrt(jnp.asarray(TOKENS, jnp.float32))
    updates = []
    firsts = []
    seconds = []
    for matrix in range(MATS):
        projector = lax.dynamic_index_in_dim(candidates[matrix], owners[matrix], 0, keepdims=False)
        head_rows = jnp.dot(cotangent[matrix], projector, preferred_element_type=jnp.float32).astype(jnp.bfloat16)
        projected = lax.dot_general(head_rows, layer_input, (((0,), (0,)), ((), ())), preferred_element_type=jnp.float32) * inverse_root
        first = beta_first * moment_first[matrix] + (1.0 - beta_first) * projected
        second = beta_second * moment_second[matrix] + (1.0 - beta_second) * projected * projected
        direction = first / (1.0 - beta_first ** STEP) / (jnp.sqrt(second / (1.0 - beta_second ** STEP)) + epsilon)
        direction = direction.astype(jnp.bfloat16)
        updates.append(jnp.dot(projector, direction, preferred_element_type=jnp.float32).astype(jnp.bfloat16))
        firsts.append(first)
        seconds.append(second)
    return (jnp.stack(updates), jnp.stack(firsts), jnp.stack(seconds))
```

```python
import functools
import math

import jax
import jax.numpy as jnp
from jax import lax
from jax.experimental import pallas as pl
from jax.experimental.pallas import tpu as pltpu
from jax.sharding import PartitionSpec as P

MATS = 2
STEP = 10

beta_first = 0.9
beta_second = 0.999
epsilon = 1e-08

TRANSPOSED = (((0,), (0,)), ((), ()))
MIB = 1 << 20


def swap(value, axis, mask):
    size = lax.axis_size(axis)
    return lax.ppermute(value, axis, [(i, i ^ mask) for i in range(size)])


def bits_of(size):
    return [1 << k for k in range(size.bit_length() - 1)]


def spread(block, bits):
    if len(bits) == 2:
        low, high = bits
        half = block.shape[0] // 2
        by_low = swap(block, "fsdp", low)
        by_high = swap(block, "fsdp", high)
        upper = swap(by_low[:half], "fsdp", high)
        lower = swap(by_high[half:], "fsdp", low)
        return {
            0: block,
            low: by_low,
            high: by_high,
            low | high: jnp.concatenate([upper, lower], axis=0),
        }
    blocks = {0: block}
    for bit in bits:
        blocks.update({mask ^ bit: swap(held, "fsdp", bit) for mask, held in list(blocks.items())})
    return blocks


def tile_of(size):
    return min(size, 256)


def product_body(count, first, places, *refs):
    blocks, inputs = refs[:count], refs[count : 2 * count]
    total = None if first else refs[2 * count][...]
    for block, rows in zip(blocks, inputs):
        term = lax.dot_general(
            block[...], rows[...], TRANSPOSED, preferred_element_type=jnp.float32
        )
        total = term if total is None else total + term
    refs[-1][...] = total


def add_products(blocks, places, layer_input, total=None):
    count = len(blocks)
    rows, kv = blocks[0].shape
    width = layer_input.shape[1]
    tile = tile_of(kv)
    in_specs = [pl.BlockSpec((rows, tile), lambda i, places: (0, i))] * count
    in_specs += [
        pl.BlockSpec((rows, width), functools.partial(lambda k, i, places: (places[k], 0), k))
        for k in range(count)
    ]
    operands = list(blocks) + [layer_input] * count
    if total is not None:
        in_specs.append(pl.BlockSpec((tile, width), lambda i, places: (i, 0)))
        operands.append(total)
    return pl.pallas_call(
        functools.partial(product_body, count, total is None),
        grid_spec=pltpu.PrefetchScalarGridSpec(
            num_scalar_prefetch=1,
            grid=(kv // tile,),
            in_specs=in_specs,
            out_specs=pl.BlockSpec((tile, width), lambda i, places: (i, 0)),
        ),
        out_shape=jax.ShapeDtypeStruct((kv, width), jnp.float32),
        compiler_params=pltpu.CompilerParams(vmem_limit_bytes=32 * MIB),
        cost_estimate=pl.CostEstimate(
            flops=2 * count * rows * kv * width,
            bytes_accessed=2 * count * rows * (kv + width) + 8 * kv * width,
            transcendentals=0,
        ),
    )(places, *operands)


def project_body(count, scale, places, *refs):
    blocks, inputs = refs[:count], refs[count : 2 * count]
    partial, projector, send, keep, held = refs[2 * count :]
    step = pl.program_id(0)
    total = partial[...]
    for block, rows in zip(blocks, inputs):
        total += lax.dot_general(
            block[...], rows[...], TRANSPOSED, preferred_element_type=jnp.float32
        )
    term = jnp.dot(
        projector[...], total.astype(jnp.bfloat16), preferred_element_type=jnp.float32
    )

    @pl.when(step == 0)
    def _():
        held[...] = term

    @pl.when(step > 0)
    def _():
        held[...] += term

    @pl.when(step == pl.num_programs(0) - 1)
    def _():
        half = send.shape[0]
        send[...] = (held[:half] * scale).astype(send.dtype)
        keep[...] = held[half:] * scale


def project(blocks, places, layer_input, partial, projector, scale):
    count = len(blocks)
    rows, kv = blocks[0].shape
    width = layer_input.shape[1]
    rank = projector.shape[0]
    tile = tile_of(kv)
    in_specs = [pl.BlockSpec((rows, tile), lambda i, places: (0, i))] * count
    in_specs += [
        pl.BlockSpec((rows, width), functools.partial(lambda k, i, places: (places[k], 0), k))
        for k in range(count)
    ]
    in_specs += [
        pl.BlockSpec((tile, width), lambda i, places: (i, 0)),
        pl.BlockSpec((rank, tile), lambda i, places: (0, i)),
    ]
    half = pl.BlockSpec((rank // 2, width), lambda i, places: (0, 0))
    return pl.pallas_call(
        functools.partial(project_body, count, scale),
        grid_spec=pltpu.PrefetchScalarGridSpec(
            num_scalar_prefetch=1,
            grid=(kv // tile,),
            in_specs=in_specs,
            out_specs=[half, half],
            scratch_shapes=[pltpu.VMEM((rank, width), jnp.float32)],
        ),
        out_shape=[
            jax.ShapeDtypeStruct((rank // 2, width), jnp.bfloat16),
            jax.ShapeDtypeStruct((rank // 2, width), jnp.float32),
        ],
        compiler_params=pltpu.CompilerParams(vmem_limit_bytes=32 * MIB),
        cost_estimate=pl.CostEstimate(
            flops=2 * count * rows * kv * width + 2 * rank * kv * width,
            bytes_accessed=2 * count * rows * (kv + width) + 4 * kv * width,
            transcendentals=0,
        ),
    )(places, *blocks, *([layer_input] * count), partial, projector)


def on_device(layer_input, cotangent, candidates, moment_first, moment_second, owners):
    replicas = lax.axis_size("dp")
    members = lax.axis_size("fsdp")
    me_dp = lax.axis_index("dp")
    me_fsdp = lax.axis_index("fsdp")
    dp_bits = bits_of(replicas)
    far_bits = bits_of(members)[1:]
    scale = 1.0 / math.sqrt(layer_input.shape[0] * replicas)
    kv = candidates.shape[2]
    kv_share = kv // replicas
    rank_share = moment_first.shape[1]

    order = [0]
    for bit in reversed(dp_bits):
        order = [mask ^ bit for mask in order] + order

    def owned(matrix):
        value = candidates[matrix, 0].T
        for bit in reversed(dp_bits):
            other = swap(value, "dp", bit)
            mine = (me_dp & bit) == (owners[matrix] & bit)
            value = jnp.where(mine, value, other)
        return value

    def assembled(value):
        blocks = spread(value, far_bits)
        masks = sorted(blocks)
        same = jnp.concatenate([blocks[mask] for mask in masks], axis=0)
        other = swap(same, "fsdp", 1)
        count = value.shape[0]
        both = jnp.concatenate([same, other], axis=0)
        rows = []
        per = members // replicas
        for mask in order:
            for sub in range(per):
                member = (me_dp ^ mask) * per + sub
                away = member ^ me_fsdp
                slot = (away >> 1) + (away & 1) * len(masks)
                rows.append(lax.dynamic_slice_in_dim(both, slot * count, count, 0))
        return jnp.concatenate(rows, axis=0)

    sends, keeps, projectors = [], [], []
    for matrix in range(MATS):
        own = cotangent[matrix]
        blocks = spread(own, far_bits)
        last = max(blocks)
        early = {mask: held for mask, held in blocks.items() if mask != last}
        early.update({mask ^ 1: swap(held, "fsdp", 1) for mask, held in early.items()})
        late = {last: blocks[last], last ^ 1: swap(blocks[last], "fsdp", 1)}
        projector = assembled(owned(matrix))
        partial = add_products(
            list(early.values()), jnp.stack([me_fsdp ^ mask for mask in early]), layer_input
        )
        send, keep = project(
            list(late.values()),
            jnp.stack([me_fsdp ^ mask for mask in late]),
            layer_input,
            partial,
            projector,
            scale,
        )
        sends.append(send)
        keeps.append(keep)
        projectors.append(projector)

    updates, firsts, seconds = [], [], []
    for matrix in range(MATS):
        send, keep = sends[matrix], keeps[matrix]
        for bit in dp_bits:
            total = keep + swap(send, "dp", bit).astype(jnp.float32)
            half = total.shape[0] // 2
            if half >= rank_share:
                send, keep = total[:half].astype(jnp.bfloat16), total[half:]
        projected = total
        first = beta_first * moment_first[matrix] + (1.0 - beta_first) * projected
        second = beta_second * moment_second[matrix] + (1.0 - beta_second) * projected * projected
        direction = (
            first
            / (1.0 - beta_first**STEP)
            / (jnp.sqrt(second / (1.0 - beta_second**STEP)) + epsilon)
        )
        direction = direction.astype(jnp.bfloat16)
        for bit in reversed(dp_bits):
            direction = jnp.concatenate([swap(direction, "dp", bit), direction], axis=0)
        own = lax.dynamic_slice_in_dim(projectors[matrix], me_dp * kv_share, kv_share, 1)
        update = lax.dot_general(own, direction, TRANSPOSED, preferred_element_type=jnp.float32)
        updates.append(update.astype(jnp.bfloat16))
        firsts.append(first)
        seconds.append(second)
    return (jnp.stack(updates), jnp.stack(firsts), jnp.stack(seconds))


def solution(mesh):
    placed = (
        P("dp", "fsdp"),
        P(None, ("dp", "fsdp"), None),
        P(None, "dp", None, "fsdp"),
        P(None, "dp", "fsdp"),
        P(None, "dp", "fsdp"),
        P(),
    )
    return jax.shard_map(
        on_device,
        mesh=mesh,
        in_specs=placed,
        out_specs=(P(None, "dp", "fsdp"), P(None, "dp", "fsdp"), P(None, "dp", "fsdp")),
        check_vma=False,
    )
```

```python
import functools
import math

import jax
import jax.numpy as jnp
from jax import lax
from jax.experimental import pallas as pl
from jax.experimental.pallas import tpu as pltpu
from jax.sharding import PartitionSpec as P

MATS = 2
STEP = 10

beta_first = 0.9
beta_second = 0.999
epsilon = 1e-08

TRANSPOSED = (((0,), (0,)), ((), ()))
MIB = 1 << 20


def swap(value, axis, mask):
    size = lax.axis_size(axis)
    return lax.ppermute(value, axis, [(i, i ^ mask) for i in range(size)])


def bits_of(size):
    return [1 << k for k in range(size.bit_length() - 1)]


def after(value, *others):
    return lax.optimization_barrier((value,) + others)[0]


def spread(block, bits):
    if len(bits) == 2:
        low, high = bits
        masks = (0, low, high, low | high)
        return {mask: swap(block, "fsdp", mask) if mask else block for mask in masks}
    blocks = {0: block}
    for bit in bits:
        blocks.update({mask ^ bit: swap(held, "fsdp", bit) for mask, held in list(blocks.items())})
    return blocks


def spread_near(block, bits):
    if len(bits) == 2:
        low, high = bits
        half = block.shape[0] // 2
        top, bottom = block[:half], block[half:]
        low_top, high_bottom = swap(top, "fsdp", low), swap(bottom, "fsdp", high)
        far = [swap(low_top, "fsdp", high), swap(high_bottom, "fsdp", low)]
        by_low = [low_top, swap(after(bottom, low_top), "fsdp", low)]
        by_high = [swap(after(top, high_bottom), "fsdp", high), high_bottom]
        first = [low_top, high_bottom]
        return {0: [block], low: by_low, high: by_high}, {low | high: far}, first
    blocks = {mask: [held] for mask, held in spread(block, bits).items()}
    last = max(blocks)
    near = {mask: held for mask, held in blocks.items() if mask != last}
    return near, {last: blocks[last]}, []


def with_partner(blocks, own=None):
    other = {
        mask ^ 1: [own] if mask == 0 and own is not None else [swap(x, "fsdp", 1) for x in held]
        for mask, held in blocks.items()
    }
    return {**blocks, **other}


def tile_of(size):
    return min(size, 256)


def whole(shape):
    return pl.BlockSpec(shape, lambda *_: (0,) * len(shape))


def gather_body(order, per, count, here, same, other, full):
    spot = 0
    for mask in order:
        for sub in range(per):
            away = ((here[0] ^ mask) * per + sub) ^ here[1]
            at = pl.multiple_of((away >> 1) * count, count)
            rows = jnp.where(
                (away & 1) == 0, same[pl.ds(at, count), :], other[pl.ds(at, count), :]
            )
            full[pl.ds(spot * count, count), :] = rows
            spot += 1


def gather_projector(same, other, here, order, per):
    rows, kv = same.shape
    count = 2 * rows // (len(order) * per)
    return pl.pallas_call(
        functools.partial(gather_body, order, per, count),
        grid_spec=pltpu.PrefetchScalarGridSpec(
            num_scalar_prefetch=1,
            grid=(1,),
            in_specs=[whole((rows, kv))] * 2,
            out_specs=whole((2 * rows, kv)),
        ),
        out_shape=jax.ShapeDtypeStruct((2 * rows, kv), same.dtype),
        compiler_params=pltpu.CompilerParams(vmem_limit_bytes=24 * MIB),
        cost_estimate=pl.CostEstimate(flops=0, bytes_accessed=8 * rows * kv, transcendentals=0),
    )(here, same, other)


def block_term(block, rows, here, mask, tile):
    pieces = [piece[:, tile] for piece in block]
    left = pieces[0] if len(pieces) == 1 else jnp.concatenate(pieces, axis=0)
    count = left.shape[0]
    start = pl.multiple_of((here[1] ^ mask) * count, count)
    return lax.dot_general(
        left, rows[pl.ds(start, count), :], TRANSPOSED, preferred_element_type=jnp.float32
    )


def regroup(refs, shape):
    refs = list(refs)
    return [[refs.pop(0) for _ in range(length)] for length in shape]


def call_in_vmem(body, here, operands, outputs, flops, cost=1.0):
    moved = sum(x.size * x.dtype.itemsize for x in list(operands) + list(outputs))
    return pl.pallas_call(
        body,
        grid_spec=pltpu.PrefetchScalarGridSpec(
            num_scalar_prefetch=1,
            grid=(),
            in_specs=[pl.BlockSpec(memory_space=pltpu.VMEM)] * len(operands),
            out_specs=[pl.BlockSpec(memory_space=pltpu.VMEM)] * len(outputs),
        ),
        out_shape=outputs,
        compiler_params=pltpu.CompilerParams(vmem_limit_bytes=32 * MIB),
        cost_estimate=pl.CostEstimate(
            flops=int(flops * cost), bytes_accessed=moved, transcendentals=0
        ),
    )(here, *operands)


def flat(blocks):
    return [piece for block in blocks.values() for piece in block]


def depth(blocks):
    return sum(piece.shape[0] for piece in flat(blocks))


def heads_body(masks, shape, part, scale, here, *refs):
    groups = regroup(refs[: sum(shape)], shape)
    rows, outs = refs[sum(shape)], refs[sum(shape) + 1 :]
    size = outs[0].shape[0] * len(outs)
    total = None
    for mask, block in zip(masks, groups):
        term = block_term(block, rows, here, mask, pl.ds(part * size, size))
        total = term if total is None else total + term
    for k, out in enumerate(outs):
        count = out.shape[0]
        out[...] = (total[k * count : (k + 1) * count] * scale).astype(out.dtype)


def heads_product(blocks, here, layer_input, part, pieces, dtype, scale):
    half = flat(blocks)[0].shape[1] // 2
    width = layer_input.shape[1]
    shape = [len(block) for block in blocks.values()]
    return call_in_vmem(
        functools.partial(heads_body, list(blocks), shape, part, scale),
        here,
        flat(blocks) + [layer_input],
        [jax.ShapeDtypeStruct((half // pieces, width), dtype)] * pieces,
        2 * depth(blocks) * half * width,
    )


def adam_body(aliased, keep, received, moment_first, moment_second, *refs):
    first_out, second_out, direction_out = refs[-3:]
    projected = keep[...] + received[...].astype(jnp.float32)
    first = beta_first * moment_first[0] + (1.0 - beta_first) * projected
    second = beta_second * moment_second[0] + (1.0 - beta_second) * projected * projected
    first_out[0] = first
    second_out[0] = second
    direction = (
        first
        / (1.0 - beta_first**STEP)
        / (jnp.sqrt(second / (1.0 - beta_second**STEP)) + epsilon)
    )
    direction_out[...] = direction.astype(direction_out.dtype)


def adam(matrix, keep, received, moment_first, moment_second, written):
    rows, width = keep.shape
    tile = tile_of(width)
    flat = pl.BlockSpec((rows, tile), lambda i: (0, i))
    deep = pl.BlockSpec((1, rows, tile), lambda i: (matrix, 0, i))
    in_specs = [flat, flat, deep, deep] + [pl.BlockSpec(memory_space=pl.ANY)] * len(written)
    return pl.pallas_call(
        functools.partial(adam_body, len(written)),
        grid=(width // tile,),
        in_specs=in_specs,
        out_specs=[deep, deep, flat],
        out_shape=[
            jax.ShapeDtypeStruct(moment_first.shape, jnp.float32),
            jax.ShapeDtypeStruct(moment_second.shape, jnp.float32),
            jax.ShapeDtypeStruct((rows, width), jnp.bfloat16),
        ],
        input_output_aliases={4 + k: k for k in range(len(written))},
        cost_estimate=pl.CostEstimate(
            flops=12 * rows * width, bytes_accessed=24 * rows * width, transcendentals=rows * width
        ),
    )(keep, received, moment_first, moment_second, *written)


def update_body(count, projector, *refs):
    out = refs[-1]
    rows = refs[0].shape[0]
    total = None
    for k in range(count):
        term = lax.dot_general(
            projector[pl.ds(k * rows, rows), :],
            refs[k][...],
            TRANSPOSED,
            preferred_element_type=jnp.float32,
        )
        total = term if total is None else total + term
    out[0] = total.astype(out.dtype)


def back_project(matrix, projector, directions, written):
    count = len(directions)
    rows, width = directions[0].shape
    rank, share = projector.shape
    tile = tile_of(width)
    in_specs = [whole((rank, share))]
    in_specs += [pl.BlockSpec((rows, tile), lambda i: (0, i))] * count
    in_specs += [pl.BlockSpec(memory_space=pl.ANY)] * len(written)
    return pl.pallas_call(
        functools.partial(update_body, count),
        grid=(width // tile,),
        in_specs=in_specs,
        out_specs=pl.BlockSpec((1, share, tile), lambda i: (matrix, 0, i)),
        out_shape=jax.ShapeDtypeStruct((MATS, share, width), jnp.bfloat16),
        input_output_aliases={1 + count + k: k for k in range(len(written))},
        cost_estimate=pl.CostEstimate(
            flops=2 * rank * share * width,
            bytes_accessed=2 * (rank + share) * width,
            transcendentals=0,
        ),
    )(projector, *directions, *written)


def product_body(masks, shape, here, *refs):
    groups = regroup(refs[: sum(shape)], shape)
    rows, out = refs[sum(shape) :]
    size = tile_of(out.shape[0])
    for at in range(0, out.shape[0], size):
        tile = pl.ds(at, size)
        total = None
        for mask, block in zip(masks, groups):
            term = block_term(block, rows, here, mask, tile)
            total = term if total is None else total + term
        out[tile, :] = total


def add_products(blocks, here, layer_input):
    kv = flat(blocks)[0].shape[1]
    width = layer_input.shape[1]
    shape = [len(block) for block in blocks.values()]
    return call_in_vmem(
        functools.partial(product_body, list(blocks), shape),
        here,
        flat(blocks) + [layer_input],
        [jax.ShapeDtypeStruct((kv, width), jnp.float32)],
        2 * depth(blocks) * kv * width,
        1.0,
    )[0]


def project_body(masks, shape, scale, here, *refs):
    groups = regroup(refs[: sum(shape)], shape)
    rows, partial, projector, product = refs[sum(shape) : sum(shape) + 4]
    outs = refs[sum(shape) + 4 :]
    size = tile_of(product.shape[0])
    for at in range(0, product.shape[0], size):
        tile = pl.ds(at, size)
        total = partial[tile, :]
        for mask, block in zip(masks, groups):
            total += block_term(block, rows, here, mask, tile)
        product[tile, :] = total.astype(product.dtype)
    apply_body(0, scale, here, projector, product, *outs)


def apply_body(first, scale, here, projector, product, *outs):
    size = outs[0].shape[0] * len(outs)
    term = jnp.dot(
        projector[pl.ds(first, size), :], product[...], preferred_element_type=jnp.float32
    )
    for k, out in enumerate(outs):
        count = out.shape[0]
        out[...] = (term[k * count : (k + 1) * count] * scale).astype(out.dtype)


def project(blocks, here, layer_input, partial, projector, pieces, scale):
    kv, width = partial.shape
    half = projector.shape[0] // 2
    shape = [len(block) for block in blocks.values()]
    product, *sends = call_in_vmem(
        functools.partial(project_body, list(blocks), shape, scale),
        here,
        flat(blocks) + [layer_input, partial, projector],
        [jax.ShapeDtypeStruct((kv, width), jnp.bfloat16)]
        + [jax.ShapeDtypeStruct((half // pieces, width), jnp.bfloat16)] * pieces,
        2 * depth(blocks) * kv * width + 2 * half * kv * width,
    )
    return product, sends


def apply_rest(projector, product, here, pieces, scale):
    half = projector.shape[0] // 2
    kv, width = product.shape
    return call_in_vmem(
        functools.partial(apply_body, half, scale),
        here,
        [projector, product],
        [jax.ShapeDtypeStruct((half // pieces, width), jnp.float32)] * pieces,
        2 * half * kv * width,
    )


def on_device(layer_input, cotangent, candidates, moment_first, moment_second, owners):
    replicas = lax.axis_size("dp")
    members = lax.axis_size("fsdp")
    me_dp = lax.axis_index("dp")
    me_fsdp = lax.axis_index("fsdp")
    dp_bits = bits_of(replicas)
    far_bits = bits_of(members)[1:]
    scale = 1.0 / math.sqrt(layer_input.shape[0] * replicas)
    kv_share = candidates.shape[2] // replicas
    per = members // replicas

    order = [0]
    for bit in reversed(dp_bits):
        order = [mask ^ bit for mask in order] + order

    here = jnp.stack([me_dp, me_fsdp]).astype(jnp.int32)

    def owned(matrix, value, *others):
        for at, bit in enumerate(dp_bits):
            if at == 1 and others:
                value = after(value, *others)
            other = swap(value, "dp", bit)
            mine = (me_dp & bit) == (owners[matrix] & bit)
            value = jnp.where(mine, value, other)
        return value

    def assembled(value, *others):
        blocks = spread(value, far_bits)
        same = jnp.concatenate([blocks[mask] for mask in sorted(blocks)], axis=0)
        other = swap(after(same, *others), "fsdp", 1)
        return gather_projector(same, other, here, order, per), same

    pieces = max(replicas // 2, 1)

    own_other = swap(cotangent[0], "fsdp", 1)
    near, far, arrived = spread_near(cotangent[0], far_bits)
    first_owned = owned(0, candidates[0, 0].T, own_other, *arrived)
    spread_first = flat(near) + [own_other]
    near_all = with_partner(near, own_other)
    projector_0, same_0 = assembled(after(first_owned, *spread_first), *flat(near_all))
    far_all = with_partner(far)
    partial = add_products(near_all, here, layer_input)
    product, send_0 = project(far_all, here, layer_input, partial, projector_0, pieces, scale)
    keep_0 = apply_rest(projector_0, product, here, pieces, scale)

    second_owned = owned(1, after(candidates[1, 0].T, first_owned))
    projector_1, _ = assembled(after(second_owned, same_0, *flat(far)))
    heads = lax.dot_general(
        cotangent[1], projector_1, (((1,), (1,)), ((), ())), preferred_element_type=jnp.float32
    ).astype(jnp.bfloat16)
    blocks = with_partner({mask: [held] for mask, held in spread(heads, far_bits).items()})
    send_1 = heads_product(blocks, here, layer_input, 0, pieces, jnp.bfloat16, scale)
    keep_1 = heads_product(blocks, here, layer_input, 1, pieces, jnp.float32, scale)

    def reduced(sends, keeps):
        for bit in dp_bits[:-1]:
            totals = [
                keep + swap(send, "dp", bit).astype(jnp.float32)
                for send, keep in zip(sends, keeps)
            ]
            half = len(totals) // 2
            sends = [total.astype(jnp.bfloat16) for total in totals[:half]]
            keeps = totals[half:]
        return keeps[0], swap(sends[0], "dp", dp_bits[-1])

    updates, moments = (), ()
    for matrix, sends, keeps, projector in (
        (0, send_0, keep_0, projector_0),
        (1, send_1, keep_1, projector_1),
    ):
        own = lax.dynamic_slice_in_dim(projector, me_dp * kv_share, kv_share, 1)
        keep, received = reduced(sends, keeps)
        first, second, direction = adam(
            matrix, keep, received, moment_first, moment_second, moments
        )
        moments = (first, second)
        directions = [direction]
        for bit in reversed(dp_bits):
            directions = [swap(piece, "dp", bit) for piece in directions] + directions
        updates = (back_project(matrix, own, directions, updates),)
    return updates + moments


def solution(mesh):
    placed = (
        P("dp", "fsdp"),
        P(None, ("dp", "fsdp"), None),
        P(None, "dp", None, "fsdp"),
        P(None, "dp", "fsdp"),
        P(None, "dp", "fsdp"),
        P(),
    )
    return jax.shard_map(
        on_device,
        mesh=mesh,
        in_specs=placed,
        out_specs=(P(None, "dp", "fsdp"), P(None, "dp", "fsdp"), P(None, "dp", "fsdp")),
        check_vma=False,
    )
```

```python
import functools
import math

import jax
import jax.numpy as jnp
from jax import lax
from jax.experimental import pallas as pl
from jax.experimental.pallas import tpu as pltpu
from jax.sharding import PartitionSpec as P

MATS = 2
STEP = 10

beta_first = 0.9
beta_second = 0.999
epsilon = 1e-08

TRANSPOSED = (((0,), (0,)), ((), ()))
MIB = 1 << 20


def swap(value, axis, mask):
    size = lax.axis_size(axis)
    return lax.ppermute(value, axis, [(i, i ^ mask) for i in range(size)])


def bits_of(size):
    return [1 << k for k in range(size.bit_length() - 1)]


def after(value, others, tokens):
    corners = [other[:16, :128] for other in others]
    value, *held = lax.optimization_barrier((value, *corners))
    tokens.extend(held)
    return value


def spread(block, bits):
    if len(bits) == 2:
        low, high = bits
        masks = (0, low, high, low | high)
        return {mask: swap(block, "fsdp", mask) if mask else block for mask in masks}
    blocks = {0: block}
    for bit in bits:
        blocks.update({mask ^ bit: swap(held, "fsdp", bit) for mask, held in list(blocks.items())})
    return blocks


def spread_near(block, bits, tokens):
    if len(bits) == 2:
        low, high = bits
        half = block.shape[0] // 2
        top, bottom = block[:half], block[half:]
        low_top, high_bottom = swap(top, "fsdp", low), swap(bottom, "fsdp", high)
        far = [swap(low_top, "fsdp", high), swap(high_bottom, "fsdp", low)]
        by_low = [low_top, swap(after(bottom, [low_top], tokens), "fsdp", low)]
        by_high = [swap(after(top, [high_bottom], tokens), "fsdp", high), high_bottom]
        first = [low_top, high_bottom]
        return {0: [block], low: by_low, high: by_high}, {low | high: far}, first
    blocks = {mask: [held] for mask, held in spread(block, bits).items()}
    last = max(blocks)
    near = {mask: held for mask, held in blocks.items() if mask != last}
    return near, {last: blocks[last]}, []


def with_partner(blocks, own=None):
    other = {
        mask ^ 1: [own] if mask == 0 and own is not None else [swap(x, "fsdp", 1) for x in held]
        for mask, held in blocks.items()
    }
    return {**blocks, **other}


def tile_of(size):
    return min(size, 256)


def whole(shape):
    return pl.BlockSpec(shape, lambda *_: (0,) * len(shape))


def gather_body(order, per, count, here, same, other, *refs):
    outs = refs[-MATS:]
    for matrix, out in enumerate(outs):
        spot = 0
        for mask in order:
            for sub in range(per):
                away = ((here[0] ^ mask) * per + sub) ^ here[1]
                at = pl.multiple_of(((away >> 1) * MATS + matrix) * count, count)
                out[pl.ds(spot * count, count), :] = jnp.where(
                    (away & 1) == 0, same[pl.ds(at, count), :], other[pl.ds(at, count), :]
                )
                spot += 1


def gather_projector(same, other, here, order, per, tokens):
    rows, kv = same.shape
    rank = 2 * rows // MATS
    return pl.pallas_call(
        functools.partial(gather_body, order, per, rank // (len(order) * per)),
        grid_spec=pltpu.PrefetchScalarGridSpec(
            num_scalar_prefetch=1,
            grid=(1,),
            in_specs=[whole((rows, kv))] * 2
            + [pl.BlockSpec(memory_space=pl.ANY)] * len(tokens),
            out_specs=[whole((rank, kv))] * MATS,
        ),
        out_shape=[jax.ShapeDtypeStruct((rank, kv), same.dtype)] * MATS,
        compiler_params=pltpu.CompilerParams(vmem_limit_bytes=16 * MIB),
        cost_estimate=pl.CostEstimate(flops=0, bytes_accessed=8 * rows * kv, transcendentals=0),
    )(here, same, other, *tokens)


def block_term(block, rows, here, mask, tile):
    pieces = [piece[:, tile] for piece in block]
    left = pieces[0] if len(pieces) == 1 else jnp.concatenate(pieces, axis=0)
    count = left.shape[0]
    start = pl.multiple_of((here[1] ^ mask) * count, count)
    return lax.dot_general(
        left, rows[pl.ds(start, count), :], TRANSPOSED, preferred_element_type=jnp.float32
    )


def regroup(refs, shape):
    refs = list(refs)
    return [[refs.pop(0) for _ in range(length)] for length in shape]


def call_in_vmem(body, here, operands, outputs, flops, tokens=()):
    moved = sum(x.size * x.dtype.itemsize for x in list(operands) + list(outputs))
    vmem = pl.BlockSpec(memory_space=pltpu.VMEM)
    return pl.pallas_call(
        body,
        grid_spec=pltpu.PrefetchScalarGridSpec(
            num_scalar_prefetch=1,
            grid=(),
            in_specs=[vmem] * len(operands) + [pl.BlockSpec(memory_space=pl.ANY)] * len(tokens),
            out_specs=[vmem] * len(outputs),
        ),
        out_shape=outputs,
        compiler_params=pltpu.CompilerParams(vmem_limit_bytes=20 * MIB),
        cost_estimate=pl.CostEstimate(
            flops=int(flops), bytes_accessed=moved, transcendentals=0
        ),
    )(here, *operands, *tokens)


def flat(blocks):
    return [piece for block in blocks.values() for piece in block]


def depth(blocks):
    return sum(piece.shape[0] for piece in flat(blocks))


def heads_body(masks, shape, part, scale, here, *refs):
    groups = regroup(refs[: sum(shape)], shape)
    rows, outs = refs[sum(shape)], refs[sum(shape) + 1 :]
    size = outs[0].shape[0] * len(outs)
    total = None
    for mask, block in zip(masks, groups):
        term = block_term(block, rows, here, mask, pl.ds(part * size, size))
        total = term if total is None else total + term
    for k, out in enumerate(outs):
        count = out.shape[0]
        out[...] = (total[k * count : (k + 1) * count] * scale).astype(out.dtype)


def heads_product(blocks, here, layer_input, part, pieces, dtype, scale):
    half = flat(blocks)[0].shape[1] // 2
    width = layer_input.shape[1]
    shape = [len(block) for block in blocks.values()]
    return call_in_vmem(
        functools.partial(heads_body, list(blocks), shape, part, scale),
        here,
        flat(blocks) + [layer_input],
        [jax.ShapeDtypeStruct((half // pieces, width), dtype)] * pieces,
        2 * depth(blocks) * half * width,
    )


def product_body(shape, here, *refs):
    groups = regroup(refs[: sum(shape)], shape)
    out = refs[-1]
    total = None
    for block, rows in zip(groups, refs[sum(shape) : -1]):
        pieces = [piece[...] for piece in block]
        left = pieces[0] if len(pieces) == 1 else jnp.concatenate(pieces, axis=0)
        term = lax.dot_general(left, rows[...], TRANSPOSED, preferred_element_type=jnp.float32)
        total = term if total is None else total + term
    out[...] = total


def row_blocks(blocks, width):
    def at(mask, i, here):
        return here[1] ^ mask, 0

    return [
        pl.BlockSpec((depth({mask: block}), width), functools.partial(at, mask))
        for mask, block in blocks.items()
    ]


def add_products(blocks, here, layer_input):
    kv = flat(blocks)[0].shape[1]
    width = layer_input.shape[1]
    tile = tile_of(kv)
    shape = [len(block) for block in blocks.values()]
    return pl.pallas_call(
        functools.partial(product_body, shape),
        grid_spec=pltpu.PrefetchScalarGridSpec(
            num_scalar_prefetch=1,
            grid=(kv // tile,),
            in_specs=[
                pl.BlockSpec((piece.shape[0], tile), lambda i, here: (0, i))
                for piece in flat(blocks)
            ]
            + row_blocks(blocks, width),
            out_specs=pl.BlockSpec((tile, width), lambda i, here: (i, 0)),
        ),
        out_shape=jax.ShapeDtypeStruct((kv, width), jnp.float32),
        compiler_params=pltpu.CompilerParams(vmem_limit_bytes=20 * MIB),
        cost_estimate=pl.CostEstimate(
            flops=2 * depth(blocks) * kv * width,
            bytes_accessed=2 * depth(blocks) * (kv + width) + 4 * kv * width,
            transcendentals=0,
        ),
    )(here, *flat(blocks), *([layer_input] * len(blocks)))


def project_body(masks, shape, scale, here, *refs):
    groups = regroup(refs[: sum(shape)], shape)
    rows, partial, projector, product = refs[sum(shape) : sum(shape) + 4]
    outs = refs[sum(shape) + 4 :]
    size = tile_of(product.shape[0])
    for at in range(0, product.shape[0], size):
        tile = pl.ds(at, size)
        total = partial[tile, :]
        for mask, block in zip(masks, groups):
            total += block_term(block, rows, here, mask, tile)
        product[tile, :] = total.astype(product.dtype)
    apply_body(0, scale, here, projector, product, *outs)


def apply_body(first, scale, here, projector, product, *outs):
    size = outs[0].shape[0] * len(outs)
    term = jnp.dot(
        projector[pl.ds(first, size), :], product[...], preferred_element_type=jnp.float32
    )
    for k, out in enumerate(outs):
        count = out.shape[0]
        out[...] = (term[k * count : (k + 1) * count] * scale).astype(out.dtype)


def project(blocks, here, layer_input, partial, projector, pieces, scale):
    kv, width = partial.shape
    half = projector.shape[0] // 2
    shape = [len(block) for block in blocks.values()]
    product, *sends = call_in_vmem(
        functools.partial(project_body, list(blocks), shape, scale),
        here,
        flat(blocks) + [layer_input, partial, projector],
        [jax.ShapeDtypeStruct((kv, width), jnp.bfloat16)]
        + [jax.ShapeDtypeStruct((half // pieces, width), jnp.bfloat16)] * pieces,
        2 * depth(blocks) * kv * width + 2 * half * kv * width,
    )
    return product, sends


def apply_rest(projector, product, here, pieces, scale):
    half = projector.shape[0] // 2
    kv, width = product.shape
    return call_in_vmem(
        functools.partial(apply_body, half, scale),
        here,
        [projector, product],
        [jax.ShapeDtypeStruct((half // pieces, width), jnp.float32)] * pieces,
        2 * half * kv * width,
    )


def on_device(layer_input, cotangent, candidates, moment_first, moment_second, owners):
    replicas = lax.axis_size("dp")
    members = lax.axis_size("fsdp")
    me_dp = lax.axis_index("dp")
    me_fsdp = lax.axis_index("fsdp")
    dp_bits = bits_of(replicas)
    far_bits = bits_of(members)[1:]
    scale = 1.0 / math.sqrt(layer_input.shape[0] * replicas)
    kv_share = candidates.shape[2] // replicas
    per = members // replicas

    order = [0]
    for bit in reversed(dp_bits):
        order = [mask ^ bit for mask in order] + order

    here = jnp.stack([me_dp, me_fsdp]).astype(jnp.int32)

    def owned(value, others):
        for at, bit in enumerate(dp_bits):
            if at == 1 and others:
                value = after(value, others, tokens)
            other = swap(value, "dp", bit)
            mine = (me_dp & bit) == (owners & bit)
            rows = jnp.repeat(mine, value.shape[0] // MATS)[:, None]
            value = jnp.where(rows, value, other)
        return value

    def assembled(value, others):
        blocks = spread(value, far_bits)
        same = jnp.concatenate([blocks[mask] for mask in sorted(blocks)], axis=0)
        same = after(same, others, tokens)
        other = swap(same, "fsdp", 1)
        return gather_projector(same, other, here, order, per, tokens)

    pieces = max(replicas // 2, 1)
    tokens = []

    own_other = swap(cotangent[0], "fsdp", 1)
    near, far, arrived = spread_near(cotangent[0], far_bits, tokens)
    both = jnp.swapaxes(candidates[:, 0], 1, 2).reshape(-1, candidates.shape[2])
    both_owned = owned(both, arrived)
    near_all = with_partner(near, own_other)
    later = [(mask, k) for mask in far_bits for k, piece in enumerate(near[mask])]
    later = [(mask, k) for mask, k in later if all(near[mask][k] is not x for x in arrived)]
    later_other = [near_all[mask ^ 1][k] for mask, k in later]
    later = [near[mask][k] for mask, k in later]
    projector_0, projector_1 = assembled(
        after(both_owned, later + flat(far), tokens), later_other
    )
    far_all = with_partner(far)
    partial = add_products(near_all, here, layer_input)
    product, send_0 = project(far_all, here, layer_input, partial, projector_0, pieces, scale)
    keep_0 = apply_rest(projector_0, product, here, pieces, scale)

    heads = lax.dot_general(
        cotangent[1], projector_1, (((1,), (1,)), ((), ())), preferred_element_type=jnp.float32
    ).astype(jnp.bfloat16)
    blocks = with_partner({mask: [held] for mask, held in spread(heads, far_bits).items()})
    send_1 = heads_product(blocks, here, layer_input, 0, pieces, jnp.bfloat16, scale)
    keep_1 = heads_product(blocks, here, layer_input, 1, pieces, jnp.float32, scale)

    def reduced(sends, keeps):
        for bit in dp_bits[:-1]:
            totals = [
                keep + swap(send, "dp", bit).astype(jnp.float32)
                for send, keep in zip(sends, keeps)
            ]
            half = len(totals) // 2
            sends = [total.astype(jnp.bfloat16) for total in totals[:half]]
            keeps = totals[half:]
        return keeps[0], swap(sends[0], "dp", dp_bits[-1])

    updates, firsts, seconds, directions = [], [], [], []
    for matrix, sends, keeps in ((0, send_0, keep_0), (1, send_1, keep_1)):
        keep, received = reduced(sends, keeps)
        if firsts:
            received, firsts[0] = lax.optimization_barrier((received, firsts[0]))
        projected = keep + received.astype(jnp.float32)
        first = beta_first * moment_first[matrix] + (1.0 - beta_first) * projected
        second = beta_second * moment_second[matrix] + (1.0 - beta_second) * projected * projected
        direction = (
            first
            / (1.0 - beta_first**STEP)
            / (jnp.sqrt(second / (1.0 - beta_second**STEP)) + epsilon)
        )
        directions.append(direction.astype(jnp.bfloat16))
        firsts.append(first)
        seconds.append(second)
    for direction, projector in zip(directions, (projector_0, projector_1)):
        own = lax.dynamic_slice_in_dim(projector, me_dp * kv_share, kv_share, 1)
        parts = [direction]
        for bit in reversed(dp_bits):
            parts = [swap(piece, "dp", bit) for piece in parts] + parts
        update = lax.dot_general(
            own, jnp.concatenate(parts, axis=0), TRANSPOSED, preferred_element_type=jnp.float32
        )
        updates.append(update.astype(jnp.bfloat16))
    return (jnp.stack(updates), jnp.stack(firsts), jnp.stack(seconds))


def solution(mesh):
    placed = (
        P("dp", "fsdp"),
        P(None, ("dp", "fsdp"), None),
        P(None, "dp", None, "fsdp"),
        P(None, "dp", "fsdp"),
        P(None, "dp", "fsdp"),
        P(),
    )
    return jax.shard_map(
        on_device,
        mesh=mesh,
        in_specs=placed,
        out_specs=(P(None, "dp", "fsdp"), P(None, "dp", "fsdp"), P(None, "dp", "fsdp")),
        check_vma=False,
    )
```

```python
import functools
import math

import jax
import jax.numpy as jnp
from jax import lax
from jax.experimental import pallas as pl
from jax.experimental.pallas import tpu as pltpu
from jax.sharding import PartitionSpec as P

MATS = 2
STEP = 10

beta_first = 0.9
beta_second = 0.999
epsilon = 1e-08

TRANSPOSED = (((0,), (0,)), ((), ()))
MIB = 1 << 20


def swap(value, axis, mask):
    size = lax.axis_size(axis)
    return lax.ppermute(value, axis, [(i, i ^ mask) for i in range(size)])


def bits_of(size):
    return [1 << k for k in range(size.bit_length() - 1)]


def after(value, others, tokens):
    corners = [other[:16, :128] for other in others]
    value, *held = lax.optimization_barrier((value, *corners))
    tokens.extend(held)
    return value


def spread(block, bits):
    if len(bits) == 2:
        low, high = bits
        masks = (0, low, high, low | high)
        return {mask: swap(block, "fsdp", mask) if mask else block for mask in masks}
    blocks = {0: block}
    for bit in bits:
        blocks.update({mask ^ bit: swap(held, "fsdp", bit) for mask, held in list(blocks.items())})
    return blocks


def spread_near(block, bits, tokens):
    if len(bits) == 2:
        low, high = bits
        half = block.shape[0] // 2
        top, bottom = block[:half], block[half:]
        low_top, high_bottom = swap(top, "fsdp", low), swap(bottom, "fsdp", high)
        far = [swap(low_top, "fsdp", high), swap(high_bottom, "fsdp", low)]
        by_low = [low_top, swap(after(bottom, [low_top], tokens), "fsdp", low)]
        by_high = [swap(after(top, [high_bottom], tokens), "fsdp", high), high_bottom]
        first = [low_top, high_bottom]
        return {0: [block], low: by_low, high: by_high}, {low | high: far}, first
    blocks = {mask: [held] for mask, held in spread(block, bits).items()}
    last = max(blocks)
    near = {mask: held for mask, held in blocks.items() if mask != last}
    return near, {last: blocks[last]}, []


def with_partner(blocks, own=None):
    other = {
        mask ^ 1: [own] if mask == 0 and own is not None else [swap(x, "fsdp", 1) for x in held]
        for mask, held in blocks.items()
    }
    return {**blocks, **other}


def tile_of(size):
    return min(size, 256)


def whole(shape):
    return pl.BlockSpec(shape, lambda *_: (0,) * len(shape))


def gather_body(order, per, count, here, same, other, *refs):
    out = refs[-1]
    spot = 0
    for mask in order:
        for sub in range(per):
            away = ((here[0] ^ mask) * per + sub) ^ here[1]
            at = pl.multiple_of((away >> 1) * count, count)
            out[pl.ds(spot * count, count), :] = jnp.where(
                (away & 1) == 0, same[pl.ds(at, count), :], other[pl.ds(at, count), :]
            )
            spot += 1


def gather_projector(same, other, here, order, per, tokens):
    rows, kv = same.shape
    rank = 2 * rows
    return pl.pallas_call(
        functools.partial(gather_body, order, per, rank // (len(order) * per)),
        grid_spec=pltpu.PrefetchScalarGridSpec(
            num_scalar_prefetch=1,
            grid=(1,),
            in_specs=[whole((rows, kv))] * 2
            + [pl.BlockSpec(memory_space=pl.ANY)] * len(tokens),
            out_specs=whole((rank, kv)),
        ),
        out_shape=jax.ShapeDtypeStruct((rank, kv), same.dtype),
        compiler_params=pltpu.CompilerParams(vmem_limit_bytes=12 * MIB),
        cost_estimate=pl.CostEstimate(flops=0, bytes_accessed=8 * rows * kv, transcendentals=0),
    )(here, same, other, *tokens)


def block_term(block, rows, here, mask, tile):
    pieces = [piece[:, tile] for piece in block]
    left = pieces[0] if len(pieces) == 1 else jnp.concatenate(pieces, axis=0)
    count = left.shape[0]
    start = pl.multiple_of((here[1] ^ mask) * count, count)
    return lax.dot_general(
        left, rows[pl.ds(start, count), :], TRANSPOSED, preferred_element_type=jnp.float32
    )


def regroup(refs, shape):
    refs = list(refs)
    return [[refs.pop(0) for _ in range(length)] for length in shape]


def call_in_vmem(body, here, operands, outputs, flops, tokens=()):
    moved = sum(x.size * x.dtype.itemsize for x in list(operands) + list(outputs))
    vmem = pl.BlockSpec(memory_space=pltpu.VMEM)
    return pl.pallas_call(
        body,
        grid_spec=pltpu.PrefetchScalarGridSpec(
            num_scalar_prefetch=1,
            grid=(),
            in_specs=[vmem] * len(operands) + [pl.BlockSpec(memory_space=pl.ANY)] * len(tokens),
            out_specs=[vmem] * len(outputs),
        ),
        out_shape=outputs,
        compiler_params=pltpu.CompilerParams(vmem_limit_bytes=20 * MIB),
        cost_estimate=pl.CostEstimate(
            flops=int(flops), bytes_accessed=moved, transcendentals=0
        ),
    )(here, *operands, *tokens)


def flat(blocks):
    return [piece for block in blocks.values() for piece in block]


def depth(blocks):
    return sum(piece.shape[0] for piece in flat(blocks))


def heads_body(masks, shape, part, pieces, scale, here, *refs):
    groups = regroup(refs[: sum(shape)], shape)
    rows, outs = refs[sum(shape)], refs[-pieces:]
    size = outs[0].shape[0] * len(outs)
    total = None
    for mask, block in zip(masks, groups):
        term = block_term(block, rows, here, mask, pl.ds(part * size, size))
        total = term if total is None else total + term
    for k, out in enumerate(outs):
        count = out.shape[0]
        out[...] = (total[k * count : (k + 1) * count] * scale).astype(out.dtype)


def heads_product(blocks, here, layer_input, part, pieces, dtype, scale, tokens=()):
    half = flat(blocks)[0].shape[1] // 2
    width = layer_input.shape[1]
    shape = [len(block) for block in blocks.values()]
    return call_in_vmem(
        functools.partial(heads_body, list(blocks), shape, part, pieces, scale),
        here,
        flat(blocks) + [layer_input],
        [jax.ShapeDtypeStruct((half // pieces, width), dtype)] * pieces,
        2 * depth(blocks) * half * width,
        tokens,
    )


def product_body(shape, here, *refs):
    groups = regroup(refs[: sum(shape)], shape)
    out = refs[-1]
    total = None
    for block, rows in zip(groups, refs[sum(shape) : -1]):
        pieces = [piece[...] for piece in block]
        left = pieces[0] if len(pieces) == 1 else jnp.concatenate(pieces, axis=0)
        term = lax.dot_general(left, rows[...], TRANSPOSED, preferred_element_type=jnp.float32)
        total = term if total is None else total + term
    out[...] = total


def row_blocks(blocks, width):
    def at(mask, i, here):
        return here[1] ^ mask, 0

    return [
        pl.BlockSpec((depth({mask: block}), width), functools.partial(at, mask))
        for mask, block in blocks.items()
    ]


def add_products(blocks, here, layer_input):
    kv = flat(blocks)[0].shape[1]
    width = layer_input.shape[1]
    tile = tile_of(kv)
    shape = [len(block) for block in blocks.values()]
    return pl.pallas_call(
        functools.partial(product_body, shape),
        grid_spec=pltpu.PrefetchScalarGridSpec(
            num_scalar_prefetch=1,
            grid=(kv // tile,),
            in_specs=[
                pl.BlockSpec((piece.shape[0], tile), lambda i, here: (0, i))
                for piece in flat(blocks)
            ]
            + row_blocks(blocks, width),
            out_specs=pl.BlockSpec((tile, width), lambda i, here: (i, 0)),
        ),
        out_shape=jax.ShapeDtypeStruct((kv, width), jnp.float32),
        compiler_params=pltpu.CompilerParams(vmem_limit_bytes=20 * MIB),
        cost_estimate=pl.CostEstimate(
            flops=2 * depth(blocks) * kv * width,
            bytes_accessed=2 * depth(blocks) * (kv + width) + 4 * kv * width,
            transcendentals=0,
        ),
    )(here, *flat(blocks), *([layer_input] * len(blocks)))


def project_body(masks, shape, scale, here, *refs):
    groups = regroup(refs[: sum(shape)], shape)
    rows, partial, projector, product = refs[sum(shape) : sum(shape) + 4]
    outs = refs[sum(shape) + 4 :]
    size = tile_of(product.shape[0])
    for at in range(0, product.shape[0], size):
        tile = pl.ds(at, size)
        total = partial[tile, :]
        for mask, block in zip(masks, groups):
            total += block_term(block, rows, here, mask, tile)
        product[tile, :] = total.astype(product.dtype)
    apply_body(0, scale, here, projector, product, *outs)


def apply_body(first, scale, here, projector, product, *outs):
    size = outs[0].shape[0] * len(outs)
    term = jnp.dot(
        projector[pl.ds(first, size), :], product[...], preferred_element_type=jnp.float32
    )
    for k, out in enumerate(outs):
        count = out.shape[0]
        out[...] = (term[k * count : (k + 1) * count] * scale).astype(out.dtype)


def project(blocks, here, layer_input, partial, projector, pieces, scale):
    kv, width = partial.shape
    half = projector.shape[0] // 2
    shape = [len(block) for block in blocks.values()]
    product, *sends = call_in_vmem(
        functools.partial(project_body, list(blocks), shape, scale),
        here,
        flat(blocks) + [layer_input, partial, projector],
        [jax.ShapeDtypeStruct((kv, width), jnp.bfloat16)]
        + [jax.ShapeDtypeStruct((half // pieces, width), jnp.bfloat16)] * pieces,
        2 * depth(blocks) * kv * width + 2 * half * kv * width,
    )
    return product, sends


def apply_rest(projector, product, here, pieces, scale):
    half = projector.shape[0] // 2
    kv, width = product.shape
    return call_in_vmem(
        functools.partial(apply_body, half, scale),
        here,
        [projector, product],
        [jax.ShapeDtypeStruct((half // pieces, width), jnp.float32)] * pieces,
        2 * half * kv * width,
    )


def on_device(layer_input, cotangent, candidates, moment_first, moment_second, owners):
    replicas = lax.axis_size("dp")
    members = lax.axis_size("fsdp")
    me_dp = lax.axis_index("dp")
    me_fsdp = lax.axis_index("fsdp")
    dp_bits = bits_of(replicas)
    far_bits = bits_of(members)[1:]
    scale = 1.0 / math.sqrt(layer_input.shape[0] * replicas)
    kv_share = candidates.shape[2] // replicas
    per = members // replicas

    order = [0]
    for bit in reversed(dp_bits):
        order = [mask ^ bit for mask in order] + order

    here = jnp.stack([me_dp, me_fsdp]).astype(jnp.int32)

    def owned(matrix, value, others, tokens):
        steps = []
        for at, bit in enumerate(dp_bits):
            if at == 1 and others:
                value = after(value, others, tokens)
            other = swap(value, "dp", bit)
            mine = (me_dp & bit) == (owners[matrix] & bit)
            value = jnp.where(mine, value, other)
            steps.append(value)
        return value, steps[0]

    def same_core(value):
        blocks = spread(value, far_bits)
        return jnp.concatenate([blocks[mask] for mask in sorted(blocks)], axis=0)

    def assembled(same, tokens):
        return gather_projector(same, swap(same, "fsdp", 1), here, order, per, tokens)

    pieces = max(replicas // 2, 1)
    tokens, tokens_1 = [], []

    near, far, arrived = spread_near(cotangent[0], far_bits, tokens)
    owned_0, step_0 = owned(0, candidates[0, 0].T, arrived, tokens)
    later = [piece for mask in far_bits for piece in near.get(mask, ())]
    later = [piece for piece in later if all(piece is not other for other in arrived)]
    same_0 = same_core(after(owned_0, later + flat(far), tokens))
    near_all = with_partner(near)
    partial = add_products(near_all, here, layer_input)
    far_all = with_partner(far)
    projector_0 = assembled(after(same_0, [partial], tokens), tokens)
    product, send_0 = project(far_all, here, layer_input, partial, projector_0, pieces, scale)
    keep_0 = apply_rest(projector_0, product, here, pieces, scale)

    owned_1, _ = owned(1, after(candidates[1, 0].T, [step_0], tokens_1), [owned_0], tokens_1)
    same_1 = same_core(after(owned_1, [same_0], tokens_1))
    projector_1 = assembled(after(same_1, send_0[:1], tokens_1), tokens_1)
    heads = lax.dot_general(
        cotangent[1], projector_1, (((1,), (1,)), ((), ())), preferred_element_type=jnp.float32
    ).astype(jnp.bfloat16)
    blocks = with_partner({mask: [held] for mask, held in spread(heads, far_bits).items()})
    arrived_0 = [swap(piece, "dp", dp_bits[0]) for piece in send_0]
    send_1 = heads_product(
        blocks, here, layer_input, 0, pieces, jnp.bfloat16, scale, arrived_0[pieces // 2 :]
    )
    arrived_1 = [swap(piece, "dp", dp_bits[0]) for piece in send_1]
    keep_1 = heads_product(blocks, here, layer_input, 1, pieces, jnp.float32, scale)

    def reduced(arrived, keeps):
        for bit in dp_bits[1:]:
            totals = [keep + piece.astype(jnp.float32) for piece, keep in zip(arrived, keeps)]
            half = len(totals) // 2
            arrived = [swap(total.astype(jnp.bfloat16), "dp", bit) for total in totals[:half]]
            keeps = totals[half:]
        return keeps[0], arrived[0]

    updates, firsts, seconds, gathered = [], [], [], []
    for matrix, arrived, keeps in ((0, arrived_0, keep_0), (1, arrived_1, keep_1)):
        keep, received = reduced(arrived, keeps)
        if gathered:
            received, firsts[0], *gathered[0][-3:-1] = lax.optimization_barrier(
                (received, firsts[0], *gathered[0][-3:-1])
            )
        projected = keep + received.astype(jnp.float32)
        first = beta_first * moment_first[matrix] + (1.0 - beta_first) * projected
        second = beta_second * moment_second[matrix] + (1.0 - beta_second) * projected * projected
        direction = (
            first
            / (1.0 - beta_first**STEP)
            / (jnp.sqrt(second / (1.0 - beta_second**STEP)) + epsilon)
        )
        parts = [direction.astype(jnp.bfloat16)]
        for bit in reversed(dp_bits):
            parts = [swap(piece, "dp", bit) for piece in parts] + parts
        gathered.append(parts)
        firsts.append(first)
        seconds.append(second)
    for parts, projector in zip(gathered, (projector_0, projector_1)):
        own = lax.dynamic_slice_in_dim(projector, me_dp * kv_share, kv_share, 1)
        update = lax.dot_general(
            own, jnp.concatenate(parts, axis=0), TRANSPOSED, preferred_element_type=jnp.float32
        )
        updates.append(update.astype(jnp.bfloat16))
    return (jnp.stack(updates), jnp.stack(firsts), jnp.stack(seconds))


def solution(mesh):
    placed = (
        P("dp", "fsdp"),
        P(None, ("dp", "fsdp"), None),
        P(None, "dp", None, "fsdp"),
        P(None, "dp", "fsdp"),
        P(None, "dp", "fsdp"),
        P(),
    )
    return jax.shard_map(
        on_device,
        mesh=mesh,
        in_specs=placed,
        out_specs=(P(None, "dp", "fsdp"), P(None, "dp", "fsdp"), P(None, "dp", "fsdp")),
        check_vma=False,
    )
```

```python
import functools
import math

import jax
import jax.numpy as jnp
from jax import lax
from jax.experimental import pallas as pl
from jax.experimental.pallas import tpu as pltpu
from jax.sharding import PartitionSpec as P

MATS = 2
STEP = 10

beta_first = 0.9
beta_second = 0.999
epsilon = 1e-08

TRANSPOSED = (((0,), (0,)), ((), ()))
MIB = 1 << 20
ORDER_HEADS = True
COST = 0.0


def swap(value, axis, mask):
    size = lax.axis_size(axis)
    return lax.ppermute(value, axis, [(i, i ^ mask) for i in range(size)])


def bits_of(size):
    return [1 << k for k in range(size.bit_length() - 1)]


def after(value, others, tokens):
    corners = [other[:16, :128] for other in others]
    value, *held = lax.optimization_barrier((value, *corners))
    tokens.extend(held)
    return value


def spread(block, bits):
    if len(bits) == 2:
        low, high = bits
        masks = (0, low, high, low | high)
        return {mask: swap(block, "fsdp", mask) if mask else block for mask in masks}
    blocks = {0: block}
    for bit in bits:
        blocks.update({mask ^ bit: swap(held, "fsdp", bit) for mask, held in list(blocks.items())})
    return blocks


def spread_near(block, bits, tokens):
    if len(bits) == 2:
        low, high = bits
        half = block.shape[0] // 2
        top, bottom = block[:half], block[half:]
        low_top, high_bottom = swap(top, "fsdp", low), swap(bottom, "fsdp", high)
        far = [swap(low_top, "fsdp", high), swap(high_bottom, "fsdp", low)]
        by_low = [low_top, swap(after(bottom, [low_top], tokens), "fsdp", low)]
        by_high = [swap(after(top, [high_bottom], tokens), "fsdp", high), high_bottom]
        first = [low_top, high_bottom]
        return {0: [block], low: by_low, high: by_high}, {low | high: far}, first
    blocks = {mask: [held] for mask, held in spread(block, bits).items()}
    last = max(blocks)
    near = {mask: held for mask, held in blocks.items() if mask != last}
    return near, {last: blocks[last]}, []


def with_partner(blocks, own=None):
    other = {
        mask ^ 1: [own] if mask == 0 and own is not None else [swap(x, "fsdp", 1) for x in held]
        for mask, held in blocks.items()
    }
    return {**blocks, **other}


def tile_of(size):
    return min(size, 256)


def whole(shape):
    return pl.BlockSpec(shape, lambda *_: (0,) * len(shape))


def gather_body(order, per, count, here, same, other, *refs):
    for matrix, out in enumerate(refs[-MATS:]):
        spot = 0
        for mask in order:
            for sub in range(per):
                away = ((here[0] ^ mask) * per + sub) ^ here[1]
                at = pl.multiple_of(((away >> 1) * MATS + matrix) * count, count)
                out[pl.ds(spot * count, count), :] = jnp.where(
                    (away & 1) == 0, same[pl.ds(at, count), :], other[pl.ds(at, count), :]
                )
                spot += 1


def gather_projector(same, other, here, order, per, tokens):
    rows, kv = same.shape
    rank = 2 * rows // MATS
    return pl.pallas_call(
        functools.partial(gather_body, order, per, rank // (len(order) * per)),
        grid_spec=pltpu.PrefetchScalarGridSpec(
            num_scalar_prefetch=1,
            grid=(1,),
            in_specs=[whole((rows, kv))] * 2
            + [pl.BlockSpec(memory_space=pl.ANY)] * len(tokens),
            out_specs=[whole((rank, kv))] * MATS,
        ),
        out_shape=[jax.ShapeDtypeStruct((rank, kv), same.dtype)] * MATS,
        compiler_params=pltpu.CompilerParams(vmem_limit_bytes=16 * MIB),
        cost_estimate=pl.CostEstimate(flops=0, bytes_accessed=8 * rows * kv, transcendentals=0),
    )(here, same, other, *tokens)


def block_term(block, rows, here, mask, tile):
    pieces = [piece[:, tile] for piece in block]
    left = pieces[0] if len(pieces) == 1 else jnp.concatenate(pieces, axis=0)
    count = left.shape[0]
    start = pl.multiple_of((here[1] ^ mask) * count, count)
    return lax.dot_general(
        left, rows[pl.ds(start, count), :], TRANSPOSED, preferred_element_type=jnp.float32
    )


def regroup(refs, shape):
    refs = list(refs)
    return [[refs.pop(0) for _ in range(length)] for length in shape]


def call_in_vmem(body, here, operands, outputs, flops, tokens=()):
    moved = sum(x.size * x.dtype.itemsize for x in list(operands) + list(outputs))
    vmem = pl.BlockSpec(memory_space=pltpu.VMEM)
    return pl.pallas_call(
        body,
        grid_spec=pltpu.PrefetchScalarGridSpec(
            num_scalar_prefetch=1,
            grid=(),
            in_specs=[vmem] * len(operands) + [pl.BlockSpec(memory_space=pl.ANY)] * len(tokens),
            out_specs=[vmem] * len(outputs),
        ),
        out_shape=outputs,
        compiler_params=pltpu.CompilerParams(vmem_limit_bytes=20 * MIB),
        cost_estimate=pl.CostEstimate(
            flops=int(flops * COST), bytes_accessed=int(moved * COST), transcendentals=0
        ),
    )(here, *operands, *tokens)


def flat(blocks):
    return [piece for block in blocks.values() for piece in block]


def depth(blocks):
    return sum(piece.shape[0] for piece in flat(blocks))


def heads_body(masks, shape, part, pieces, scale, here, *refs):
    groups = regroup(refs[: sum(shape)], shape)
    rows, outs = refs[sum(shape)], refs[-pieces:]
    size = outs[0].shape[0] * len(outs)
    total = None
    for mask, block in zip(masks, groups):
        term = block_term(block, rows, here, mask, pl.ds(part * size, size))
        total = term if total is None else total + term
    for k, out in enumerate(outs):
        count = out.shape[0]
        out[...] = (total[k * count : (k + 1) * count] * scale).astype(out.dtype)


def heads_product(blocks, here, layer_input, part, pieces, dtype, scale, tokens=()):
    half = flat(blocks)[0].shape[1] // 2
    width = layer_input.shape[1]
    shape = [len(block) for block in blocks.values()]
    return call_in_vmem(
        functools.partial(heads_body, list(blocks), shape, part, pieces, scale),
        here,
        flat(blocks) + [layer_input],
        [jax.ShapeDtypeStruct((half // pieces, width), dtype)] * pieces,
        2 * depth(blocks) * half * width,
        tokens,
    )


def product_body(shape, here, *refs):
    groups = regroup(refs[: sum(shape)], shape)
    out = refs[-1]
    total = None
    for block, rows in zip(groups, refs[sum(shape) : -1]):
        pieces = [piece[...] for piece in block]
        left = pieces[0] if len(pieces) == 1 else jnp.concatenate(pieces, axis=0)
        term = lax.dot_general(left, rows[...], TRANSPOSED, preferred_element_type=jnp.float32)
        total = term if total is None else total + term
    out[...] = total


def row_blocks(blocks, width):
    def at(mask, i, here):
        return here[1] ^ mask, 0

    return [
        pl.BlockSpec((depth({mask: block}), width), functools.partial(at, mask))
        for mask, block in blocks.items()
    ]


def add_products(blocks, here, layer_input):
    kv = flat(blocks)[0].shape[1]
    width = layer_input.shape[1]
    tile = tile_of(kv)
    shape = [len(block) for block in blocks.values()]
    return pl.pallas_call(
        functools.partial(product_body, shape),
        grid_spec=pltpu.PrefetchScalarGridSpec(
            num_scalar_prefetch=1,
            grid=(kv // tile,),
            in_specs=[
                pl.BlockSpec((piece.shape[0], tile), lambda i, here: (0, i))
                for piece in flat(blocks)
            ]
            + row_blocks(blocks, width),
            out_specs=pl.BlockSpec((tile, width), lambda i, here: (i, 0)),
        ),
        out_shape=jax.ShapeDtypeStruct((kv, width), jnp.float32),
        compiler_params=pltpu.CompilerParams(vmem_limit_bytes=20 * MIB),
        cost_estimate=pl.CostEstimate(
            flops=2 * depth(blocks) * kv * width,
            bytes_accessed=2 * depth(blocks) * (kv + width) + 4 * kv * width,
            transcendentals=0,
        ),
    )(here, *flat(blocks), *([layer_input] * len(blocks)))


def project_body(masks, shape, scale, here, *refs):
    groups = regroup(refs[: sum(shape)], shape)
    rows, partial, projector, product = refs[sum(shape) : sum(shape) + 4]
    outs = refs[sum(shape) + 4 :]
    size = tile_of(product.shape[0])
    for at in range(0, product.shape[0], size):
        tile = pl.ds(at, size)
        total = partial[tile, :]
        for mask, block in zip(masks, groups):
            total += block_term(block, rows, here, mask, tile)
        product[tile, :] = total.astype(product.dtype)
    apply_body(0, scale, here, projector, product, *outs)


def apply_body(first, scale, here, projector, product, *outs):
    size = outs[0].shape[0] * len(outs)
    term = jnp.dot(
        projector[pl.ds(first, size), :], product[...], preferred_element_type=jnp.float32
    )
    for k, out in enumerate(outs):
        count = out.shape[0]
        out[...] = (term[k * count : (k + 1) * count] * scale).astype(out.dtype)


def project(blocks, here, layer_input, partial, projector, pieces, scale):
    kv, width = partial.shape
    half = projector.shape[0] // 2
    shape = [len(block) for block in blocks.values()]
    product, *sends = call_in_vmem(
        functools.partial(project_body, list(blocks), shape, scale),
        here,
        flat(blocks) + [layer_input, partial, projector],
        [jax.ShapeDtypeStruct((kv, width), jnp.bfloat16)]
        + [jax.ShapeDtypeStruct((half // pieces, width), jnp.bfloat16)] * pieces,
        2 * depth(blocks) * kv * width + 2 * half * kv * width,
    )
    return product, sends


def apply_rest(projector, product, here, pieces, scale):
    half = projector.shape[0] // 2
    kv, width = product.shape
    return call_in_vmem(
        functools.partial(apply_body, half, scale),
        here,
        [projector, product],
        [jax.ShapeDtypeStruct((half // pieces, width), jnp.float32)] * pieces,
        2 * half * kv * width,
    )


def on_device(layer_input, cotangent, candidates, moment_first, moment_second, owners):
    replicas = lax.axis_size("dp")
    members = lax.axis_size("fsdp")
    me_dp = lax.axis_index("dp")
    me_fsdp = lax.axis_index("fsdp")
    dp_bits = bits_of(replicas)
    far_bits = bits_of(members)[1:]
    scale = 1.0 / math.sqrt(layer_input.shape[0] * replicas)
    kv_share = candidates.shape[2] // replicas
    per = members // replicas

    order = [0]
    for bit in reversed(dp_bits):
        order = [mask ^ bit for mask in order] + order

    here = jnp.stack([me_dp, me_fsdp]).astype(jnp.int32)

    def owned(value, others, tokens):
        for at, bit in enumerate(dp_bits):
            if at == 1 and others:
                value = after(value, others, tokens)
            other = swap(value, "dp", bit)
            mine = (me_dp & bit) == (owners & bit)
            rows = jnp.repeat(mine, value.shape[0] // MATS)[:, None]
            value = jnp.where(rows, value, other)
        return value

    pieces = max(replicas // 2, 1)
    tokens, tokens_1 = [], []

    near, far, arrived = spread_near(cotangent[0], far_bits, tokens)
    both = jnp.swapaxes(candidates[:, 0], 1, 2).reshape(-1, candidates.shape[2])
    both = owned(both, arrived, tokens)
    later = [piece for mask in far_bits for piece in near.get(mask, ())]
    later = [piece for piece in later if all(piece is not other for other in arrived)]
    blocks = spread(after(both, later + flat(far), tokens), far_bits)
    same = jnp.concatenate([blocks[mask] for mask in sorted(blocks)], axis=0)
    near_all = with_partner(near)
    partial = add_products(near_all, here, layer_input)
    far_all = with_partner(far)
    same = after(same, [partial], tokens)
    projectors = gather_projector(same, swap(same, "fsdp", 1), here, order, per, tokens)
    product, send_0 = project(far_all, here, layer_input, partial, projectors[0], pieces, scale)
    keep_0 = apply_rest(projectors[0], product, here, pieces, scale)
    arrived_0 = [swap(piece, "dp", dp_bits[0]) for piece in send_0]

    def forward(arrived, keeps):
        totals = [keep + piece.astype(jnp.float32) for piece, keep in zip(arrived, keeps)]
        half = len(totals) // 2
        return [total.astype(jnp.bfloat16) for total in totals[:half]], totals[half:]

    def reduced(arrived, keeps, sends=None):
        for bit in dp_bits[1:]:
            made, keeps = forward(arrived, keeps)
            arrived = [swap(piece, "dp", bit) for piece in (sends or made)]
            sends = None
        return keeps[0], arrived[0]

    heads = lax.dot_general(
        cotangent[1], projectors[1], (((1,), (1,)), ((), ())), preferred_element_type=jnp.float32
    ).astype(jnp.bfloat16)
    if ORDER_HEADS:
        heads = after(heads, send_0[:1], tokens_1)
    blocks = spread(heads, far_bits)
    if len(dp_bits) > 1:
        next_0, _ = forward(arrived_0, keep_0)
        moved = [mask for mask in blocks if mask]
        held = lax.optimization_barrier(tuple(blocks[mask] for mask in moved) + (next_0[0],))
        blocks.update(zip(moved, held))
        tokens_1.append(held[-1])
    blocks = with_partner({mask: [held] for mask, held in blocks.items()})
    send_1 = heads_product(
        blocks, here, layer_input, 0, 1, jnp.bfloat16, scale, arrived_0[pieces // 2 :] + tokens_1
    )
    keep_1 = heads_product(blocks, here, layer_input, 1, pieces, jnp.float32, scale)
    arrived_1 = jnp.split(swap(send_1[0], "dp", dp_bits[0]), pieces)

    updates, firsts, seconds, gathered = [], [], [], []
    for matrix, arrived, keeps in ((0, arrived_0, keep_0), (1, arrived_1, keep_1)):
        keep, received = reduced(arrived, keeps)
        if gathered:
            received, firsts[0], *gathered[0][:-1] = lax.optimization_barrier(
                (received, firsts[0], *gathered[0][:-1])
            )
        projected = keep + received.astype(jnp.float32)
        first = beta_first * moment_first[matrix] + (1.0 - beta_first) * projected
        second = beta_second * moment_second[matrix] + (1.0 - beta_second) * projected * projected
        direction = (
            first
            / (1.0 - beta_first**STEP)
            / (jnp.sqrt(second / (1.0 - beta_second**STEP)) + epsilon)
        )
        parts = [direction.astype(jnp.bfloat16)]
        for bit in reversed(dp_bits):
            parts = [swap(piece, "dp", bit) for piece in parts] + parts
        gathered.append(parts)
        firsts.append(first)
        seconds.append(second)
    for parts, projector in zip(gathered, projectors):
        own = lax.dynamic_slice_in_dim(projector, me_dp * kv_share, kv_share, 1)
        update = lax.dot_general(
            own, jnp.concatenate(parts, axis=0), TRANSPOSED, preferred_element_type=jnp.float32
        )
        updates.append(update.astype(jnp.bfloat16))
    return (jnp.stack(updates), jnp.stack(firsts), jnp.stack(seconds))


def solution(mesh):
    placed = (
        P("dp", "fsdp"),
        P(None, ("dp", "fsdp"), None),
        P(None, "dp", None, "fsdp"),
        P(None, "dp", "fsdp"),
        P(None, "dp", "fsdp"),
        P(),
    )
    return jax.shard_map(
        on_device,
        mesh=mesh,
        in_specs=placed,
        out_specs=(P(None, "dp", "fsdp"), P(None, "dp", "fsdp"), P(None, "dp", "fsdp")),
        check_vma=False,
    )
```

```python
import functools
import math

import jax
import jax.numpy as jnp
from jax import lax
from jax.experimental import pallas as pl
from jax.experimental.pallas import tpu as pltpu
from jax.sharding import PartitionSpec as P

MATS = 2
STEP = 10

beta_first = 0.9
beta_second = 0.999
epsilon = 1e-08

TRANSPOSED = (((0,), (0,)), ((), ()))
MIB = 1 << 20


def swap(value, axis, mask):
    size = lax.axis_size(axis)
    return lax.ppermute(value, axis, [(i, i ^ mask) for i in range(size)])


def bits_of(size):
    return [1 << k for k in range(size.bit_length() - 1)]


def after(value, others, tokens):
    corners = [other[:16, :128] for other in others]
    value, *held = lax.optimization_barrier((value, *corners))
    tokens.extend(held)
    return value


def spread(block, bits):
    if len(bits) == 2:
        low, high = bits
        masks = (0, low, high, low | high)
        return {mask: swap(block, "fsdp", mask) if mask else block for mask in masks}
    blocks = {0: block}
    for bit in bits:
        blocks.update({mask ^ bit: swap(held, "fsdp", bit) for mask, held in list(blocks.items())})
    return blocks


def spread_near(block, bits, tokens):
    if len(bits) == 2:
        low, high = bits
        half = block.shape[0] // 2
        top, bottom = block[:half], block[half:]
        low_top, high_bottom = swap(top, "fsdp", low), swap(bottom, "fsdp", high)
        far = [swap(low_top, "fsdp", high), swap(high_bottom, "fsdp", low)]
        by_low = [low_top, swap(after(bottom, [low_top], tokens), "fsdp", low)]
        by_high = [swap(after(top, [high_bottom], tokens), "fsdp", high), high_bottom]
        first = [low_top, high_bottom]
        return {0: [block], low: by_low, high: by_high}, {low | high: far}, first
    blocks = {mask: [held] for mask, held in spread(block, bits).items()}
    last = max(blocks)
    near = {mask: held for mask, held in blocks.items() if mask != last}
    return near, {last: blocks[last]}, []


def with_partner(blocks, own=None):
    other = {
        mask ^ 1: [own] if mask == 0 and own is not None else [swap(x, "fsdp", 1) for x in held]
        for mask, held in blocks.items()
    }
    return {**blocks, **other}


def tile_of(size):
    return min(size, 256)


def whole(shape):
    return pl.BlockSpec(shape, lambda *_: (0,) * len(shape))


def gather_body(order, per, count, here, same, other, *refs):
    for matrix, out in enumerate(refs[-MATS:]):
        spot = 0
        for mask in order:
            for sub in range(per):
                away = ((here[0] ^ mask) * per + sub) ^ here[1]
                at = pl.multiple_of(((away >> 1) * MATS + matrix) * count, count)
                out[pl.ds(spot * count, count), :] = jnp.where(
                    (away & 1) == 0, same[pl.ds(at, count), :], other[pl.ds(at, count), :]
                )
                spot += 1


def gather_projector(same, other, here, order, per, tokens):
    rows, kv = same.shape
    rank = 2 * rows // MATS
    return pl.pallas_call(
        functools.partial(gather_body, order, per, rank // (len(order) * per)),
        grid_spec=pltpu.PrefetchScalarGridSpec(
            num_scalar_prefetch=1,
            grid=(1,),
            in_specs=[whole((rows, kv))] * 2
            + [pl.BlockSpec(memory_space=pl.ANY)] * len(tokens),
            out_specs=[whole((rank, kv))] * MATS,
        ),
        out_shape=[jax.ShapeDtypeStruct((rank, kv), same.dtype)] * MATS,
        compiler_params=pltpu.CompilerParams(vmem_limit_bytes=16 * MIB),
        cost_estimate=pl.CostEstimate(flops=0, bytes_accessed=8 * rows * kv, transcendentals=0),
    )(here, same, other, *tokens)


def block_term(block, rows, here, mask, tile):
    pieces = [piece[:, tile] for piece in block]
    left = pieces[0] if len(pieces) == 1 else jnp.concatenate(pieces, axis=0)
    count = left.shape[0]
    start = pl.multiple_of((here[1] ^ mask) * count, count)
    return lax.dot_general(
        left, rows[pl.ds(start, count), :], TRANSPOSED, preferred_element_type=jnp.float32
    )


def regroup(refs, shape):
    refs = list(refs)
    return [[refs.pop(0) for _ in range(length)] for length in shape]


def call_in_vmem(body, here, operands, outputs, flops, tokens=()):
    moved = sum(x.size * x.dtype.itemsize for x in list(operands) + list(outputs))
    vmem = pl.BlockSpec(memory_space=pltpu.VMEM)
    return pl.pallas_call(
        body,
        grid_spec=pltpu.PrefetchScalarGridSpec(
            num_scalar_prefetch=1,
            grid=(),
            in_specs=[vmem] * len(operands) + [pl.BlockSpec(memory_space=pl.ANY)] * len(tokens),
            out_specs=[vmem] * len(outputs),
        ),
        out_shape=outputs,
        compiler_params=pltpu.CompilerParams(vmem_limit_bytes=20 * MIB),
        cost_estimate=pl.CostEstimate(
            flops=int(flops), bytes_accessed=int(moved), transcendentals=0
        ),
    )(here, *operands, *tokens)


def flat(blocks):
    return [piece for block in blocks.values() for piece in block]


def depth(blocks):
    return sum(piece.shape[0] for piece in flat(blocks))


def heads_body(masks, shape, part, pieces, scale, here, *refs):
    groups = regroup(refs[: sum(shape)], shape)
    rows, outs = refs[sum(shape)], refs[-pieces:]
    size = outs[0].shape[0] * len(outs)
    total = None
    for mask, block in zip(masks, groups):
        term = block_term(block, rows, here, mask, pl.ds(part * size, size))
        total = term if total is None else total + term
    for k, out in enumerate(outs):
        count = out.shape[0]
        out[...] = (total[k * count : (k + 1) * count] * scale).astype(out.dtype)


def heads_product(blocks, here, layer_input, part, pieces, dtype, scale, tokens=()):
    half = flat(blocks)[0].shape[1] // 2
    width = layer_input.shape[1]
    shape = [len(block) for block in blocks.values()]
    return call_in_vmem(
        functools.partial(heads_body, list(blocks), shape, part, pieces, scale),
        here,
        flat(blocks) + [layer_input],
        [jax.ShapeDtypeStruct((half // pieces, width), dtype)] * pieces,
        2 * depth(blocks) * half * width,
        tokens,
    )


def product_body(shape, here, *refs):
    groups = regroup(refs[: sum(shape)], shape)
    out = refs[-1]
    total = None
    for block, rows in zip(groups, refs[sum(shape) : -1]):
        pieces = [piece[...] for piece in block]
        left = pieces[0] if len(pieces) == 1 else jnp.concatenate(pieces, axis=0)
        term = lax.dot_general(left, rows[...], TRANSPOSED, preferred_element_type=jnp.float32)
        total = term if total is None else total + term
    out[...] = total


def row_blocks(blocks, width):
    def at(mask, i, here):
        return here[1] ^ mask, 0

    return [
        pl.BlockSpec((depth({mask: block}), width), functools.partial(at, mask))
        for mask, block in blocks.items()
    ]


def add_products(blocks, here, layer_input):
    kv = flat(blocks)[0].shape[1]
    width = layer_input.shape[1]
    tile = tile_of(kv)
    shape = [len(block) for block in blocks.values()]
    return pl.pallas_call(
        functools.partial(product_body, shape),
        grid_spec=pltpu.PrefetchScalarGridSpec(
            num_scalar_prefetch=1,
            grid=(kv // tile,),
            in_specs=[
                pl.BlockSpec((piece.shape[0], tile), lambda i, here: (0, i))
                for piece in flat(blocks)
            ]
            + row_blocks(blocks, width),
            out_specs=pl.BlockSpec((tile, width), lambda i, here: (i, 0)),
        ),
        out_shape=jax.ShapeDtypeStruct((kv, width), jnp.float32),
        compiler_params=pltpu.CompilerParams(vmem_limit_bytes=20 * MIB),
        cost_estimate=pl.CostEstimate(
            flops=2 * depth(blocks) * kv * width,
            bytes_accessed=2 * depth(blocks) * (kv + width) + 4 * kv * width,
            transcendentals=0,
        ),
    )(here, *flat(blocks), *([layer_input] * len(blocks)))


def project_body(masks, shape, scale, here, *refs):
    groups = regroup(refs[: sum(shape)], shape)
    rows, partial, projector, product = refs[sum(shape) : sum(shape) + 4]
    outs = refs[sum(shape) + 4 :]
    size = tile_of(product.shape[0])
    for at in range(0, product.shape[0], size):
        tile = pl.ds(at, size)
        total = partial[tile, :]
        for mask, block in zip(masks, groups):
            total += block_term(block, rows, here, mask, tile)
        product[tile, :] = total.astype(product.dtype)
    apply_body(0, scale, here, projector, product, *outs)


def apply_body(first, scale, here, projector, product, *outs):
    size = outs[0].shape[0] * len(outs)
    term = jnp.dot(
        projector[pl.ds(first, size), :], product[...], preferred_element_type=jnp.float32
    )
    for k, out in enumerate(outs):
        count = out.shape[0]
        out[...] = (term[k * count : (k + 1) * count] * scale).astype(out.dtype)


def project(blocks, here, layer_input, partial, projector, pieces, scale):
    kv, width = partial.shape
    half = projector.shape[0] // 2
    shape = [len(block) for block in blocks.values()]
    product, *sends = call_in_vmem(
        functools.partial(project_body, list(blocks), shape, scale),
        here,
        flat(blocks) + [layer_input, partial, projector],
        [jax.ShapeDtypeStruct((kv, width), jnp.bfloat16)]
        + [jax.ShapeDtypeStruct((half // pieces, width), jnp.bfloat16)] * pieces,
        2 * depth(blocks) * kv * width + 2 * half * kv * width,
    )
    return product, sends


def apply_rest(projector, product, here, pieces, scale):
    half = projector.shape[0] // 2
    kv, width = product.shape
    return call_in_vmem(
        functools.partial(apply_body, half, scale),
        here,
        [projector, product],
        [jax.ShapeDtypeStruct((half // pieces, width), jnp.float32)] * pieces,
        2 * half * kv * width,
    )


def on_device(layer_input, cotangent, candidates, moment_first, moment_second, owners):
    replicas = lax.axis_size("dp")
    members = lax.axis_size("fsdp")
    me_dp = lax.axis_index("dp")
    me_fsdp = lax.axis_index("fsdp")
    dp_bits = bits_of(replicas)
    far_bits = bits_of(members)[1:]
    scale = 1.0 / math.sqrt(layer_input.shape[0] * replicas)
    kv_share = candidates.shape[2] // replicas
    per = members // replicas

    order = [0]
    for bit in reversed(dp_bits):
        order = [mask ^ bit for mask in order] + order

    here = jnp.stack([me_dp, me_fsdp]).astype(jnp.int32)

    def owned(value, others, tokens):
        for at, bit in enumerate(dp_bits):
            if at == 1 and others:
                value = after(value, others, tokens)
            other = swap(value, "dp", bit)
            mine = (me_dp & bit) == (owners & bit)
            rows = jnp.repeat(mine, value.shape[0] // MATS)[:, None]
            value = jnp.where(rows, value, other)
        return value

    pieces = max(replicas // 2, 1)
    tokens, tokens_1 = [], []

    near, far, arrived = spread_near(cotangent[0], far_bits, tokens)
    both = jnp.swapaxes(candidates[:, 0], 1, 2).reshape(-1, candidates.shape[2])
    both = owned(both, arrived, tokens)
    later = [piece for mask in far_bits for piece in near.get(mask, ())]
    later = [piece for piece in later if all(piece is not other for other in arrived)]
    blocks = spread(after(both, later + flat(far), tokens), far_bits)
    same = jnp.concatenate([blocks[mask] for mask in sorted(blocks)], axis=0)
    near_all = with_partner(near)
    partial = add_products(near_all, here, layer_input)
    far_all = with_partner(far)
    same = after(same, [partial], tokens)
    projectors = gather_projector(same, swap(same, "fsdp", 1), here, order, per, tokens)
    product, send_0 = project(far_all, here, layer_input, partial, projectors[0], pieces, scale)
    keep_0 = apply_rest(projectors[0], product, here, pieces, scale)
    arrived_0 = [swap(piece, "dp", dp_bits[0]) for piece in send_0]

    def reduced(arrived, keeps):
        for bit in dp_bits[1:]:
            totals = [keep + piece.astype(jnp.float32) for piece, keep in zip(arrived, keeps)]
            half = len(totals) // 2
            arrived = [swap(total.astype(jnp.bfloat16), "dp", bit) for total in totals[:half]]
            keeps = totals[half:]
        return keeps[0], arrived[0]

    heads = lax.dot_general(
        cotangent[1], projectors[1], (((1,), (1,)), ((), ())), preferred_element_type=jnp.float32
    ).astype(jnp.bfloat16)
    blocks = spread(heads, far_bits)
    open_0 = reduced(arrived_0, keep_0)
    tokens_1 += arrived_0[pieces // 2 :]
    blocks = with_partner({mask: [held] for mask, held in blocks.items()})
    send_1 = heads_product(blocks, here, layer_input, 0, pieces, jnp.bfloat16, scale, tokens_1)
    keep_1 = heads_product(blocks, here, layer_input, 1, pieces, jnp.float32, scale)
    arrived_1 = [swap(piece, "dp", dp_bits[0]) for piece in send_1]

    updates, firsts, seconds, gathered = [], [], [], []
    for matrix, (keep, received) in enumerate((open_0, reduced(arrived_1, keep_1))):
        if gathered:
            received, firsts[0], *gathered[0][:-1] = lax.optimization_barrier(
                (received, firsts[0], *gathered[0][:-1])
            )
        projected = keep + received.astype(jnp.float32)
        first = beta_first * moment_first[matrix] + (1.0 - beta_first) * projected
        second = beta_second * moment_second[matrix] + (1.0 - beta_second) * projected * projected
        direction = (
            first
            / (1.0 - beta_first**STEP)
            / (jnp.sqrt(second / (1.0 - beta_second**STEP)) + epsilon)
        )
        parts = [direction.astype(jnp.bfloat16)]
        for bit in reversed(dp_bits):
            parts = [swap(piece, "dp", bit) for piece in parts] + parts
        gathered.append(parts)
        firsts.append(first)
        seconds.append(second)
    for parts, projector in zip(gathered, projectors):
        own = lax.dynamic_slice_in_dim(projector, me_dp * kv_share, kv_share, 1)
        update = lax.dot_general(
            own, jnp.concatenate(parts, axis=0), TRANSPOSED, preferred_element_type=jnp.float32
        )
        updates.append(update.astype(jnp.bfloat16))
    update = jnp.zeros((MATS,) + updates[0].shape, updates[0].dtype)
    for matrix in range(MATS):
        update = lax.dynamic_update_slice(update, updates[matrix][None], (matrix, 0, 0))
    return (update, jnp.stack(firsts), jnp.stack(seconds))


def solution(mesh):
    placed = (
        P("dp", "fsdp"),
        P(None, ("dp", "fsdp"), None),
        P(None, "dp", None, "fsdp"),
        P(None, "dp", "fsdp"),
        P(None, "dp", "fsdp"),
        P(),
    )
    return jax.shard_map(
        on_device,
        mesh=mesh,
        in_specs=placed,
        out_specs=(P(None, "dp", "fsdp"), P(None, "dp", "fsdp"), P(None, "dp", "fsdp")),
        check_vma=False,
    )
```

```python
import functools
import math

import jax
import jax.numpy as jnp
from jax import lax
from jax.experimental import pallas as pl
from jax.experimental.pallas import tpu as pltpu
from jax.sharding import PartitionSpec as P

MATS = 2
STEP = 10

beta_first = 0.9
beta_second = 0.999
epsilon = 1e-08

TRANSPOSED = (((0,), (0,)), ((), ()))
MIB = 1 << 20


def swap(value, axis, mask):
    size = lax.axis_size(axis)
    return lax.ppermute(value, axis, [(i, i ^ mask) for i in range(size)])


def bits_of(size):
    return [1 << k for k in range(size.bit_length() - 1)]


def after(value, others, tokens):
    corners = [other[:16, :128] for other in others]
    value, *held = lax.optimization_barrier((value, *corners))
    tokens.extend(held)
    return value


def spread(block, bits):
    if len(bits) == 2:
        low, high = bits
        masks = (0, low, high, low | high)
        return {mask: swap(block, "fsdp", mask) if mask else block for mask in masks}
    blocks = {0: block}
    for bit in bits:
        blocks.update({mask ^ bit: swap(held, "fsdp", bit) for mask, held in list(blocks.items())})
    return blocks


def spread_near(block, bits, tokens):
    if len(bits) == 2:
        low, high = bits
        half = block.shape[0] // 2
        top, bottom = block[:half], block[half:]
        low_top, high_bottom = swap(top, "fsdp", low), swap(bottom, "fsdp", high)
        far = [swap(low_top, "fsdp", high), swap(high_bottom, "fsdp", low)]
        by_low = [low_top, swap(after(bottom, [low_top], tokens), "fsdp", low)]
        by_high = [swap(after(top, [high_bottom], tokens), "fsdp", high), high_bottom]
        first = [low_top, high_bottom]
        return {0: [block], low: by_low, high: by_high}, {low | high: far}, first
    blocks = {mask: [held] for mask, held in spread(block, bits).items()}
    last = max(blocks)
    near = {mask: held for mask, held in blocks.items() if mask != last}
    return near, {last: blocks[last]}, []


def with_partner(blocks, own=None):
    other = {
        mask ^ 1: [own] if mask == 0 and own is not None else [swap(x, "fsdp", 1) for x in held]
        for mask, held in blocks.items()
    }
    return {**blocks, **other}


def tile_of(size):
    return min(size, 256)


def whole(shape):
    return pl.BlockSpec(shape, lambda *_: (0,) * len(shape))


def gather_body(order, per, count, here, same, other, *refs):
    for matrix, out in enumerate(refs[-MATS:]):
        spot = 0
        for mask in order:
            for sub in range(per):
                away = ((here[0] ^ mask) * per + sub) ^ here[1]
                at = pl.multiple_of(((away >> 1) * MATS + matrix) * count, count)
                out[pl.ds(spot * count, count), :] = jnp.where(
                    (away & 1) == 0, same[pl.ds(at, count), :], other[pl.ds(at, count), :]
                )
                spot += 1


def gather_projector(same, other, here, order, per, tokens):
    rows, kv = same.shape
    rank = 2 * rows // MATS
    return pl.pallas_call(
        functools.partial(gather_body, order, per, rank // (len(order) * per)),
        grid_spec=pltpu.PrefetchScalarGridSpec(
            num_scalar_prefetch=1,
            grid=(1,),
            in_specs=[whole((rows, kv))] * 2
            + [pl.BlockSpec(memory_space=pl.ANY)] * len(tokens),
            out_specs=[whole((rank, kv))] * MATS,
        ),
        out_shape=[jax.ShapeDtypeStruct((rank, kv), same.dtype)] * MATS,
        compiler_params=pltpu.CompilerParams(vmem_limit_bytes=16 * MIB),
        cost_estimate=pl.CostEstimate(flops=0, bytes_accessed=8 * rows * kv, transcendentals=0),
    )(here, same, other, *tokens)


def block_term(block, rows, here, mask, tile):
    pieces = [piece[:, tile] for piece in block]
    left = pieces[0] if len(pieces) == 1 else jnp.concatenate(pieces, axis=0)
    count = left.shape[0]
    start = pl.multiple_of((here[1] ^ mask) * count, count)
    return lax.dot_general(
        left, rows[pl.ds(start, count), :], TRANSPOSED, preferred_element_type=jnp.float32
    )


def regroup(refs, shape):
    refs = list(refs)
    return [[refs.pop(0) for _ in range(length)] for length in shape]


def call_in_vmem(body, here, operands, outputs, flops, tokens=()):
    moved = sum(x.size * x.dtype.itemsize for x in list(operands) + list(outputs))
    vmem = pl.BlockSpec(memory_space=pltpu.VMEM)
    return pl.pallas_call(
        body,
        grid_spec=pltpu.PrefetchScalarGridSpec(
            num_scalar_prefetch=1,
            grid=(),
            in_specs=[vmem] * len(operands) + [pl.BlockSpec(memory_space=pl.ANY)] * len(tokens),
            out_specs=[vmem] * len(outputs),
        ),
        out_shape=outputs,
        compiler_params=pltpu.CompilerParams(vmem_limit_bytes=20 * MIB),
        cost_estimate=pl.CostEstimate(
            flops=int(flops), bytes_accessed=int(moved), transcendentals=0
        ),
    )(here, *operands, *tokens)


def flat(blocks):
    return [piece for block in blocks.values() for piece in block]


def depth(blocks):
    return sum(piece.shape[0] for piece in flat(blocks))


def heads_body(masks, shape, part, pieces, scale, here, *refs):
    groups = regroup(refs[: sum(shape)], shape)
    rows, outs = refs[sum(shape)], refs[-pieces:]
    size = outs[0].shape[0] * len(outs)
    total = None
    for mask, block in zip(masks, groups):
        term = block_term(block, rows, here, mask, pl.ds(part * size, size))
        total = term if total is None else total + term
    for k, out in enumerate(outs):
        count = out.shape[0]
        out[...] = (total[k * count : (k + 1) * count] * scale).astype(out.dtype)


def heads_product(blocks, here, layer_input, part, pieces, dtype, scale, tokens=()):
    half = flat(blocks)[0].shape[1] // 2
    width = layer_input.shape[1]
    shape = [len(block) for block in blocks.values()]
    return call_in_vmem(
        functools.partial(heads_body, list(blocks), shape, part, pieces, scale),
        here,
        flat(blocks) + [layer_input],
        [jax.ShapeDtypeStruct((half // pieces, width), dtype)] * pieces,
        2 * depth(blocks) * half * width,
        tokens,
    )


def product_body(shape, here, *refs):
    groups = regroup(refs[: sum(shape)], shape)
    out = refs[-1]
    total = None
    for block, rows in zip(groups, refs[sum(shape) : -1]):
        pieces = [piece[...] for piece in block]
        left = pieces[0] if len(pieces) == 1 else jnp.concatenate(pieces, axis=0)
        term = lax.dot_general(left, rows[...], TRANSPOSED, preferred_element_type=jnp.float32)
        total = term if total is None else total + term
    out[...] = total


def row_blocks(blocks, width):
    def at(mask, i, here):
        return here[1] ^ mask, 0

    return [
        pl.BlockSpec((depth({mask: block}), width), functools.partial(at, mask))
        for mask, block in blocks.items()
    ]


def add_products(blocks, here, layer_input):
    kv = flat(blocks)[0].shape[1]
    width = layer_input.shape[1]
    tile = tile_of(kv)
    shape = [len(block) for block in blocks.values()]
    return pl.pallas_call(
        functools.partial(product_body, shape),
        grid_spec=pltpu.PrefetchScalarGridSpec(
            num_scalar_prefetch=1,
            grid=(kv // tile,),
            in_specs=[
                pl.BlockSpec((piece.shape[0], tile), lambda i, here: (0, i))
                for piece in flat(blocks)
            ]
            + row_blocks(blocks, width),
            out_specs=pl.BlockSpec((tile, width), lambda i, here: (i, 0)),
        ),
        out_shape=jax.ShapeDtypeStruct((kv, width), jnp.float32),
        compiler_params=pltpu.CompilerParams(vmem_limit_bytes=20 * MIB),
        cost_estimate=pl.CostEstimate(
            flops=2 * depth(blocks) * kv * width,
            bytes_accessed=2 * depth(blocks) * (kv + width) + 4 * kv * width,
            transcendentals=0,
        ),
    )(here, *flat(blocks), *([layer_input] * len(blocks)))


def project_body(masks, shape, scale, here, *refs):
    groups = regroup(refs[: sum(shape)], shape)
    rows, partial, projector, product = refs[sum(shape) : sum(shape) + 4]
    outs = refs[sum(shape) + 4 :]
    size = tile_of(product.shape[0])
    for at in range(0, product.shape[0], size):
        tile = pl.ds(at, size)
        total = partial[tile, :]
        for mask, block in zip(masks, groups):
            total += block_term(block, rows, here, mask, tile)
        product[tile, :] = total.astype(product.dtype)
    apply_body(0, scale, here, projector, product, *outs)


def apply_body(first, scale, here, projector, product, *outs):
    size = outs[0].shape[0] * len(outs)
    term = jnp.dot(
        projector[pl.ds(first, size), :], product[...], preferred_element_type=jnp.float32
    )
    for k, out in enumerate(outs):
        count = out.shape[0]
        out[...] = (term[k * count : (k + 1) * count] * scale).astype(out.dtype)


def project(blocks, here, layer_input, partial, projector, pieces, scale):
    kv, width = partial.shape
    half = projector.shape[0] // 2
    shape = [len(block) for block in blocks.values()]
    product, *sends = call_in_vmem(
        functools.partial(project_body, list(blocks), shape, scale),
        here,
        flat(blocks) + [layer_input, partial, projector],
        [jax.ShapeDtypeStruct((kv, width), jnp.bfloat16)]
        + [jax.ShapeDtypeStruct((half // pieces, width), jnp.bfloat16)] * pieces,
        2 * depth(blocks) * kv * width + 2 * half * kv * width,
    )
    return product, sends


def apply_rest(projector, product, here, pieces, scale):
    half = projector.shape[0] // 2
    kv, width = product.shape
    return call_in_vmem(
        functools.partial(apply_body, half, scale),
        here,
        [projector, product],
        [jax.ShapeDtypeStruct((half // pieces, width), jnp.float32)] * pieces,
        2 * half * kv * width,
    )


def on_device(layer_input, cotangent, candidates, moment_first, moment_second, owners):
    replicas = lax.axis_size("dp")
    members = lax.axis_size("fsdp")
    me_dp = lax.axis_index("dp")
    me_fsdp = lax.axis_index("fsdp")
    dp_bits = bits_of(replicas)
    far_bits = bits_of(members)[1:]
    scale = 1.0 / math.sqrt(layer_input.shape[0] * replicas)
    kv_share = candidates.shape[2] // replicas
    per = members // replicas

    order = [0]
    for bit in reversed(dp_bits):
        order = [mask ^ bit for mask in order] + order

    here = jnp.stack([me_dp, me_fsdp]).astype(jnp.int32)

    def owned(value, others, tokens):
        for at, bit in enumerate(dp_bits):
            if at == 1 and others:
                value = after(value, others, tokens)
            other = swap(value, "dp", bit)
            mine = (me_dp & bit) == (owners & bit)
            rows = jnp.repeat(mine, value.shape[0] // MATS)[:, None]
            value = jnp.where(rows, value, other)
        return value

    pieces = max(replicas // 2, 1)
    tokens, tokens_1 = [], []

    near, far, arrived = spread_near(cotangent[0], far_bits, tokens)
    both = jnp.swapaxes(candidates[:, 0], 1, 2).reshape(-1, candidates.shape[2])
    both = owned(both, arrived, tokens)
    later = [piece for mask in far_bits for piece in near.get(mask, ())]
    later = [piece for piece in later if all(piece is not other for other in arrived)]
    blocks = spread(after(both, later + flat(far), tokens), far_bits)
    same = jnp.concatenate([blocks[mask] for mask in sorted(blocks)], axis=0)
    near_all = with_partner(near)
    partial = add_products(near_all, here, layer_input)
    far_all = with_partner(far)
    same = after(same, [partial], tokens)
    projectors = gather_projector(same, swap(same, "fsdp", 1), here, order, per, tokens)
    product, send_0 = project(far_all, here, layer_input, partial, projectors[0], pieces, scale)
    keep_0 = apply_rest(projectors[0], product, here, pieces, scale)
    arrived_0 = [swap(piece, "dp", dp_bits[0]) for piece in send_0]

    def reduced(arrived, keeps):
        for bit in dp_bits[1:]:
            totals = [keep + piece.astype(jnp.float32) for piece, keep in zip(arrived, keeps)]
            half = len(totals) // 2
            arrived = [swap(total.astype(jnp.bfloat16), "dp", bit) for total in totals[:half]]
            keeps = totals[half:]
        return keeps[0], arrived[0]

    heads = lax.dot_general(
        cotangent[1], projectors[1], (((1,), (1,)), ((), ())), preferred_element_type=jnp.float32
    ).astype(jnp.bfloat16)
    blocks = spread(heads, far_bits)
    open_0 = reduced(arrived_0, keep_0)
    tokens_1 += arrived_0[pieces // 2 :]
    blocks = with_partner({mask: [held] for mask, held in blocks.items()})
    send_1 = heads_product(blocks, here, layer_input, 0, pieces, jnp.bfloat16, scale, tokens_1)
    keep_1 = heads_product(blocks, here, layer_input, 1, pieces, jnp.float32, scale)
    arrived_1 = [swap(piece, "dp", dp_bits[0]) for piece in send_1]

    updates, firsts, seconds, gathered = [], [], [], []
    open_1 = list(reduced(arrived_1, keep_1))
    for matrix, (keep, received) in enumerate((open_0, open_1)):
        if gathered:
            received, firsts[0], *gathered[0][:-1] = lax.optimization_barrier(
                (received, firsts[0], *gathered[0][:-1])
            )
        projected = keep + received.astype(jnp.float32)
        first = beta_first * moment_first[matrix] + (1.0 - beta_first) * projected
        second = beta_second * moment_second[matrix] + (1.0 - beta_second) * projected * projected
        direction = (
            first
            / (1.0 - beta_first**STEP)
            / (jnp.sqrt(second / (1.0 - beta_second**STEP)) + epsilon)
        )
        parts = [direction.astype(jnp.bfloat16)]
        for bit in reversed(dp_bits):
            if matrix == 0 and bit == dp_bits[0] and len(parts) > 1:
                parts[0], open_1[0] = lax.optimization_barrier((parts[0], open_1[0]))
            parts = [swap(piece, "dp", bit) for piece in parts] + parts
        gathered.append(parts)
        firsts.append(first)
        seconds.append(second)
    for parts, projector in zip(gathered, projectors):
        own = lax.dynamic_slice_in_dim(projector, me_dp * kv_share, kv_share, 1)
        update = lax.dot_general(
            own, jnp.concatenate(parts, axis=0), TRANSPOSED, preferred_element_type=jnp.float32
        )
        updates.append(update.astype(jnp.bfloat16))
    update = jnp.zeros((MATS,) + updates[0].shape, updates[0].dtype)
    for matrix in range(MATS):
        update = lax.dynamic_update_slice(update, updates[matrix][None], (matrix, 0, 0))
    return (update, jnp.stack(firsts), jnp.stack(seconds))


def solution(mesh):
    placed = (
        P("dp", "fsdp"),
        P(None, ("dp", "fsdp"), None),
        P(None, "dp", None, "fsdp"),
        P(None, "dp", "fsdp"),
        P(None, "dp", "fsdp"),
        P(),
    )
    return jax.shard_map(
        on_device,
        mesh=mesh,
        in_specs=placed,
        out_specs=(P(None, "dp", "fsdp"), P(None, "dp", "fsdp"), P(None, "dp", "fsdp")),
        check_vma=False,
    )
```

```python
import functools
import math

import jax
import jax.numpy as jnp
from jax import lax
from jax.experimental import pallas as pl
from jax.experimental.pallas import tpu as pltpu
from jax.sharding import PartitionSpec as P

MATS = 2
STEP = 10

beta_first = 0.9
beta_second = 0.999
epsilon = 1e-08

TRANSPOSED = (((0,), (0,)), ((), ()))
MIB = 1 << 20


def swap(value, axis, mask):
    size = lax.axis_size(axis)
    return lax.ppermute(value, axis, [(i, i ^ mask) for i in range(size)])


def bits_of(size):
    return [1 << k for k in range(size.bit_length() - 1)]


def after(value, others, tokens):
    corners = [other[:16, :128] for other in others]
    value, *held = lax.optimization_barrier((value, *corners))
    tokens.extend(held)
    return value


def spread(block, bits):
    if len(bits) == 2:
        low, high = bits
        masks = (0, low, high, low | high)
        return {mask: swap(block, "fsdp", mask) if mask else block for mask in masks}
    blocks = {0: block}
    for bit in bits:
        blocks.update({mask ^ bit: swap(held, "fsdp", bit) for mask, held in list(blocks.items())})
    return blocks


def spread_near(block, bits, tokens):
    if len(bits) == 2:
        low, high = bits
        half = block.shape[0] // 2
        top, bottom = block[:half], block[half:]
        low_top, high_bottom = swap(top, "fsdp", low), swap(bottom, "fsdp", high)
        far = [swap(low_top, "fsdp", high), swap(high_bottom, "fsdp", low)]
        by_low = [low_top, swap(after(bottom, [low_top], tokens), "fsdp", low)]
        by_high = [swap(after(top, [high_bottom], tokens), "fsdp", high), high_bottom]
        first = [low_top, high_bottom]
        return {0: [block], low: by_low, high: by_high}, {low | high: far}, first
    blocks = {mask: [held] for mask, held in spread(block, bits).items()}
    last = max(blocks)
    near = {mask: held for mask, held in blocks.items() if mask != last}
    return near, {last: blocks[last]}, []


def with_partner(blocks, own=None):
    other = {
        mask ^ 1: [own] if mask == 0 and own is not None else [swap(x, "fsdp", 1) for x in held]
        for mask, held in blocks.items()
    }
    return {**blocks, **other}


def tile_of(size):
    return min(size, 256)


def whole(shape):
    return pl.BlockSpec(shape, lambda *_: (0,) * len(shape))


def gather_body(order, per, count, here, same, other, *refs):
    for matrix, out in enumerate(refs[-MATS:]):
        spot = 0
        for mask in order:
            for sub in range(per):
                away = ((here[0] ^ mask) * per + sub) ^ here[1]
                at = pl.multiple_of(((away >> 1) * MATS + matrix) * count, count)
                out[pl.ds(spot * count, count), :] = jnp.where(
                    (away & 1) == 0, same[pl.ds(at, count), :], other[pl.ds(at, count), :]
                )
                spot += 1


def gather_projector(same, other, here, order, per, tokens):
    rows, kv = same.shape
    rank = 2 * rows // MATS
    return pl.pallas_call(
        functools.partial(gather_body, order, per, rank // (len(order) * per)),
        grid_spec=pltpu.PrefetchScalarGridSpec(
            num_scalar_prefetch=1,
            grid=(1,),
            in_specs=[whole((rows, kv))] * 2
            + [pl.BlockSpec(memory_space=pl.ANY)] * len(tokens),
            out_specs=[whole((rank, kv))] * MATS,
        ),
        out_shape=[jax.ShapeDtypeStruct((rank, kv), same.dtype)] * MATS,
        compiler_params=pltpu.CompilerParams(vmem_limit_bytes=16 * MIB),
        cost_estimate=pl.CostEstimate(flops=0, bytes_accessed=8 * rows * kv, transcendentals=0),
    )(here, same, other, *tokens)


def block_term(block, rows, here, mask, tile):
    pieces = [piece[:, tile] for piece in block]
    left = pieces[0] if len(pieces) == 1 else jnp.concatenate(pieces, axis=0)
    count = left.shape[0]
    start = pl.multiple_of((here[1] ^ mask) * count, count)
    return lax.dot_general(
        left, rows[pl.ds(start, count), :], TRANSPOSED, preferred_element_type=jnp.float32
    )


def regroup(refs, shape):
    refs = list(refs)
    return [[refs.pop(0) for _ in range(length)] for length in shape]


def call_in_vmem(body, here, operands, outputs, flops, tokens=()):
    moved = sum(x.size * x.dtype.itemsize for x in list(operands) + list(outputs))
    vmem = pl.BlockSpec(memory_space=pltpu.VMEM)
    return pl.pallas_call(
        body,
        grid_spec=pltpu.PrefetchScalarGridSpec(
            num_scalar_prefetch=1,
            grid=(),
            in_specs=[vmem] * len(operands) + [pl.BlockSpec(memory_space=pl.ANY)] * len(tokens),
            out_specs=[vmem] * len(outputs),
        ),
        out_shape=outputs,
        compiler_params=pltpu.CompilerParams(vmem_limit_bytes=20 * MIB),
        cost_estimate=pl.CostEstimate(
            flops=int(flops), bytes_accessed=int(moved), transcendentals=0
        ),
    )(here, *operands, *tokens)


def flat(blocks):
    return [piece for block in blocks.values() for piece in block]


def depth(blocks):
    return sum(piece.shape[0] for piece in flat(blocks))


def heads_body(masks, shape, part, pieces, scale, here, *refs):
    groups = regroup(refs[: sum(shape)], shape)
    rows, outs = refs[sum(shape)], refs[-pieces:]
    size = outs[0].shape[0] * len(outs)
    total = None
    for mask, block in zip(masks, groups):
        term = block_term(block, rows, here, mask, pl.ds(part * size, size))
        total = term if total is None else total + term
    for k, out in enumerate(outs):
        count = out.shape[0]
        out[...] = (total[k * count : (k + 1) * count] * scale).astype(out.dtype)


def heads_product(blocks, here, layer_input, part, pieces, dtype, scale, tokens=()):
    half = flat(blocks)[0].shape[1] // 2
    width = layer_input.shape[1]
    shape = [len(block) for block in blocks.values()]
    return call_in_vmem(
        functools.partial(heads_body, list(blocks), shape, part, pieces, scale),
        here,
        flat(blocks) + [layer_input],
        [jax.ShapeDtypeStruct((half // pieces, width), dtype)] * pieces,
        2 * depth(blocks) * half * width,
        tokens,
    )


def product_body(shape, here, *refs):
    groups = regroup(refs[: sum(shape)], shape)
    out = refs[-1]
    total = None
    for block, rows in zip(groups, refs[sum(shape) : -1]):
        pieces = [piece[...] for piece in block]
        left = pieces[0] if len(pieces) == 1 else jnp.concatenate(pieces, axis=0)
        term = lax.dot_general(left, rows[...], TRANSPOSED, preferred_element_type=jnp.float32)
        total = term if total is None else total + term
    out[...] = total


def row_blocks(blocks, width):
    def at(mask, i, here):
        return here[1] ^ mask, 0

    return [
        pl.BlockSpec((depth({mask: block}), width), functools.partial(at, mask))
        for mask, block in blocks.items()
    ]


def add_products(blocks, here, layer_input):
    kv = flat(blocks)[0].shape[1]
    width = layer_input.shape[1]
    tile = tile_of(kv)
    shape = [len(block) for block in blocks.values()]
    return pl.pallas_call(
        functools.partial(product_body, shape),
        grid_spec=pltpu.PrefetchScalarGridSpec(
            num_scalar_prefetch=1,
            grid=(kv // tile,),
            in_specs=[
                pl.BlockSpec((piece.shape[0], tile), lambda i, here: (0, i))
                for piece in flat(blocks)
            ]
            + row_blocks(blocks, width),
            out_specs=pl.BlockSpec((tile, width), lambda i, here: (i, 0)),
        ),
        out_shape=jax.ShapeDtypeStruct((kv, width), jnp.float32),
        compiler_params=pltpu.CompilerParams(vmem_limit_bytes=20 * MIB),
        cost_estimate=pl.CostEstimate(
            flops=2 * depth(blocks) * kv * width,
            bytes_accessed=2 * depth(blocks) * (kv + width) + 4 * kv * width,
            transcendentals=0,
        ),
    )(here, *flat(blocks), *([layer_input] * len(blocks)))


def project_body(masks, shape, scale, here, *refs):
    groups = regroup(refs[: sum(shape)], shape)
    rows, partial, projector, product = refs[sum(shape) : sum(shape) + 4]
    outs = refs[sum(shape) + 4 :]
    size = tile_of(product.shape[0])
    for at in range(0, product.shape[0], size):
        tile = pl.ds(at, size)
        total = partial[tile, :]
        for mask, block in zip(masks, groups):
            total += block_term(block, rows, here, mask, tile)
        product[tile, :] = total.astype(product.dtype)
    apply_body(0, scale, here, projector, product, *outs)


def apply_body(first, scale, here, projector, product, *outs):
    size = outs[0].shape[0] * len(outs)
    term = jnp.dot(
        projector[pl.ds(first, size), :], product[...], preferred_element_type=jnp.float32
    )
    for k, out in enumerate(outs):
        count = out.shape[0]
        out[...] = (term[k * count : (k + 1) * count] * scale).astype(out.dtype)


def project(blocks, here, layer_input, partial, projector, pieces, scale):
    kv, width = partial.shape
    half = projector.shape[0] // 2
    shape = [len(block) for block in blocks.values()]
    product, *sends = call_in_vmem(
        functools.partial(project_body, list(blocks), shape, scale),
        here,
        flat(blocks) + [layer_input, partial, projector],
        [jax.ShapeDtypeStruct((kv, width), jnp.bfloat16)]
        + [jax.ShapeDtypeStruct((half // pieces, width), jnp.bfloat16)] * pieces,
        2 * depth(blocks) * kv * width + 2 * half * kv * width,
    )
    return product, sends


def apply_rest(projector, product, here, pieces, scale):
    half = projector.shape[0] // 2
    kv, width = product.shape
    return call_in_vmem(
        functools.partial(apply_body, half, scale),
        here,
        [projector, product],
        [jax.ShapeDtypeStruct((half // pieces, width), jnp.float32)] * pieces,
        2 * half * kv * width,
    )


def on_device(layer_input, cotangent, candidates, moment_first, moment_second, owners):
    replicas = lax.axis_size("dp")
    members = lax.axis_size("fsdp")
    me_dp = lax.axis_index("dp")
    me_fsdp = lax.axis_index("fsdp")
    dp_bits = bits_of(replicas)
    far_bits = bits_of(members)[1:]
    scale = 1.0 / math.sqrt(layer_input.shape[0] * replicas)
    kv_share = candidates.shape[2] // replicas
    per = members // replicas

    order = [0]
    for bit in reversed(dp_bits):
        order = [mask ^ bit for mask in order] + order

    here = jnp.stack([me_dp, me_fsdp]).astype(jnp.int32)

    def owned(value, others, tokens):
        for at, bit in enumerate(dp_bits):
            if at == 1 and others:
                value = after(value, others, tokens)
            other = swap(value, "dp", bit)
            mine = (me_dp & bit) == (owners & bit)
            rows = jnp.repeat(mine, value.shape[0] // MATS)[:, None]
            value = jnp.where(rows, value, other)
        return value

    pieces = max(replicas // 2, 1)
    tokens, tokens_1 = [], []

    near, far, arrived = spread_near(cotangent[0], far_bits, tokens)
    both = jnp.swapaxes(candidates[:, 0], 1, 2).reshape(-1, candidates.shape[2])
    both = owned(both, arrived, tokens)
    later = [piece for mask in far_bits for piece in near.get(mask, ())]
    later = [piece for piece in later if all(piece is not other for other in arrived)]
    blocks = spread(after(both, later + flat(far), tokens), far_bits)
    same = jnp.concatenate([blocks[mask] for mask in sorted(blocks)], axis=0)
    near_all = with_partner(near)
    partial = add_products(near_all, here, layer_input)
    far_all = with_partner(far)
    same = after(same, [partial], tokens)
    projectors = gather_projector(same, swap(same, "fsdp", 1), here, order, per, tokens)
    product, send_0 = project(far_all, here, layer_input, partial, projectors[0], pieces, scale)
    keep_0 = apply_rest(projectors[0], product, here, pieces, scale)
    arrived_0 = [swap(piece, "dp", dp_bits[0]) for piece in send_0]

    def reduced(arrived, keeps):
        for bit in dp_bits[1:]:
            totals = [keep + piece.astype(jnp.float32) for piece, keep in zip(arrived, keeps)]
            half = len(totals) // 2
            arrived = [swap(total.astype(jnp.bfloat16), "dp", bit) for total in totals[:half]]
            keeps = totals[half:]
        return keeps[0], arrived[0]

    heads = lax.dot_general(
        cotangent[1], projectors[1], (((1,), (1,)), ((), ())), preferred_element_type=jnp.float32
    ).astype(jnp.bfloat16)
    blocks = spread(heads, far_bits)
    open_0 = reduced(arrived_0, keep_0)
    tokens_1 += arrived_0[pieces // 2 :]
    blocks = with_partner({mask: [held] for mask, held in blocks.items()})
    send_1 = heads_product(blocks, here, layer_input, 0, pieces, jnp.bfloat16, scale, tokens_1)
    keep_1 = heads_product(blocks, here, layer_input, 1, pieces, jnp.float32, scale)
    arrived_1 = [swap(piece, "dp", dp_bits[0]) for piece in send_1]

    updates, firsts, seconds, gathered = [], [], [], []
    open_1 = list(reduced(arrived_1, keep_1))
    for matrix, (keep, received) in enumerate((open_0, open_1)):
        if gathered:
            received, firsts[0], *gathered[0][-3:-1] = lax.optimization_barrier(
                (received, firsts[0], *gathered[0][-3:-1])
            )
        projected = keep + received.astype(jnp.float32)
        first = beta_first * moment_first[matrix] + (1.0 - beta_first) * projected
        second = beta_second * moment_second[matrix] + (1.0 - beta_second) * projected * projected
        direction = (
            first
            / (1.0 - beta_first**STEP)
            / (jnp.sqrt(second / (1.0 - beta_second**STEP)) + epsilon)
        )
        parts = [direction.astype(jnp.bfloat16)]
        for bit in reversed(dp_bits):
            if matrix == 0 and bit == dp_bits[0] and len(parts) > 1:
                parts[0], open_1[0] = lax.optimization_barrier((parts[0], open_1[0]))
            parts = [swap(piece, "dp", bit) for piece in parts] + parts
        gathered.append(parts)
        firsts.append(first)
        seconds.append(second)
    for parts, projector in zip(gathered, projectors):
        own = lax.dynamic_slice_in_dim(projector, me_dp * kv_share, kv_share, 1)
        update = lax.dot_general(
            own, jnp.concatenate(parts, axis=0), TRANSPOSED, preferred_element_type=jnp.float32
        )
        updates.append(update.astype(jnp.bfloat16))
    update = jnp.zeros((MATS,) + updates[0].shape, updates[0].dtype)
    for matrix in range(MATS):
        update = lax.dynamic_update_slice(update, updates[matrix][None], (matrix, 0, 0))
    return (update, jnp.stack(firsts), jnp.stack(seconds))


def solution(mesh):
    placed = (
        P("dp", "fsdp"),
        P(None, ("dp", "fsdp"), None),
        P(None, "dp", None, "fsdp"),
        P(None, "dp", "fsdp"),
        P(None, "dp", "fsdp"),
        P(),
    )
    return jax.shard_map(
        on_device,
        mesh=mesh,
        in_specs=placed,
        out_specs=(P(None, "dp", "fsdp"), P(None, "dp", "fsdp"), P(None, "dp", "fsdp")),
        check_vma=False,
    )
```

```python
import functools
import math

import jax
import jax.numpy as jnp
from jax import lax
from jax.experimental import pallas as pl
from jax.experimental.pallas import tpu as pltpu
from jax.sharding import PartitionSpec as P

MATS = 2
STEP = 10

beta_first = 0.9
beta_second = 0.999
epsilon = 1e-08

TRANSPOSED = (((0,), (0,)), ((), ()))
MIB = 1 << 20


def swap(value, axis, mask):
    size = lax.axis_size(axis)
    return lax.ppermute(value, axis, [(i, i ^ mask) for i in range(size)])


def bits_of(size):
    return [1 << k for k in range(size.bit_length() - 1)]


def after(value, others, tokens):
    corners = [other[:16, :128] for other in others]
    value, *held = lax.optimization_barrier((value, *corners))
    tokens.extend(held)
    return value


def spread(block, bits):
    if len(bits) == 2:
        low, high = bits
        masks = (0, low, high, low | high)
        return {mask: swap(block, "fsdp", mask) if mask else block for mask in masks}
    blocks = {0: block}
    for bit in bits:
        blocks.update({mask ^ bit: swap(held, "fsdp", bit) for mask, held in list(blocks.items())})
    return blocks


def spread_near(block, bits, tokens):
    if len(bits) == 2:
        low, high = bits
        half = block.shape[0] // 2
        top, bottom = block[:half], block[half:]
        low_top, high_bottom = swap(top, "fsdp", low), swap(bottom, "fsdp", high)
        far = [swap(low_top, "fsdp", high), swap(high_bottom, "fsdp", low)]
        by_low = [low_top, swap(after(bottom, [low_top], tokens), "fsdp", low)]
        by_high = [swap(after(top, [high_bottom], tokens), "fsdp", high), high_bottom]
        first = [low_top, high_bottom]
        return {0: [block], low: by_low, high: by_high}, {low | high: far}, first
    blocks = {mask: [held] for mask, held in spread(block, bits).items()}
    last = max(blocks)
    near = {mask: held for mask, held in blocks.items() if mask != last}
    return near, {last: blocks[last]}, []


def with_partner(blocks, own=None):
    other = {
        mask ^ 1: [own] if mask == 0 and own is not None else [swap(x, "fsdp", 1) for x in held]
        for mask, held in blocks.items()
    }
    return {**blocks, **other}


def tile_of(size):
    return min(size, 256)


def whole(shape):
    return pl.BlockSpec(shape, lambda *_: (0,) * len(shape))


def gather_body(order, per, count, here, same, other, *refs):
    for matrix, out in enumerate(refs[-MATS:]):
        spot = 0
        for mask in order:
            for sub in range(per):
                away = ((here[0] ^ mask) * per + sub) ^ here[1]
                at = pl.multiple_of(((away >> 1) * MATS + matrix) * count, count)
                out[pl.ds(spot * count, count), :] = jnp.where(
                    (away & 1) == 0, same[pl.ds(at, count), :], other[pl.ds(at, count), :]
                )
                spot += 1


def gather_projector(same, other, here, order, per, tokens):
    rows, kv = same.shape
    rank = 2 * rows // MATS
    return pl.pallas_call(
        functools.partial(gather_body, order, per, rank // (len(order) * per)),
        grid_spec=pltpu.PrefetchScalarGridSpec(
            num_scalar_prefetch=1,
            grid=(1,),
            in_specs=[whole((rows, kv))] * 2
            + [pl.BlockSpec(memory_space=pl.ANY)] * len(tokens),
            out_specs=[whole((rank, kv))] * MATS,
        ),
        out_shape=[jax.ShapeDtypeStruct((rank, kv), same.dtype)] * MATS,
        compiler_params=pltpu.CompilerParams(vmem_limit_bytes=16 * MIB),
        cost_estimate=pl.CostEstimate(flops=0, bytes_accessed=8 * rows * kv, transcendentals=0),
    )(here, same, other, *tokens)


def block_term(block, rows, here, mask, tile):
    pieces = [piece[:, tile] for piece in block]
    left = pieces[0] if len(pieces) == 1 else jnp.concatenate(pieces, axis=0)
    count = left.shape[0]
    start = pl.multiple_of((here[1] ^ mask) * count, count)
    return lax.dot_general(
        left, rows[pl.ds(start, count), :], TRANSPOSED, preferred_element_type=jnp.float32
    )


def regroup(refs, shape):
    refs = list(refs)
    return [[refs.pop(0) for _ in range(length)] for length in shape]


def call_in_vmem(body, here, operands, outputs, flops, tokens=()):
    moved = sum(x.size * x.dtype.itemsize for x in list(operands) + list(outputs))
    vmem = pl.BlockSpec(memory_space=pltpu.VMEM)
    return pl.pallas_call(
        body,
        grid_spec=pltpu.PrefetchScalarGridSpec(
            num_scalar_prefetch=1,
            grid=(),
            in_specs=[vmem] * len(operands) + [pl.BlockSpec(memory_space=pl.ANY)] * len(tokens),
            out_specs=[vmem] * len(outputs),
        ),
        out_shape=outputs,
        compiler_params=pltpu.CompilerParams(vmem_limit_bytes=20 * MIB),
        cost_estimate=pl.CostEstimate(
            flops=int(flops), bytes_accessed=int(moved), transcendentals=0
        ),
    )(here, *operands, *tokens)


def flat(blocks):
    return [piece for block in blocks.values() for piece in block]


def depth(blocks):
    return sum(piece.shape[0] for piece in flat(blocks))


def heads_body(masks, shape, part, pieces, scale, here, *refs):
    groups = regroup(refs[: sum(shape)], shape)
    rows, outs = refs[sum(shape)], refs[-pieces:]
    size = outs[0].shape[0] * len(outs)
    total = None
    for mask, block in zip(masks, groups):
        term = block_term(block, rows, here, mask, pl.ds(part * size, size))
        total = term if total is None else total + term
    for k, out in enumerate(outs):
        count = out.shape[0]
        out[...] = (total[k * count : (k + 1) * count] * scale).astype(out.dtype)


def heads_product(blocks, here, layer_input, part, pieces, dtype, scale, tokens=()):
    half = flat(blocks)[0].shape[1] // 2
    width = layer_input.shape[1]
    shape = [len(block) for block in blocks.values()]
    return call_in_vmem(
        functools.partial(heads_body, list(blocks), shape, part, pieces, scale),
        here,
        flat(blocks) + [layer_input],
        [jax.ShapeDtypeStruct((half // pieces, width), dtype)] * pieces,
        2 * depth(blocks) * half * width,
        tokens,
    )


def product_body(shape, here, *refs):
    groups = regroup(refs[: sum(shape)], shape)
    out = refs[-1]
    total = None
    for block, rows in zip(groups, refs[sum(shape) : -1]):
        pieces = [piece[...] for piece in block]
        left = pieces[0] if len(pieces) == 1 else jnp.concatenate(pieces, axis=0)
        term = lax.dot_general(left, rows[...], TRANSPOSED, preferred_element_type=jnp.float32)
        total = term if total is None else total + term
    out[...] = total


def row_blocks(blocks, width):
    def at(mask, i, here):
        return here[1] ^ mask, 0

    return [
        pl.BlockSpec((depth({mask: block}), width), functools.partial(at, mask))
        for mask, block in blocks.items()
    ]


def add_products(blocks, here, layer_input):
    kv = flat(blocks)[0].shape[1]
    width = layer_input.shape[1]
    tile = tile_of(kv)
    shape = [len(block) for block in blocks.values()]
    return pl.pallas_call(
        functools.partial(product_body, shape),
        grid_spec=pltpu.PrefetchScalarGridSpec(
            num_scalar_prefetch=1,
            grid=(kv // tile,),
            in_specs=[
                pl.BlockSpec((piece.shape[0], tile), lambda i, here: (0, i))
                for piece in flat(blocks)
            ]
            + row_blocks(blocks, width),
            out_specs=pl.BlockSpec((tile, width), lambda i, here: (i, 0)),
        ),
        out_shape=jax.ShapeDtypeStruct((kv, width), jnp.float32),
        compiler_params=pltpu.CompilerParams(vmem_limit_bytes=20 * MIB),
        cost_estimate=pl.CostEstimate(
            flops=2 * depth(blocks) * kv * width,
            bytes_accessed=2 * depth(blocks) * (kv + width) + 4 * kv * width,
            transcendentals=0,
        ),
    )(here, *flat(blocks), *([layer_input] * len(blocks)))


def project_body(masks, shape, scale, here, *refs):
    groups = regroup(refs[: sum(shape)], shape)
    rows, partial, projector, product = refs[sum(shape) : sum(shape) + 4]
    outs = refs[sum(shape) + 4 :]
    size = tile_of(product.shape[0])
    for at in range(0, product.shape[0], size):
        tile = pl.ds(at, size)
        total = partial[tile, :]
        for mask, block in zip(masks, groups):
            total += block_term(block, rows, here, mask, tile)
        product[tile, :] = total.astype(product.dtype)
    apply_body(0, scale, here, projector, product, *outs)


def apply_body(first, scale, here, projector, product, *outs):
    size = outs[0].shape[0] * len(outs)
    term = jnp.dot(
        projector[pl.ds(first, size), :], product[...], preferred_element_type=jnp.float32
    )
    for k, out in enumerate(outs):
        count = out.shape[0]
        out[...] = (term[k * count : (k + 1) * count] * scale).astype(out.dtype)


def project(blocks, here, layer_input, partial, projector, pieces, scale):
    kv, width = partial.shape
    half = projector.shape[0] // 2
    shape = [len(block) for block in blocks.values()]
    product, *sends = call_in_vmem(
        functools.partial(project_body, list(blocks), shape, scale),
        here,
        flat(blocks) + [layer_input, partial, projector],
        [jax.ShapeDtypeStruct((kv, width), jnp.bfloat16)]
        + [jax.ShapeDtypeStruct((half // pieces, width), jnp.bfloat16)] * pieces,
        2 * depth(blocks) * kv * width + 2 * half * kv * width,
    )
    return product, sends


def apply_rest(projector, product, here, pieces, scale):
    half = projector.shape[0] // 2
    kv, width = product.shape
    return call_in_vmem(
        functools.partial(apply_body, half, scale),
        here,
        [projector, product],
        [jax.ShapeDtypeStruct((half // pieces, width), jnp.float32)] * pieces,
        2 * half * kv * width,
    )


def on_device(layer_input, cotangent, candidates, moment_first, moment_second, owners):
    replicas = lax.axis_size("dp")
    members = lax.axis_size("fsdp")
    me_dp = lax.axis_index("dp")
    me_fsdp = lax.axis_index("fsdp")
    dp_bits = bits_of(replicas)
    far_bits = bits_of(members)[1:]
    scale = 1.0 / math.sqrt(layer_input.shape[0] * replicas)
    kv_share = candidates.shape[2] // replicas
    per = members // replicas

    order = [0]
    for bit in reversed(dp_bits):
        order = [mask ^ bit for mask in order] + order

    here = jnp.stack([me_dp, me_fsdp]).astype(jnp.int32)

    def owned(value, others, tokens):
        for at, bit in enumerate(dp_bits):
            if at == 1 and others:
                value = after(value, others, tokens)
            other = swap(value, "dp", bit)
            mine = (me_dp & bit) == (owners & bit)
            rows = jnp.repeat(mine, value.shape[0] // MATS)[:, None]
            value = jnp.where(rows, value, other)
        return value

    pieces = max(replicas // 2, 1)
    tokens, tokens_1 = [], []

    near, far, arrived = spread_near(cotangent[0], far_bits, tokens)
    both = jnp.swapaxes(candidates[:, 0], 1, 2).reshape(-1, candidates.shape[2])
    both = owned(both, arrived, tokens)
    later = [piece for mask in far_bits for piece in near.get(mask, ())]
    later = [piece for piece in later if all(piece is not other for other in arrived)]
    blocks = spread(after(both, later + flat(far), tokens), far_bits)
    same = jnp.concatenate([blocks[mask] for mask in sorted(blocks)], axis=0)
    near_all = with_partner(near)
    partial = add_products(near_all, here, layer_input)
    far_all = with_partner(far)
    same = after(same, [partial], tokens)
    projectors = gather_projector(same, swap(same, "fsdp", 1), here, order, per, tokens)
    product, send_0 = project(far_all, here, layer_input, partial, projectors[0], pieces, scale)
    keep_0 = apply_rest(projectors[0], product, here, pieces, scale)
    arrived_0 = [swap(piece, "dp", dp_bits[0]) for piece in send_0]

    def reduced(arrived, keeps):
        for bit in dp_bits[1:]:
            totals = [keep + piece.astype(jnp.float32) for piece, keep in zip(arrived, keeps)]
            half = len(totals) // 2
            arrived = [swap(total.astype(jnp.bfloat16), "dp", bit) for total in totals[:half]]
            keeps = totals[half:]
        return keeps[0], arrived[0]

    heads = lax.dot_general(
        cotangent[1], projectors[1], (((1,), (1,)), ((), ())), preferred_element_type=jnp.float32
    ).astype(jnp.bfloat16)
    blocks = spread(heads, far_bits)
    open_0 = reduced(arrived_0, keep_0)
    blocks = with_partner({mask: [held] for mask, held in blocks.items()})
    send_1 = heads_product(blocks, here, layer_input, 0, pieces, jnp.bfloat16, scale, tokens_1)
    keep_1 = heads_product(
        blocks, here, layer_input, 1, pieces, jnp.float32, scale, arrived_0[pieces // 2 :]
    )
    arrived_1 = [swap(piece, "dp", dp_bits[0]) for piece in send_1]

    updates, firsts, seconds, gathered = [], [], [], []
    open_1 = list(reduced(arrived_1, keep_1))
    for matrix, (keep, received) in enumerate((open_0, open_1)):
        if gathered:
            received, firsts[0], *gathered[0][-3:-1] = lax.optimization_barrier(
                (received, firsts[0], *gathered[0][-3:-1])
            )
        projected = keep + received.astype(jnp.float32)
        first = beta_first * moment_first[matrix] + (1.0 - beta_first) * projected
        second = beta_second * moment_second[matrix] + (1.0 - beta_second) * projected * projected
        direction = (
            first
            / (1.0 - beta_first**STEP)
            / (jnp.sqrt(second / (1.0 - beta_second**STEP)) + epsilon)
        )
        parts = [direction.astype(jnp.bfloat16)]
        for bit in reversed(dp_bits):
            if matrix == 0 and bit == dp_bits[0] and len(parts) > 1:
                parts[0], open_1[0] = lax.optimization_barrier((parts[0], open_1[0]))
            parts = [swap(piece, "dp", bit) for piece in parts] + parts
        gathered.append(parts)
        firsts.append(first)
        seconds.append(second)
    for parts, projector in zip(gathered, projectors):
        own = lax.dynamic_slice_in_dim(projector, me_dp * kv_share, kv_share, 1)
        update = lax.dot_general(
            own, jnp.concatenate(parts, axis=0), TRANSPOSED, preferred_element_type=jnp.float32
        )
        updates.append(update.astype(jnp.bfloat16))
    update = jnp.zeros((MATS,) + updates[0].shape, updates[0].dtype)
    for matrix in range(MATS):
        update = lax.dynamic_update_slice(update, updates[matrix][None], (matrix, 0, 0))
    return (update, jnp.stack(firsts), jnp.stack(seconds))


def solution(mesh):
    placed = (
        P("dp", "fsdp"),
        P(None, ("dp", "fsdp"), None),
        P(None, "dp", None, "fsdp"),
        P(None, "dp", "fsdp"),
        P(None, "dp", "fsdp"),
        P(),
    )
    return jax.shard_map(
        on_device,
        mesh=mesh,
        in_specs=placed,
        out_specs=(P(None, "dp", "fsdp"), P(None, "dp", "fsdp"), P(None, "dp", "fsdp")),
        check_vma=False,
    )
```

```python
import functools
import math

import jax
import jax.numpy as jnp
from jax import lax
from jax.experimental import pallas as pl
from jax.experimental.pallas import tpu as pltpu
from jax.sharding import PartitionSpec as P

MATS = 2
STEP = 10

beta_first = 0.9
beta_second = 0.999
epsilon = 1e-08

TRANSPOSED = (((0,), (0,)), ((), ()))
MIB = 1 << 20
CUTS = 2


def swap(value, axis, mask):
    size = lax.axis_size(axis)
    return lax.ppermute(value, axis, [(i, i ^ mask) for i in range(size)])


def bits_of(size):
    return [1 << k for k in range(size.bit_length() - 1)]


def after(value, others, tokens):
    corners = [other[:16, :128] for other in others]
    value, *held = lax.optimization_barrier((value, *corners))
    tokens.extend(held)
    return value


def spread(block, bits):
    if len(bits) == 2:
        low, high = bits
        masks = (0, low, high, low | high)
        return {mask: swap(block, "fsdp", mask) if mask else block for mask in masks}
    blocks = {0: block}
    for bit in bits:
        blocks.update({mask ^ bit: swap(held, "fsdp", bit) for mask, held in list(blocks.items())})
    return blocks


def spread_near(block, bits, tokens):
    if len(bits) == 2:
        low, high = bits
        half = block.shape[0] // 2
        top, bottom = block[:half], block[half:]
        low_top, high_bottom = swap(top, "fsdp", low), swap(bottom, "fsdp", high)
        far = [swap(low_top, "fsdp", high), swap(high_bottom, "fsdp", low)]
        by_low = [low_top, swap(after(bottom, [low_top], tokens), "fsdp", low)]
        by_high = [swap(after(top, [high_bottom], tokens), "fsdp", high), high_bottom]
        first = [low_top, high_bottom]
        return {0: [block], low: by_low, high: by_high}, {low | high: far}, first
    blocks = {mask: [held] for mask, held in spread(block, bits).items()}
    last = max(blocks)
    near = {mask: held for mask, held in blocks.items() if mask != last}
    return near, {last: blocks[last]}, []


def with_partner(blocks, own=None):
    other = {
        mask ^ 1: [own] if mask == 0 and own is not None else [swap(x, "fsdp", 1) for x in held]
        for mask, held in blocks.items()
    }
    return {**blocks, **other}


def tile_of(size):
    return min(size, 256)


def whole(shape):
    return pl.BlockSpec(shape, lambda *_: (0,) * len(shape))


def gather_body(order, per, count, here, same, other, *refs):
    for matrix, out in enumerate(refs[-MATS:]):
        spot = 0
        for mask in order:
            for sub in range(per):
                away = ((here[0] ^ mask) * per + sub) ^ here[1]
                at = pl.multiple_of(((away >> 1) * MATS + matrix) * count, count)
                out[pl.ds(spot * count, count), :] = jnp.where(
                    (away & 1) == 0, same[pl.ds(at, count), :], other[pl.ds(at, count), :]
                )
                spot += 1


def gather_projector(same, other, here, order, per, tokens):
    rows, kv = same.shape
    rank = 2 * rows // MATS
    return pl.pallas_call(
        functools.partial(gather_body, order, per, rank // (len(order) * per)),
        grid_spec=pltpu.PrefetchScalarGridSpec(
            num_scalar_prefetch=1,
            grid=(1,),
            in_specs=[whole((rows, kv))] * 2
            + [pl.BlockSpec(memory_space=pl.ANY)] * len(tokens),
            out_specs=[whole((rank, kv))] * MATS,
        ),
        out_shape=[jax.ShapeDtypeStruct((rank, kv), same.dtype)] * MATS,
        compiler_params=pltpu.CompilerParams(vmem_limit_bytes=16 * MIB),
        cost_estimate=pl.CostEstimate(flops=0, bytes_accessed=8 * rows * kv, transcendentals=0),
    )(here, same, other, *tokens)


def block_term(block, rows, here, mask, tile):
    pieces = [piece[:, tile] for piece in block]
    left = pieces[0] if len(pieces) == 1 else jnp.concatenate(pieces, axis=0)
    count = left.shape[0]
    start = pl.multiple_of((here[1] ^ mask) * count, count)
    return lax.dot_general(
        left, rows[pl.ds(start, count), :], TRANSPOSED, preferred_element_type=jnp.float32
    )


def regroup(refs, shape):
    refs = list(refs)
    return [[refs.pop(0) for _ in range(length)] for length in shape]


def call_in_vmem(body, here, operands, outputs, flops, tokens=()):
    moved = sum(x.size * x.dtype.itemsize for x in list(operands) + list(outputs))
    vmem = pl.BlockSpec(memory_space=pltpu.VMEM)
    return pl.pallas_call(
        body,
        grid_spec=pltpu.PrefetchScalarGridSpec(
            num_scalar_prefetch=1,
            grid=(),
            in_specs=[vmem] * len(operands) + [pl.BlockSpec(memory_space=pl.ANY)] * len(tokens),
            out_specs=[vmem] * len(outputs),
        ),
        out_shape=outputs,
        compiler_params=pltpu.CompilerParams(vmem_limit_bytes=20 * MIB),
        cost_estimate=pl.CostEstimate(
            flops=int(flops), bytes_accessed=int(moved), transcendentals=0
        ),
    )(here, *operands, *tokens)


def flat(blocks):
    return [piece for block in blocks.values() for piece in block]


def depth(blocks):
    return sum(piece.shape[0] for piece in flat(blocks))


def heads_body(masks, shape, part, pieces, scale, here, *refs):
    groups = regroup(refs[: sum(shape)], shape)
    rows, outs = refs[sum(shape)], refs[-pieces:]
    size = outs[0].shape[0] * len(outs)
    total = None
    for mask, block in zip(masks, groups):
        term = block_term(block, rows, here, mask, pl.ds(part * size, size))
        total = term if total is None else total + term
    for k, out in enumerate(outs):
        count = out.shape[0]
        out[...] = (total[k * count : (k + 1) * count] * scale).astype(out.dtype)


def heads_product(blocks, here, layer_input, part, pieces, dtype, scale, tokens=()):
    half = flat(blocks)[0].shape[1] // 2
    width = layer_input.shape[1]
    shape = [len(block) for block in blocks.values()]
    return call_in_vmem(
        functools.partial(heads_body, list(blocks), shape, part, pieces, scale),
        here,
        flat(blocks) + [layer_input],
        [jax.ShapeDtypeStruct((half // pieces, width), dtype)] * pieces,
        2 * depth(blocks) * half * width,
        tokens,
    )


def product_body(shape, here, *refs):
    groups = regroup(refs[: sum(shape)], shape)
    out = refs[-1]
    total = None
    for block, rows in zip(groups, refs[sum(shape) : -1]):
        pieces = [piece[...] for piece in block]
        left = pieces[0] if len(pieces) == 1 else jnp.concatenate(pieces, axis=0)
        term = lax.dot_general(left, rows[...], TRANSPOSED, preferred_element_type=jnp.float32)
        total = term if total is None else total + term
    out[...] = total


def row_blocks(blocks, width):
    def at(mask, i, here):
        return here[1] ^ mask, 0

    return [
        pl.BlockSpec((depth({mask: block}), width), functools.partial(at, mask))
        for mask, block in blocks.items()
    ]


def add_products(blocks, here, layer_input):
    kv = flat(blocks)[0].shape[1]
    width = layer_input.shape[1]
    tile = tile_of(kv)
    shape = [len(block) for block in blocks.values()]
    return pl.pallas_call(
        functools.partial(product_body, shape),
        grid_spec=pltpu.PrefetchScalarGridSpec(
            num_scalar_prefetch=1,
            grid=(kv // tile,),
            in_specs=[
                pl.BlockSpec((piece.shape[0], tile), lambda i, here: (0, i))
                for piece in flat(blocks)
            ]
            + row_blocks(blocks, width),
            out_specs=pl.BlockSpec((tile, width), lambda i, here: (i, 0)),
        ),
        out_shape=jax.ShapeDtypeStruct((kv, width), jnp.float32),
        compiler_params=pltpu.CompilerParams(vmem_limit_bytes=20 * MIB),
        cost_estimate=pl.CostEstimate(
            flops=2 * depth(blocks) * kv * width,
            bytes_accessed=2 * depth(blocks) * (kv + width) + 4 * kv * width,
            transcendentals=0,
        ),
    )(here, *flat(blocks), *([layer_input] * len(blocks)))


def project_body(masks, shape, scale, here, *refs):
    groups = regroup(refs[: sum(shape)], shape)
    rows, partial, projector, product = refs[sum(shape) : sum(shape) + 4]
    outs = refs[sum(shape) + 4 :]
    size = tile_of(product.shape[0])
    for at in range(0, product.shape[0], size):
        tile = pl.ds(at, size)
        total = partial[tile, :]
        for mask, block in zip(masks, groups):
            total += block_term(block, rows, here, mask, tile)
        product[tile, :] = total.astype(product.dtype)
    apply_body(0, scale, here, projector, product, *outs)


def apply_body(first, scale, here, projector, product, *outs):
    size = outs[0].shape[0] * len(outs)
    term = jnp.dot(
        projector[pl.ds(first, size), :], product[...], preferred_element_type=jnp.float32
    )
    for k, out in enumerate(outs):
        count = out.shape[0]
        out[...] = (term[k * count : (k + 1) * count] * scale).astype(out.dtype)


def project(blocks, here, layer_input, partial, projector, pieces, scale):
    kv, width = partial.shape
    half = projector.shape[0] // 2
    shape = [len(block) for block in blocks.values()]
    product, *sends = call_in_vmem(
        functools.partial(project_body, list(blocks), shape, scale),
        here,
        flat(blocks) + [layer_input, partial, projector],
        [jax.ShapeDtypeStruct((kv, width), jnp.bfloat16)]
        + [jax.ShapeDtypeStruct((half // pieces, width), jnp.bfloat16)] * pieces,
        2 * depth(blocks) * kv * width + 2 * half * kv * width,
    )
    return product, sends


def apply_rest(projector, product, here, pieces, scale):
    half = projector.shape[0] // 2
    kv, width = product.shape
    return call_in_vmem(
        functools.partial(apply_body, half, scale),
        here,
        [projector, product],
        [jax.ShapeDtypeStruct((half // pieces, width), jnp.float32)] * pieces,
        2 * half * kv * width,
    )


def on_device(layer_input, cotangent, candidates, moment_first, moment_second, owners):
    replicas = lax.axis_size("dp")
    members = lax.axis_size("fsdp")
    me_dp = lax.axis_index("dp")
    me_fsdp = lax.axis_index("fsdp")
    dp_bits = bits_of(replicas)
    far_bits = bits_of(members)[1:]
    scale = 1.0 / math.sqrt(layer_input.shape[0] * replicas)
    kv_share = candidates.shape[2] // replicas
    per = members // replicas
    rank_share = moment_first.shape[1]

    order = [0]
    for bit in reversed(dp_bits):
        order = [mask ^ bit for mask in order] + order

    here = jnp.stack([me_dp, me_fsdp]).astype(jnp.int32)

    def owned(value, others, tokens):
        for at, bit in enumerate(dp_bits):
            if at == 1 and others:
                value = after(value, others, tokens)
            other = swap(value, "dp", bit)
            mine = (me_dp & bit) == (owners & bit)
            rows = jnp.repeat(mine, value.shape[0] // MATS)[:, None]
            value = jnp.where(rows, value, other)
        return value

    pieces = max(replicas // 2, 1)
    tokens, tokens_1 = [], []

    near, far, arrived = spread_near(cotangent[0], far_bits, tokens)
    both = jnp.swapaxes(candidates[:, 0], 1, 2).reshape(-1, candidates.shape[2])
    both = owned(both, arrived, tokens)
    later = [piece for mask in far_bits for piece in near.get(mask, ())]
    later = [piece for piece in later if all(piece is not other for other in arrived)]
    blocks = spread(after(both, later + flat(far), tokens), far_bits)
    same = jnp.concatenate([blocks[mask] for mask in sorted(blocks)], axis=0)
    near_all = with_partner(near)
    partial = add_products(near_all, here, layer_input)
    far_all = with_partner(far)
    same = after(same, [partial], tokens)
    projectors = gather_projector(same, swap(same, "fsdp", 1), here, order, per, tokens)
    product, send_0 = project(far_all, here, layer_input, partial, projectors[0], pieces, scale)
    keep_0 = apply_rest(projectors[0], product, here, pieces, scale)
    arrived_0 = [swap(piece, "dp", dp_bits[0]) for piece in send_0]

    def reduced(arrived, keeps, cuts=1):
        for bit in dp_bits[1:]:
            totals = [keep + piece.astype(jnp.float32) for piece, keep in zip(arrived, keeps)]
            half = len(totals) // 2
            sends = [total.astype(jnp.bfloat16) for total in totals[:half]]
            if half == 1:
                sends = jnp.split(sends[0], cuts)
            arrived = [swap(piece, "dp", bit) for piece in sends]
            keeps = totals[half:]
        return keeps[0], arrived

    heads = lax.dot_general(
        cotangent[1], projectors[1], (((1,), (1,)), ((), ())), preferred_element_type=jnp.float32
    ).astype(jnp.bfloat16)
    blocks = spread(heads, far_bits)
    open_0 = reduced(arrived_0, keep_0)
    blocks = with_partner({mask: [held] for mask, held in blocks.items()})
    send_1 = heads_product(blocks, here, layer_input, 0, pieces, jnp.bfloat16, scale, tokens_1)
    keep_1 = heads_product(
        blocks, here, layer_input, 1, pieces, jnp.float32, scale, arrived_0[pieces // 2 :]
    )
    arrived_1 = [swap(piece, "dp", dp_bits[0]) for piece in send_1]

    keep_1, received_1 = reduced(arrived_1, keep_1, CUTS)
    units = [(0, 0, open_0[0], open_0[1][0])]
    rows = rank_share // CUTS
    for cut, piece in enumerate(received_1):
        units.append((1, cut * rows, keep_1[cut * rows : (cut + 1) * rows], piece))
    firsts, seconds, gathered = [], [], []
    for unit, (matrix, start, keep, received) in enumerate(units):
        if unit:
            ahead = gathered[-1][-3 : -1 if unit == 1 else -2]
            received, firsts[-1], *ahead = lax.optimization_barrier((received, firsts[-1], *ahead))
            gathered[-1][-3 : -3 + len(ahead)] = ahead
        projected = keep + received.astype(jnp.float32)
        here_rows = slice(start, start + keep.shape[0])
        first = beta_first * moment_first[matrix, here_rows] + (1.0 - beta_first) * projected
        second = (
            beta_second * moment_second[matrix, here_rows]
            + (1.0 - beta_second) * projected * projected
        )
        direction = (
            first
            / (1.0 - beta_first**STEP)
            / (jnp.sqrt(second / (1.0 - beta_second**STEP)) + epsilon)
        )
        parts = [direction.astype(jnp.bfloat16)]
        for bit in reversed(dp_bits):
            if unit == 0 and bit == dp_bits[0] and len(parts) > 1:
                parts[0], kept = lax.optimization_barrier((parts[0], keep_1))
                units[1:] = [
                    (m, at, kept[at : at + k.shape[0]], piece) for m, at, k, piece in units[1:]
                ]
            parts = [swap(piece, "dp", bit) for piece in parts] + parts
        gathered.append(parts)
        firsts.append(first)
        seconds.append(second)
    values = [None] * MATS
    for (matrix, start, keep, _), parts in zip(units, gathered):
        own = lax.dynamic_slice_in_dim(projectors[matrix], me_dp * kv_share, kv_share, 1)
        own = own.reshape(replicas, rank_share, kv_share)[:, start : start + keep.shape[0]]
        value = lax.dot_general(
            own.reshape(-1, kv_share),
            jnp.concatenate(parts, axis=0),
            TRANSPOSED,
            preferred_element_type=jnp.float32,
        )
        values[matrix] = value if values[matrix] is None else values[matrix] + value
    update = jnp.stack([value.astype(jnp.bfloat16) for value in values])
    return (
        update,
        jnp.concatenate(firsts, axis=0).reshape(moment_first.shape),
        jnp.concatenate(seconds, axis=0).reshape(moment_second.shape),
    )


def solution(mesh):
    placed = (
        P("dp", "fsdp"),
        P(None, ("dp", "fsdp"), None),
        P(None, "dp", None, "fsdp"),
        P(None, "dp", "fsdp"),
        P(None, "dp", "fsdp"),
        P(),
    )
    return jax.shard_map(
        on_device,
        mesh=mesh,
        in_specs=placed,
        out_specs=(P(None, "dp", "fsdp"), P(None, "dp", "fsdp"), P(None, "dp", "fsdp")),
        check_vma=False,
    )
```

```python
import functools
import math

import jax
import jax.numpy as jnp
from jax import lax
from jax.experimental import pallas as pl
from jax.experimental.pallas import tpu as pltpu
from jax.sharding import PartitionSpec as P

MATS = 2
STEP = 10

beta_first = 0.9
beta_second = 0.999
epsilon = 1e-08

TRANSPOSED = (((0,), (0,)), ((), ()))
MIB = 1 << 20


def swap(value, axis, mask):
    size = lax.axis_size(axis)
    return lax.ppermute(value, axis, [(i, i ^ mask) for i in range(size)])


def bits_of(size):
    return [1 << k for k in range(size.bit_length() - 1)]


def after(value, others, tokens):
    corners = [other[:16, :128] for other in others]
    value, *held = lax.optimization_barrier((value, *corners))
    tokens.extend(held)
    return value


def spread(block, bits):
    if len(bits) == 2:
        low, high = bits
        masks = (0, low, high, low | high)
        return {mask: swap(block, "fsdp", mask) if mask else block for mask in masks}
    blocks = {0: block}
    for bit in bits:
        blocks.update({mask ^ bit: swap(held, "fsdp", bit) for mask, held in list(blocks.items())})
    return blocks


def spread_near(block, bits, tokens):
    if len(bits) == 2:
        low, high = bits
        half = block.shape[0] // 2
        top, bottom = block[:half], block[half:]
        low_top, high_bottom = swap(top, "fsdp", low), swap(bottom, "fsdp", high)
        far = [swap(low_top, "fsdp", high), swap(high_bottom, "fsdp", low)]
        by_low = [low_top, swap(after(bottom, [low_top], tokens), "fsdp", low)]
        by_high = [swap(after(top, [high_bottom], tokens), "fsdp", high), high_bottom]
        first = [low_top, high_bottom]
        return {0: [block], low: by_low, high: by_high}, {low | high: far}, first
    blocks = {mask: [held] for mask, held in spread(block, bits).items()}
    last = max(blocks)
    near = {mask: held for mask, held in blocks.items() if mask != last}
    return near, {last: blocks[last]}, []


def with_partner(blocks, own=None):
    other = {
        mask ^ 1: [own] if mask == 0 and own is not None else [swap(x, "fsdp", 1) for x in held]
        for mask, held in blocks.items()
    }
    return {**blocks, **other}


def tile_of(size):
    return min(size, 256)


def whole(shape):
    return pl.BlockSpec(shape, lambda *_: (0,) * len(shape))


def gather_body(order, per, count, here, same, other, *refs):
    for matrix, out in enumerate(refs[-MATS:]):
        spot = 0
        for mask in order:
            for sub in range(per):
                away = ((here[0] ^ mask) * per + sub) ^ here[1]
                at = pl.multiple_of(((away >> 1) * MATS + matrix) * count, count)
                out[pl.ds(spot * count, count), :] = jnp.where(
                    (away & 1) == 0, same[pl.ds(at, count), :], other[pl.ds(at, count), :]
                )
                spot += 1


def gather_projector(same, other, here, order, per, tokens):
    rows, kv = same.shape
    rank = 2 * rows // MATS
    return pl.pallas_call(
        functools.partial(gather_body, order, per, rank // (len(order) * per)),
        grid_spec=pltpu.PrefetchScalarGridSpec(
            num_scalar_prefetch=1,
            grid=(1,),
            in_specs=[whole((rows, kv))] * 2
            + [pl.BlockSpec(memory_space=pl.ANY)] * len(tokens),
            out_specs=[whole((rank, kv))] * MATS,
        ),
        out_shape=[jax.ShapeDtypeStruct((rank, kv), same.dtype)] * MATS,
        compiler_params=pltpu.CompilerParams(vmem_limit_bytes=16 * MIB),
        cost_estimate=pl.CostEstimate(flops=0, bytes_accessed=8 * rows * kv, transcendentals=0),
    )(here, same, other, *tokens)


def block_term(block, rows, here, mask, tile):
    pieces = [piece[:, tile] for piece in block]
    left = pieces[0] if len(pieces) == 1 else jnp.concatenate(pieces, axis=0)
    count = left.shape[0]
    start = pl.multiple_of((here[1] ^ mask) * count, count)
    return lax.dot_general(
        left, rows[pl.ds(start, count), :], TRANSPOSED, preferred_element_type=jnp.float32
    )


def regroup(refs, shape):
    refs = list(refs)
    return [[refs.pop(0) for _ in range(length)] for length in shape]


def call_in_vmem(body, here, operands, outputs, flops, tokens=()):
    moved = sum(x.size * x.dtype.itemsize for x in list(operands) + list(outputs))
    vmem = pl.BlockSpec(memory_space=pltpu.VMEM)
    return pl.pallas_call(
        body,
        grid_spec=pltpu.PrefetchScalarGridSpec(
            num_scalar_prefetch=1,
            grid=(),
            in_specs=[vmem] * len(operands) + [pl.BlockSpec(memory_space=pl.ANY)] * len(tokens),
            out_specs=[vmem] * len(outputs),
        ),
        out_shape=outputs,
        compiler_params=pltpu.CompilerParams(vmem_limit_bytes=20 * MIB),
        cost_estimate=pl.CostEstimate(
            flops=int(flops), bytes_accessed=int(moved), transcendentals=0
        ),
    )(here, *operands, *tokens)


def flat(blocks):
    return [piece for block in blocks.values() for piece in block]


def depth(blocks):
    return sum(piece.shape[0] for piece in flat(blocks))


def heads_body(masks, shape, part, pieces, scale, here, *refs):
    groups = regroup(refs[: sum(shape)], shape)
    rows, outs = refs[sum(shape)], refs[-pieces:]
    size = outs[0].shape[0] * len(outs)
    total = None
    for mask, block in zip(masks, groups):
        term = block_term(block, rows, here, mask, pl.ds(part * size, size))
        total = term if total is None else total + term
    for k, out in enumerate(outs):
        count = out.shape[0]
        out[...] = (total[k * count : (k + 1) * count] * scale).astype(out.dtype)


def heads_product(blocks, here, layer_input, part, pieces, dtype, scale, tokens=()):
    half = flat(blocks)[0].shape[1] // 2
    width = layer_input.shape[1]
    shape = [len(block) for block in blocks.values()]
    return call_in_vmem(
        functools.partial(heads_body, list(blocks), shape, part, pieces, scale),
        here,
        flat(blocks) + [layer_input],
        [jax.ShapeDtypeStruct((half // pieces, width), dtype)] * pieces,
        2 * depth(blocks) * half * width,
        tokens,
    )


def product_body(shape, here, *refs):
    groups = regroup(refs[: sum(shape)], shape)
    out = refs[-1]
    total = None
    for block, rows in zip(groups, refs[sum(shape) : -1]):
        pieces = [piece[...] for piece in block]
        left = pieces[0] if len(pieces) == 1 else jnp.concatenate(pieces, axis=0)
        term = lax.dot_general(left, rows[...], TRANSPOSED, preferred_element_type=jnp.float32)
        total = term if total is None else total + term
    out[...] = total


def row_blocks(blocks, width):
    def at(mask, i, here):
        return here[1] ^ mask, 0

    return [
        pl.BlockSpec((depth({mask: block}), width), functools.partial(at, mask))
        for mask, block in blocks.items()
    ]


def add_products(blocks, here, layer_input):
    kv = flat(blocks)[0].shape[1]
    width = layer_input.shape[1]
    tile = tile_of(kv)
    shape = [len(block) for block in blocks.values()]
    return pl.pallas_call(
        functools.partial(product_body, shape),
        grid_spec=pltpu.PrefetchScalarGridSpec(
            num_scalar_prefetch=1,
            grid=(kv // tile,),
            in_specs=[
                pl.BlockSpec((piece.shape[0], tile), lambda i, here: (0, i))
                for piece in flat(blocks)
            ]
            + row_blocks(blocks, width),
            out_specs=pl.BlockSpec((tile, width), lambda i, here: (i, 0)),
        ),
        out_shape=jax.ShapeDtypeStruct((kv, width), jnp.float32),
        compiler_params=pltpu.CompilerParams(vmem_limit_bytes=20 * MIB),
        cost_estimate=pl.CostEstimate(
            flops=2 * depth(blocks) * kv * width,
            bytes_accessed=2 * depth(blocks) * (kv + width) + 4 * kv * width,
            transcendentals=0,
        ),
    )(here, *flat(blocks), *([layer_input] * len(blocks)))


def project_body(masks, shape, scale, here, *refs):
    groups = regroup(refs[: sum(shape)], shape)
    rows, partial, projector, product = refs[sum(shape) : sum(shape) + 4]
    outs = refs[sum(shape) + 4 :]
    size = tile_of(product.shape[0])
    for at in range(0, product.shape[0], size):
        tile = pl.ds(at, size)
        total = partial[tile, :]
        for mask, block in zip(masks, groups):
            total += block_term(block, rows, here, mask, tile)
        product[tile, :] = total.astype(product.dtype)
    apply_body(0, scale, here, projector, product, *outs)


def apply_body(first, scale, here, projector, product, *outs):
    size = outs[0].shape[0] * len(outs)
    term = jnp.dot(
        projector[pl.ds(first, size), :], product[...], preferred_element_type=jnp.float32
    )
    for k, out in enumerate(outs):
        count = out.shape[0]
        out[...] = (term[k * count : (k + 1) * count] * scale).astype(out.dtype)


def project(blocks, here, layer_input, partial, projector, pieces, scale):
    kv, width = partial.shape
    half = projector.shape[0] // 2
    shape = [len(block) for block in blocks.values()]
    product, *sends = call_in_vmem(
        functools.partial(project_body, list(blocks), shape, scale),
        here,
        flat(blocks) + [layer_input, partial, projector],
        [jax.ShapeDtypeStruct((kv, width), jnp.bfloat16)]
        + [jax.ShapeDtypeStruct((half // pieces, width), jnp.bfloat16)] * pieces,
        2 * depth(blocks) * kv * width + 2 * half * kv * width,
    )
    return product, sends


def apply_rest(projector, product, here, pieces, scale):
    half = projector.shape[0] // 2
    kv, width = product.shape
    return call_in_vmem(
        functools.partial(apply_body, half, scale),
        here,
        [projector, product],
        [jax.ShapeDtypeStruct((half // pieces, width), jnp.float32)] * pieces,
        2 * half * kv * width,
    )


def on_device(layer_input, cotangent, candidates, moment_first, moment_second, owners):
    replicas = lax.axis_size("dp")
    members = lax.axis_size("fsdp")
    me_dp = lax.axis_index("dp")
    me_fsdp = lax.axis_index("fsdp")
    dp_bits = bits_of(replicas)
    far_bits = bits_of(members)[1:]
    scale = 1.0 / math.sqrt(layer_input.shape[0] * replicas)
    kv_share = candidates.shape[2] // replicas
    per = members // replicas

    order = [0]
    for bit in reversed(dp_bits):
        order = [mask ^ bit for mask in order] + order

    here = jnp.stack([me_dp, me_fsdp]).astype(jnp.int32)

    def owned(value, others, tokens):
        for at, bit in enumerate(dp_bits):
            if at == 1 and others:
                value = after(value, others, tokens)
            other = swap(value, "dp", bit)
            mine = (me_dp & bit) == (owners & bit)
            rows = jnp.repeat(mine, value.shape[0] // MATS)[:, None]
            value = jnp.where(rows, value, other)
        return value

    pieces = max(replicas // 2, 1)
    tokens = []

    near, far, arrived = spread_near(cotangent[0], far_bits, tokens)
    both = jnp.swapaxes(candidates[:, 0], 1, 2).reshape(-1, candidates.shape[2])
    both = owned(both, arrived, tokens)
    later = [piece for mask in far_bits for piece in near.get(mask, ())]
    later = [piece for piece in later if all(piece is not other for other in arrived)]
    blocks = spread(after(both, later + flat(far), tokens), far_bits)
    same = jnp.concatenate([blocks[mask] for mask in sorted(blocks)], axis=0)
    near_all = with_partner(near)
    partial = add_products(near_all, here, layer_input)
    far_all = with_partner(far)
    same = after(same, [partial], tokens)
    projectors = gather_projector(same, swap(same, "fsdp", 1), here, order, per, tokens)
    product, send_0 = project(far_all, here, layer_input, partial, projectors[0], pieces, scale)
    keep_0 = apply_rest(projectors[0], product, here, pieces, scale)
    arrived_0 = [swap(piece, "dp", dp_bits[0]) for piece in send_0]

    def reduced(arrived, keeps):
        for bit in dp_bits[1:]:
            totals = [keep + piece.astype(jnp.float32) for piece, keep in zip(arrived, keeps)]
            half = len(totals) // 2
            arrived = [swap(total.astype(jnp.bfloat16), "dp", bit) for total in totals[:half]]
            keeps = totals[half:]
        return keeps[0], arrived[0]

    heads = lax.dot_general(
        cotangent[1], projectors[1], (((1,), (1,)), ((), ())), preferred_element_type=jnp.float32
    ).astype(jnp.bfloat16)
    blocks = spread(heads, far_bits)
    open_0 = reduced(arrived_0, keep_0)
    blocks = with_partner({mask: [held] for mask, held in blocks.items()})
    send_1 = heads_product(blocks, here, layer_input, 0, 1, jnp.bfloat16, scale)
    keep_1 = heads_product(
        blocks, here, layer_input, 1, pieces, jnp.float32, scale, arrived_0[pieces // 2 :]
    )
    arrived_1 = jnp.split(swap(send_1[0], "dp", dp_bits[0]), pieces)

    updates, firsts, seconds, gathered = [], [], [], []
    open_1 = list(reduced(arrived_1, keep_1))
    for matrix, (keep, received) in enumerate((open_0, open_1)):
        if gathered:
            received, firsts[0], *gathered[0][-3:-1] = lax.optimization_barrier(
                (received, firsts[0], *gathered[0][-3:-1])
            )
        projected = keep + received.astype(jnp.float32)
        first = beta_first * moment_first[matrix] + (1.0 - beta_first) * projected
        second = beta_second * moment_second[matrix] + (1.0 - beta_second) * projected * projected
        direction = (
            first
            / (1.0 - beta_first**STEP)
            / (jnp.sqrt(second / (1.0 - beta_second**STEP)) + epsilon)
        )
        parts = [direction.astype(jnp.bfloat16)]
        for bit in reversed(dp_bits):
            if matrix == 0 and bit == dp_bits[0] and len(parts) > 1:
                parts[0], open_1[0] = lax.optimization_barrier((parts[0], open_1[0]))
            parts = [swap(piece, "dp", bit) for piece in parts] + parts
        gathered.append(parts)
        firsts.append(first)
        seconds.append(second)
    for parts, projector in zip(gathered, projectors):
        own = lax.dynamic_slice_in_dim(projector, me_dp * kv_share, kv_share, 1)
        update = lax.dot_general(
            own, jnp.concatenate(parts, axis=0), TRANSPOSED, preferred_element_type=jnp.float32
        )
        updates.append(update.astype(jnp.bfloat16))
    update = jnp.zeros((MATS,) + updates[0].shape, updates[0].dtype)
    for matrix in range(MATS):
        update = lax.dynamic_update_slice(update, updates[matrix][None], (matrix, 0, 0))
    return (update, jnp.stack(firsts), jnp.stack(seconds))


def solution(mesh):
    placed = (
        P("dp", "fsdp"),
        P(None, ("dp", "fsdp"), None),
        P(None, "dp", None, "fsdp"),
        P(None, "dp", "fsdp"),
        P(None, "dp", "fsdp"),
        P(),
    )
    return jax.shard_map(
        on_device,
        mesh=mesh,
        in_specs=placed,
        out_specs=(P(None, "dp", "fsdp"), P(None, "dp", "fsdp"), P(None, "dp", "fsdp")),
        check_vma=False,
    )
```

```python
import functools
import math

import jax
import jax.numpy as jnp
from jax import lax
from jax.experimental import pallas as pl
from jax.experimental.pallas import tpu as pltpu
from jax.sharding import PartitionSpec as P

MATS = 2
STEP = 10

beta_first = 0.9
beta_second = 0.999
epsilon = 1e-08

TRANSPOSED = (((0,), (0,)), ((), ()))
MIB = 1 << 20


def swap(value, axis, mask):
    size = lax.axis_size(axis)
    return lax.ppermute(value, axis, [(i, i ^ mask) for i in range(size)])


def bits_of(size):
    return [1 << k for k in range(size.bit_length() - 1)]


def after(value, others, tokens):
    corners = [other[:16, :128] for other in others]
    value, *held = lax.optimization_barrier((value, *corners))
    tokens.extend(held)
    return value


def spread(block, bits):
    if len(bits) == 2:
        low, high = bits
        masks = (0, low, high, low | high)
        return {mask: swap(block, "fsdp", mask) if mask else block for mask in masks}
    blocks = {0: block}
    for bit in bits:
        blocks.update({mask ^ bit: swap(held, "fsdp", bit) for mask, held in list(blocks.items())})
    return blocks


def spread_near(block, bits, tokens):
    if len(bits) == 2:
        low, high = bits
        half = block.shape[0] // 2
        top, bottom = block[:half], block[half:]
        low_top, high_bottom = swap(top, "fsdp", low), swap(bottom, "fsdp", high)
        far = [swap(low_top, "fsdp", high), swap(high_bottom, "fsdp", low)]
        by_low = [low_top, swap(after(bottom, [low_top], tokens), "fsdp", low)]
        by_high = [swap(after(top, [high_bottom], tokens), "fsdp", high), high_bottom]
        first = [low_top, high_bottom]
        return {0: [block], low: by_low, high: by_high}, {low | high: far}, first
    blocks = {mask: [held] for mask, held in spread(block, bits).items()}
    last = max(blocks)
    near = {mask: held for mask, held in blocks.items() if mask != last}
    return near, {last: blocks[last]}, []


def with_partner(blocks, own=None):
    other = {
        mask ^ 1: [own] if mask == 0 and own is not None else [swap(x, "fsdp", 1) for x in held]
        for mask, held in blocks.items()
    }
    return {**blocks, **other}


def tile_of(size):
    return min(size, 256)


def whole(shape):
    return pl.BlockSpec(shape, lambda *_: (0,) * len(shape))


def gather_body(order, per, count, here, same, other, *refs):
    for matrix, out in enumerate(refs[-MATS:]):
        spot = 0
        for mask in order:
            for sub in range(per):
                away = ((here[0] ^ mask) * per + sub) ^ here[1]
                at = pl.multiple_of(((away >> 1) * MATS + matrix) * count, count)
                out[pl.ds(spot * count, count), :] = jnp.where(
                    (away & 1) == 0, same[pl.ds(at, count), :], other[pl.ds(at, count), :]
                )
                spot += 1


def gather_projector(same, other, here, order, per, tokens):
    rows, kv = same.shape
    rank = 2 * rows // MATS
    return pl.pallas_call(
        functools.partial(gather_body, order, per, rank // (len(order) * per)),
        grid_spec=pltpu.PrefetchScalarGridSpec(
            num_scalar_prefetch=1,
            grid=(1,),
            in_specs=[whole((rows, kv))] * 2
            + [pl.BlockSpec(memory_space=pl.ANY)] * len(tokens),
            out_specs=[whole((rank, kv))] * MATS,
        ),
        out_shape=[jax.ShapeDtypeStruct((rank, kv), same.dtype)] * MATS,
        compiler_params=pltpu.CompilerParams(vmem_limit_bytes=16 * MIB),
        cost_estimate=pl.CostEstimate(flops=0, bytes_accessed=8 * rows * kv, transcendentals=0),
    )(here, same, other, *tokens)


def block_term(block, rows, here, mask, tile):
    pieces = [piece[:, tile] for piece in block]
    left = pieces[0] if len(pieces) == 1 else jnp.concatenate(pieces, axis=0)
    count = left.shape[0]
    start = pl.multiple_of((here[1] ^ mask) * count, count)
    return lax.dot_general(
        left, rows[pl.ds(start, count), :], TRANSPOSED, preferred_element_type=jnp.float32
    )


def regroup(refs, shape):
    refs = list(refs)
    return [[refs.pop(0) for _ in range(length)] for length in shape]


def call_in_vmem(body, here, operands, outputs, flops, tokens=()):
    moved = sum(x.size * x.dtype.itemsize for x in list(operands) + list(outputs))
    vmem = pl.BlockSpec(memory_space=pltpu.VMEM)
    return pl.pallas_call(
        body,
        grid_spec=pltpu.PrefetchScalarGridSpec(
            num_scalar_prefetch=1,
            grid=(),
            in_specs=[vmem] * len(operands) + [pl.BlockSpec(memory_space=pl.ANY)] * len(tokens),
            out_specs=[vmem] * len(outputs),
        ),
        out_shape=outputs,
        compiler_params=pltpu.CompilerParams(vmem_limit_bytes=20 * MIB),
        cost_estimate=pl.CostEstimate(
            flops=int(flops), bytes_accessed=int(moved), transcendentals=0
        ),
    )(here, *operands, *tokens)


def flat(blocks):
    return [piece for block in blocks.values() for piece in block]


def depth(blocks):
    return sum(piece.shape[0] for piece in flat(blocks))


def heads_body(masks, shape, part, pieces, scale, here, *refs):
    groups = regroup(refs[: sum(shape)], shape)
    rows, outs = refs[sum(shape)], refs[-pieces:]
    size = outs[0].shape[0] * len(outs)
    total = None
    for mask, block in zip(masks, groups):
        term = block_term(block, rows, here, mask, pl.ds(part * size, size))
        total = term if total is None else total + term
    for k, out in enumerate(outs):
        count = out.shape[0]
        out[...] = (total[k * count : (k + 1) * count] * scale).astype(out.dtype)


def heads_product(blocks, here, layer_input, part, pieces, dtype, scale, tokens=()):
    half = flat(blocks)[0].shape[1] // 2
    width = layer_input.shape[1]
    shape = [len(block) for block in blocks.values()]
    return call_in_vmem(
        functools.partial(heads_body, list(blocks), shape, part, pieces, scale),
        here,
        flat(blocks) + [layer_input],
        [jax.ShapeDtypeStruct((half // pieces, width), dtype)] * pieces,
        2 * depth(blocks) * half * width,
        tokens,
    )


def product_body(shape, here, *refs):
    groups = regroup(refs[: sum(shape)], shape)
    out = refs[-1]
    total = None
    for block, rows in zip(groups, refs[sum(shape) : -1]):
        pieces = [piece[...] for piece in block]
        left = pieces[0] if len(pieces) == 1 else jnp.concatenate(pieces, axis=0)
        term = lax.dot_general(left, rows[...], TRANSPOSED, preferred_element_type=jnp.float32)
        total = term if total is None else total + term
    out[...] = total


def row_blocks(blocks, width):
    def at(mask, i, here):
        return here[1] ^ mask, 0

    return [
        pl.BlockSpec((depth({mask: block}), width), functools.partial(at, mask))
        for mask, block in blocks.items()
    ]


def add_products(blocks, here, layer_input):
    kv = flat(blocks)[0].shape[1]
    width = layer_input.shape[1]
    tile = tile_of(kv)
    shape = [len(block) for block in blocks.values()]
    return pl.pallas_call(
        functools.partial(product_body, shape),
        grid_spec=pltpu.PrefetchScalarGridSpec(
            num_scalar_prefetch=1,
            grid=(kv // tile,),
            in_specs=[
                pl.BlockSpec((piece.shape[0], tile), lambda i, here: (0, i))
                for piece in flat(blocks)
            ]
            + row_blocks(blocks, width),
            out_specs=pl.BlockSpec((tile, width), lambda i, here: (i, 0)),
        ),
        out_shape=jax.ShapeDtypeStruct((kv, width), jnp.float32),
        compiler_params=pltpu.CompilerParams(vmem_limit_bytes=20 * MIB),
        cost_estimate=pl.CostEstimate(
            flops=2 * depth(blocks) * kv * width,
            bytes_accessed=2 * depth(blocks) * (kv + width) + 4 * kv * width,
            transcendentals=0,
        ),
    )(here, *flat(blocks), *([layer_input] * len(blocks)))


def project_body(masks, shape, scale, here, *refs):
    groups = regroup(refs[: sum(shape)], shape)
    rows, partial, projector, product = refs[sum(shape) : sum(shape) + 4]
    outs = refs[sum(shape) + 4 :]
    size = tile_of(product.shape[0])
    for at in range(0, product.shape[0], size):
        tile = pl.ds(at, size)
        total = partial[tile, :]
        for mask, block in zip(masks, groups):
            total += block_term(block, rows, here, mask, tile)
        product[tile, :] = total.astype(product.dtype)
    apply_body(0, scale, here, projector, product, *outs)


def apply_body(first, scale, here, projector, product, *outs):
    size = outs[0].shape[0] * len(outs)
    term = jnp.dot(
        projector[pl.ds(first, size), :], product[...], preferred_element_type=jnp.float32
    )
    for k, out in enumerate(outs):
        count = out.shape[0]
        out[...] = (term[k * count : (k + 1) * count] * scale).astype(out.dtype)


def project(blocks, here, layer_input, partial, projector, pieces, scale):
    kv, width = partial.shape
    half = projector.shape[0] // 2
    shape = [len(block) for block in blocks.values()]
    product, *sends = call_in_vmem(
        functools.partial(project_body, list(blocks), shape, scale),
        here,
        flat(blocks) + [layer_input, partial, projector],
        [jax.ShapeDtypeStruct((kv, width), jnp.bfloat16)]
        + [jax.ShapeDtypeStruct((half // pieces, width), jnp.bfloat16)] * pieces,
        2 * depth(blocks) * kv * width + 2 * half * kv * width,
    )
    return product, sends


def apply_rest(projector, product, here, pieces, scale):
    half = projector.shape[0] // 2
    kv, width = product.shape
    return call_in_vmem(
        functools.partial(apply_body, half, scale),
        here,
        [projector, product],
        [jax.ShapeDtypeStruct((half // pieces, width), jnp.float32)] * pieces,
        2 * half * kv * width,
    )


def on_device(layer_input, cotangent, candidates, moment_first, moment_second, owners):
    replicas = lax.axis_size("dp")
    members = lax.axis_size("fsdp")
    me_dp = lax.axis_index("dp")
    me_fsdp = lax.axis_index("fsdp")
    dp_bits = bits_of(replicas)
    far_bits = bits_of(members)[1:]
    scale = 1.0 / math.sqrt(layer_input.shape[0] * replicas)
    kv_share = candidates.shape[2] // replicas
    per = members // replicas

    order = [0]
    for bit in reversed(dp_bits):
        order = [mask ^ bit for mask in order] + order

    here = jnp.stack([me_dp, me_fsdp]).astype(jnp.int32)

    def owned(value, others, tokens):
        for at, bit in enumerate(dp_bits):
            if at == 1 and others:
                value = after(value, others, tokens)
            other = swap(value, "dp", bit)
            mine = (me_dp & bit) == (owners & bit)
            rows = jnp.repeat(mine, value.shape[0] // MATS)[:, None]
            value = jnp.where(rows, value, other)
        return value

    pieces = max(replicas // 2, 1)
    tokens = []

    near, far, arrived = spread_near(cotangent[0], far_bits, tokens)
    both = jnp.swapaxes(candidates[:, 0], 1, 2).reshape(-1, candidates.shape[2])
    both = owned(both, arrived, tokens)
    later = [piece for mask in far_bits for piece in near.get(mask, ())]
    later = [piece for piece in later if all(piece is not other for other in arrived)]
    blocks = spread(after(both, later + flat(far), tokens), far_bits)
    same = jnp.concatenate([blocks[mask] for mask in sorted(blocks)], axis=0)
    near_all = with_partner(near)
    partial = add_products(near_all, here, layer_input)
    far_all = with_partner(far)
    same = after(same, [partial], tokens)
    projectors = gather_projector(same, swap(same, "fsdp", 1), here, order, per, tokens)
    product, send_0 = project(far_all, here, layer_input, partial, projectors[0], pieces, scale)
    keep_0 = apply_rest(projectors[0], product, here, pieces, scale)
    arrived_0 = [swap(piece, "dp", dp_bits[0]) for piece in send_0]

    def reduced(arrived, keeps):
        for bit in dp_bits[1:]:
            totals = [keep + piece.astype(jnp.float32) for piece, keep in zip(arrived, keeps)]
            half = len(totals) // 2
            arrived = [swap(total.astype(jnp.bfloat16), "dp", bit) for total in totals[:half]]
            keeps = totals[half:]
        return keeps[0], arrived[0]

    heads = lax.dot_general(
        cotangent[1], projectors[1], (((1,), (1,)), ((), ())), preferred_element_type=jnp.float32
    ).astype(jnp.bfloat16)
    blocks = spread(heads, far_bits)
    open_0 = reduced(arrived_0, keep_0)
    blocks = with_partner({mask: [held] for mask, held in blocks.items()})
    send_1 = heads_product(blocks, here, layer_input, 0, pieces, jnp.bfloat16, scale)
    keep_1 = heads_product(
        blocks, here, layer_input, 1, pieces, jnp.float32, scale, arrived_0[pieces // 2 :]
    )
    arrived_1 = [swap(piece, "dp", dp_bits[0]) for piece in send_1]

    updates, firsts, seconds, gathered = [], [], [], []
    for matrix, (keep, received) in enumerate((open_0, reduced(arrived_1, keep_1))):
        if gathered:
            received, firsts[0], *gathered[0][:-1] = lax.optimization_barrier(
                (received, firsts[0], *gathered[0][:-1])
            )
        projected = keep + received.astype(jnp.float32)
        first = beta_first * moment_first[matrix] + (1.0 - beta_first) * projected
        second = beta_second * moment_second[matrix] + (1.0 - beta_second) * projected * projected
        direction = (
            first
            / (1.0 - beta_first**STEP)
            / (jnp.sqrt(second / (1.0 - beta_second**STEP)) + epsilon)
        )
        parts = [direction.astype(jnp.bfloat16)]
        for bit in reversed(dp_bits):
            parts = [swap(piece, "dp", bit) for piece in parts] + parts
        gathered.append(parts)
        firsts.append(first)
        seconds.append(second)
    for parts, projector in zip(gathered, projectors):
        own = lax.dynamic_slice_in_dim(projector, me_dp * kv_share, kv_share, 1)
        update = lax.dot_general(
            own, jnp.concatenate(parts, axis=0), TRANSPOSED, preferred_element_type=jnp.float32
        )
        updates.append(update.astype(jnp.bfloat16))
    update = jnp.zeros((MATS,) + updates[0].shape, updates[0].dtype)
    for matrix in range(MATS):
        update = lax.dynamic_update_slice(update, updates[matrix][None], (matrix, 0, 0))
    return (update, jnp.stack(firsts), jnp.stack(seconds))


def solution(mesh):
    placed = (
        P("dp", "fsdp"),
        P(None, ("dp", "fsdp"), None),
        P(None, "dp", None, "fsdp"),
        P(None, "dp", "fsdp"),
        P(None, "dp", "fsdp"),
        P(),
    )
    return jax.shard_map(
        on_device,
        mesh=mesh,
        in_specs=placed,
        out_specs=(P(None, "dp", "fsdp"), P(None, "dp", "fsdp"), P(None, "dp", "fsdp")),
        check_vma=False,
    )
```

```python
import functools
import math

import jax
import jax.numpy as jnp
from jax import lax
from jax.experimental import pallas as pl
from jax.experimental.pallas import tpu as pltpu
from jax.sharding import PartitionSpec as P

MATS = 2
STEP = 10

beta_first = 0.9
beta_second = 0.999
epsilon = 1e-08

TRANSPOSED = (((0,), (0,)), ((), ()))
MIB = 1 << 20


def swap(value, axis, mask):
    size = lax.axis_size(axis)
    return lax.ppermute(value, axis, [(i, i ^ mask) for i in range(size)])


def bits_of(size):
    return [1 << k for k in range(size.bit_length() - 1)]


def after(value, others, tokens):
    corners = [other[:16, :128] for other in others]
    value, *held = lax.optimization_barrier((value, *corners))
    tokens.extend(held)
    return value


def spread(block, bits):
    if len(bits) == 2:
        low, high = bits
        masks = (0, low, high, low | high)
        return {mask: swap(block, "fsdp", mask) if mask else block for mask in masks}
    blocks = {0: block}
    for bit in bits:
        blocks.update({mask ^ bit: swap(held, "fsdp", bit) for mask, held in list(blocks.items())})
    return blocks


def spread_near(block, bits, tokens):
    if len(bits) == 2:
        low, high = bits
        half = block.shape[0] // 2
        top, bottom = block[:half], block[half:]
        low_top, high_bottom = swap(top, "fsdp", low), swap(bottom, "fsdp", high)
        far = [swap(low_top, "fsdp", high), swap(high_bottom, "fsdp", low)]
        by_low = [low_top, swap(after(bottom, [low_top], tokens), "fsdp", low)]
        by_high = [swap(after(top, [high_bottom], tokens), "fsdp", high), high_bottom]
        first = [low_top, high_bottom]
        return {0: [block], low: by_low, high: by_high}, {low | high: far}, first
    blocks = {mask: [held] for mask, held in spread(block, bits).items()}
    last = max(blocks)
    near = {mask: held for mask, held in blocks.items() if mask != last}
    return near, {last: blocks[last]}, []


def with_partner(blocks, own=None):
    other = {
        mask ^ 1: [own] if mask == 0 and own is not None else [swap(x, "fsdp", 1) for x in held]
        for mask, held in blocks.items()
    }
    return {**blocks, **other}


def tile_of(size):
    return min(size, 256)


def whole(shape):
    return pl.BlockSpec(shape, lambda *_: (0,) * len(shape))


def gather_body(order, per, count, here, same, other, *refs):
    for matrix, out in enumerate(refs[-MATS:]):
        spot = 0
        for mask in order:
            for sub in range(per):
                away = ((here[0] ^ mask) * per + sub) ^ here[1]
                at = pl.multiple_of(((away >> 1) * MATS + matrix) * count, count)
                out[pl.ds(spot * count, count), :] = jnp.where(
                    (away & 1) == 0, same[pl.ds(at, count), :], other[pl.ds(at, count), :]
                )
                spot += 1


def gather_projector(same, other, here, order, per, tokens):
    rows, kv = same.shape
    rank = 2 * rows // MATS
    return pl.pallas_call(
        functools.partial(gather_body, order, per, rank // (len(order) * per)),
        grid_spec=pltpu.PrefetchScalarGridSpec(
            num_scalar_prefetch=1,
            grid=(1,),
            in_specs=[whole((rows, kv))] * 2
            + [pl.BlockSpec(memory_space=pl.ANY)] * len(tokens),
            out_specs=[whole((rank, kv))] * MATS,
        ),
        out_shape=[jax.ShapeDtypeStruct((rank, kv), same.dtype)] * MATS,
        compiler_params=pltpu.CompilerParams(vmem_limit_bytes=16 * MIB),
        cost_estimate=pl.CostEstimate(flops=0, bytes_accessed=8 * rows * kv, transcendentals=0),
    )(here, same, other, *tokens)


def block_term(block, rows, here, mask, tile):
    pieces = [piece[:, tile] for piece in block]
    left = pieces[0] if len(pieces) == 1 else jnp.concatenate(pieces, axis=0)
    count = left.shape[0]
    start = pl.multiple_of((here[1] ^ mask) * count, count)
    return lax.dot_general(
        left, rows[pl.ds(start, count), :], TRANSPOSED, preferred_element_type=jnp.float32
    )


def regroup(refs, shape):
    refs = list(refs)
    return [[refs.pop(0) for _ in range(length)] for length in shape]


def call_in_vmem(body, here, operands, outputs, flops, tokens=()):
    moved = sum(x.size * x.dtype.itemsize for x in list(operands) + list(outputs))
    vmem = pl.BlockSpec(memory_space=pltpu.VMEM)
    return pl.pallas_call(
        body,
        grid_spec=pltpu.PrefetchScalarGridSpec(
            num_scalar_prefetch=1,
            grid=(),
            in_specs=[vmem] * len(operands) + [pl.BlockSpec(memory_space=pl.ANY)] * len(tokens),
            out_specs=[vmem] * len(outputs),
        ),
        out_shape=outputs,
        compiler_params=pltpu.CompilerParams(vmem_limit_bytes=20 * MIB),
        cost_estimate=pl.CostEstimate(
            flops=int(flops), bytes_accessed=int(moved), transcendentals=0
        ),
    )(here, *operands, *tokens)


def flat(blocks):
    return [piece for block in blocks.values() for piece in block]


def depth(blocks):
    return sum(piece.shape[0] for piece in flat(blocks))


def heads_body(masks, shape, part, pieces, scale, here, *refs):
    groups = regroup(refs[: sum(shape)], shape)
    rows, outs = refs[sum(shape)], refs[-pieces:]
    size = outs[0].shape[0] * len(outs)
    total = None
    for mask, block in zip(masks, groups):
        term = block_term(block, rows, here, mask, pl.ds(part * size, size))
        total = term if total is None else total + term
    for k, out in enumerate(outs):
        count = out.shape[0]
        out[...] = (total[k * count : (k + 1) * count] * scale).astype(out.dtype)


def heads_product(blocks, here, layer_input, part, pieces, dtype, scale, tokens=()):
    half = flat(blocks)[0].shape[1] // 2
    width = layer_input.shape[1]
    shape = [len(block) for block in blocks.values()]
    return call_in_vmem(
        functools.partial(heads_body, list(blocks), shape, part, pieces, scale),
        here,
        flat(blocks) + [layer_input],
        [jax.ShapeDtypeStruct((half // pieces, width), dtype)] * pieces,
        2 * depth(blocks) * half * width,
        tokens,
    )


def product_body(shape, here, *refs):
    groups = regroup(refs[: sum(shape)], shape)
    out = refs[-1]
    total = None
    for block, rows in zip(groups, refs[sum(shape) : -1]):
        pieces = [piece[...] for piece in block]
        left = pieces[0] if len(pieces) == 1 else jnp.concatenate(pieces, axis=0)
        term = lax.dot_general(left, rows[...], TRANSPOSED, preferred_element_type=jnp.float32)
        total = term if total is None else total + term
    out[...] = total


def row_blocks(blocks, width):
    def at(mask, i, here):
        return here[1] ^ mask, 0

    return [
        pl.BlockSpec((depth({mask: block}), width), functools.partial(at, mask))
        for mask, block in blocks.items()
    ]


def add_products(blocks, here, layer_input):
    kv = flat(blocks)[0].shape[1]
    width = layer_input.shape[1]
    tile = tile_of(kv)
    shape = [len(block) for block in blocks.values()]
    return pl.pallas_call(
        functools.partial(product_body, shape),
        grid_spec=pltpu.PrefetchScalarGridSpec(
            num_scalar_prefetch=1,
            grid=(kv // tile,),
            in_specs=[
                pl.BlockSpec((piece.shape[0], tile), lambda i, here: (0, i))
                for piece in flat(blocks)
            ]
            + row_blocks(blocks, width),
            out_specs=pl.BlockSpec((tile, width), lambda i, here: (i, 0)),
        ),
        out_shape=jax.ShapeDtypeStruct((kv, width), jnp.float32),
        compiler_params=pltpu.CompilerParams(vmem_limit_bytes=20 * MIB),
        cost_estimate=pl.CostEstimate(
            flops=2 * depth(blocks) * kv * width,
            bytes_accessed=2 * depth(blocks) * (kv + width) + 4 * kv * width,
            transcendentals=0,
        ),
    )(here, *flat(blocks), *([layer_input] * len(blocks)))


def project_body(masks, shape, scale, here, *refs):
    groups = regroup(refs[: sum(shape)], shape)
    rows, partial, projector, product = refs[sum(shape) : sum(shape) + 4]
    outs = refs[sum(shape) + 4 :]
    size = tile_of(product.shape[0])
    for at in range(0, product.shape[0], size):
        tile = pl.ds(at, size)
        total = partial[tile, :]
        for mask, block in zip(masks, groups):
            total += block_term(block, rows, here, mask, tile)
        product[tile, :] = total.astype(product.dtype)
    apply_body(0, scale, here, projector, product, *outs)


def apply_body(first, scale, here, projector, product, *outs):
    size = outs[0].shape[0] * len(outs)
    term = jnp.dot(
        projector[pl.ds(first, size), :], product[...], preferred_element_type=jnp.float32
    )
    for k, out in enumerate(outs):
        count = out.shape[0]
        out[...] = (term[k * count : (k + 1) * count] * scale).astype(out.dtype)


def project(blocks, here, layer_input, partial, projector, pieces, scale):
    kv, width = partial.shape
    half = projector.shape[0] // 2
    shape = [len(block) for block in blocks.values()]
    product, *sends = call_in_vmem(
        functools.partial(project_body, list(blocks), shape, scale),
        here,
        flat(blocks) + [layer_input, partial, projector],
        [jax.ShapeDtypeStruct((kv, width), jnp.bfloat16)]
        + [jax.ShapeDtypeStruct((half // pieces, width), jnp.bfloat16)] * pieces,
        2 * depth(blocks) * kv * width + 2 * half * kv * width,
    )
    return product, sends


def apply_rest(projector, product, here, pieces, scale):
    half = projector.shape[0] // 2
    kv, width = product.shape
    return call_in_vmem(
        functools.partial(apply_body, half, scale),
        here,
        [projector, product],
        [jax.ShapeDtypeStruct((half // pieces, width), jnp.float32)] * pieces,
        2 * half * kv * width,
    )


def on_device(layer_input, cotangent, candidates, moment_first, moment_second, owners):
    replicas = lax.axis_size("dp")
    members = lax.axis_size("fsdp")
    me_dp = lax.axis_index("dp")
    me_fsdp = lax.axis_index("fsdp")
    dp_bits = bits_of(replicas)
    far_bits = bits_of(members)[1:]
    scale = 1.0 / math.sqrt(layer_input.shape[0] * replicas)
    kv_share = candidates.shape[2] // replicas
    per = members // replicas

    order = [0]
    for bit in reversed(dp_bits):
        order = [mask ^ bit for mask in order] + order

    here = jnp.stack([me_dp, me_fsdp]).astype(jnp.int32)

    def owned(value, others, tokens):
        for at, bit in enumerate(dp_bits):
            if at == 1 and others:
                value = after(value, others, tokens)
            other = swap(value, "dp", bit)
            mine = (me_dp & bit) == (owners & bit)
            rows = jnp.repeat(mine, value.shape[0] // MATS)[:, None]
            value = jnp.where(rows, value, other)
        return value

    pieces = max(replicas // 2, 1)
    tokens = []

    near, far, arrived = spread_near(cotangent[0], far_bits, tokens)
    both = jnp.swapaxes(candidates[:, 0], 1, 2).reshape(-1, candidates.shape[2])
    both = owned(both, arrived, tokens)
    later = [piece for mask in far_bits for piece in near.get(mask, ())]
    later = [piece for piece in later if all(piece is not other for other in arrived)]
    blocks = spread(after(both, later + flat(far), tokens), far_bits)
    same = jnp.concatenate([blocks[mask] for mask in sorted(blocks)], axis=0)
    near_all = with_partner(near)
    partial = add_products(near_all, here, layer_input)
    far_all = with_partner(far)
    same = after(same, [partial], tokens)
    projectors = gather_projector(same, swap(same, "fsdp", 1), here, order, per, tokens)
    product, send_0 = project(far_all, here, layer_input, partial, projectors[0], pieces, scale)
    keep_0 = apply_rest(projectors[0], product, here, pieces, scale)
    arrived_0 = [swap(piece, "dp", dp_bits[0]) for piece in send_0]

    def reduced(arrived, keeps):
        for bit in dp_bits[1:]:
            totals = [keep + piece.astype(jnp.float32) for piece, keep in zip(arrived, keeps)]
            half = len(totals) // 2
            arrived = [swap(total.astype(jnp.bfloat16), "dp", bit) for total in totals[:half]]
            keeps = totals[half:]
        return keeps[0], arrived[0]

    heads = lax.dot_general(
        cotangent[1], projectors[1], (((1,), (1,)), ((), ())), preferred_element_type=jnp.float32
    ).astype(jnp.bfloat16)
    blocks = spread(heads, far_bits)
    open_0 = reduced(arrived_0, keep_0)
    blocks = with_partner({mask: [held] for mask, held in blocks.items()})
    send_1 = heads_product(blocks, here, layer_input, 0, pieces, jnp.bfloat16, scale)
    keep_1 = heads_product(
        blocks, here, layer_input, 1, pieces, jnp.float32, scale, arrived_0[pieces // 2 :]
    )
    arrived_1 = [swap(piece, "dp", dp_bits[0]) for piece in send_1]

    def moments(matrix, keep, received):
        projected = keep + received.astype(jnp.float32)
        return (
            beta_first * moment_first[matrix] + (1.0 - beta_first) * projected,
            beta_second * moment_second[matrix] + (1.0 - beta_second) * projected * projected,
        )

    updates, firsts, seconds, gathered = [], [], [], []
    for matrix, (keep, received) in enumerate((open_0, reduced(arrived_1, keep_1))):
        if gathered:
            received, *gathered[0][-3:-1] = lax.optimization_barrier(
                (received, *gathered[0][-3:-1])
            )
        first, second = moments(matrix, keep, received)
        direction = (
            first
            / (1.0 - beta_first**STEP)
            / (jnp.sqrt(second / (1.0 - beta_second**STEP)) + epsilon)
        ).astype(jnp.bfloat16)
        direction, keep, received = lax.optimization_barrier((direction, keep, received))
        first, second = moments(matrix, keep, received)
        parts = [direction]
        for bit in reversed(dp_bits):
            parts = [swap(piece, "dp", bit) for piece in parts] + parts
        gathered.append(parts)
        firsts.append(first)
        seconds.append(second)
    for parts, projector in zip(gathered, projectors):
        own = lax.dynamic_slice_in_dim(projector, me_dp * kv_share, kv_share, 1)
        update = lax.dot_general(
            own, jnp.concatenate(parts, axis=0), TRANSPOSED, preferred_element_type=jnp.float32
        )
        updates.append(update.astype(jnp.bfloat16))
    update = jnp.zeros((MATS,) + updates[0].shape, updates[0].dtype)
    for matrix in range(MATS):
        update = lax.dynamic_update_slice(update, updates[matrix][None], (matrix, 0, 0))
    return (update, jnp.stack(firsts), jnp.stack(seconds))


def solution(mesh):
    placed = (
        P("dp", "fsdp"),
        P(None, ("dp", "fsdp"), None),
        P(None, "dp", None, "fsdp"),
        P(None, "dp", "fsdp"),
        P(None, "dp", "fsdp"),
        P(),
    )
    return jax.shard_map(
        on_device,
        mesh=mesh,
        in_specs=placed,
        out_specs=(P(None, "dp", "fsdp"), P(None, "dp", "fsdp"), P(None, "dp", "fsdp")),
        check_vma=False,
    )
```

```python
import functools
import math

import jax
import jax.numpy as jnp
from jax import lax
from jax.experimental import pallas as pl
from jax.experimental.pallas import tpu as pltpu
from jax.sharding import PartitionSpec as P

MATS = 2
STEP = 10

beta_first = 0.9
beta_second = 0.999
epsilon = 1e-08

TRANSPOSED = (((0,), (0,)), ((), ()))
MIB = 1 << 20


def swap(value, axis, mask):
    size = lax.axis_size(axis)
    return lax.ppermute(value, axis, [(i, i ^ mask) for i in range(size)])


def bits_of(size):
    return [1 << k for k in range(size.bit_length() - 1)]


def after(value, others, tokens):
    corners = [other[:16, :128] for other in others]
    value, *held = lax.optimization_barrier((value, *corners))
    tokens.extend(held)
    return value


def spread(block, bits):
    if len(bits) == 2:
        low, high = bits
        masks = (0, low, high, low | high)
        return {mask: swap(block, "fsdp", mask) if mask else block for mask in masks}
    blocks = {0: block}
    for bit in bits:
        blocks.update({mask ^ bit: swap(held, "fsdp", bit) for mask, held in list(blocks.items())})
    return blocks


def spread_near(block, bits, tokens):
    if len(bits) == 2:
        low, high = bits
        half = block.shape[0] // 2
        top, bottom = block[:half], block[half:]
        low_top, high_bottom = swap(top, "fsdp", low), swap(bottom, "fsdp", high)
        far = [swap(low_top, "fsdp", high), swap(high_bottom, "fsdp", low)]
        by_low = [low_top, swap(after(bottom, [low_top], tokens), "fsdp", low)]
        by_high = [swap(after(top, [high_bottom], tokens), "fsdp", high), high_bottom]
        first = [low_top, high_bottom]
        return {0: [block], low: by_low, high: by_high}, {low | high: far}, first
    blocks = {mask: [held] for mask, held in spread(block, bits).items()}
    last = max(blocks)
    near = {mask: held for mask, held in blocks.items() if mask != last}
    return near, {last: blocks[last]}, []


def with_partner(blocks, own=None):
    other = {
        mask ^ 1: [own] if mask == 0 and own is not None else [swap(x, "fsdp", 1) for x in held]
        for mask, held in blocks.items()
    }
    return {**blocks, **other}


def tile_of(size):
    return min(size, 256)


def whole(shape):
    return pl.BlockSpec(shape, lambda *_: (0,) * len(shape))


def gather_body(order, per, count, here, same, other, *refs):
    for matrix, out in enumerate(refs[-MATS:]):
        spot = 0
        for mask in order:
            for sub in range(per):
                away = ((here[0] ^ mask) * per + sub) ^ here[1]
                at = pl.multiple_of(((away >> 1) * MATS + matrix) * count, count)
                out[pl.ds(spot * count, count), :] = jnp.where(
                    (away & 1) == 0, same[pl.ds(at, count), :], other[pl.ds(at, count), :]
                )
                spot += 1


def gather_projector(same, other, here, order, per, tokens):
    rows, kv = same.shape
    rank = 2 * rows // MATS
    return pl.pallas_call(
        functools.partial(gather_body, order, per, rank // (len(order) * per)),
        grid_spec=pltpu.PrefetchScalarGridSpec(
            num_scalar_prefetch=1,
            grid=(1,),
            in_specs=[whole((rows, kv))] * 2
            + [pl.BlockSpec(memory_space=pl.ANY)] * len(tokens),
            out_specs=[whole((rank, kv))] * MATS,
        ),
        out_shape=[jax.ShapeDtypeStruct((rank, kv), same.dtype)] * MATS,
        compiler_params=pltpu.CompilerParams(vmem_limit_bytes=16 * MIB),
        cost_estimate=pl.CostEstimate(flops=0, bytes_accessed=8 * rows * kv, transcendentals=0),
    )(here, same, other, *tokens)


def block_term(block, rows, here, mask, tile):
    pieces = [piece[:, tile] for piece in block]
    left = pieces[0] if len(pieces) == 1 else jnp.concatenate(pieces, axis=0)
    count = left.shape[0]
    start = pl.multiple_of((here[1] ^ mask) * count, count)
    return lax.dot_general(
        left, rows[pl.ds(start, count), :], TRANSPOSED, preferred_element_type=jnp.float32
    )


def regroup(refs, shape):
    refs = list(refs)
    return [[refs.pop(0) for _ in range(length)] for length in shape]


def call_in_vmem(body, here, operands, outputs, flops, tokens=()):
    moved = sum(x.size * x.dtype.itemsize for x in list(operands) + list(outputs))
    vmem = pl.BlockSpec(memory_space=pltpu.VMEM)
    return pl.pallas_call(
        body,
        grid_spec=pltpu.PrefetchScalarGridSpec(
            num_scalar_prefetch=1,
            grid=(),
            in_specs=[vmem] * len(operands) + [pl.BlockSpec(memory_space=pl.ANY)] * len(tokens),
            out_specs=[vmem] * len(outputs),
        ),
        out_shape=outputs,
        compiler_params=pltpu.CompilerParams(vmem_limit_bytes=20 * MIB),
        cost_estimate=pl.CostEstimate(
            flops=int(flops), bytes_accessed=int(moved), transcendentals=0
        ),
    )(here, *operands, *tokens)


def flat(blocks):
    return [piece for block in blocks.values() for piece in block]


def depth(blocks):
    return sum(piece.shape[0] for piece in flat(blocks))


def heads_body(masks, shape, part, pieces, scale, here, *refs):
    groups = regroup(refs[: sum(shape)], shape)
    rows, outs = refs[sum(shape)], refs[-pieces:]
    size = outs[0].shape[0] * len(outs)
    total = None
    for mask, block in zip(masks, groups):
        term = block_term(block, rows, here, mask, pl.ds(part * size, size))
        total = term if total is None else total + term
    for k, out in enumerate(outs):
        count = out.shape[0]
        out[...] = (total[k * count : (k + 1) * count] * scale).astype(out.dtype)


def heads_product(blocks, here, layer_input, part, pieces, dtype, scale, tokens=()):
    half = flat(blocks)[0].shape[1] // 2
    width = layer_input.shape[1]
    shape = [len(block) for block in blocks.values()]
    return call_in_vmem(
        functools.partial(heads_body, list(blocks), shape, part, pieces, scale),
        here,
        flat(blocks) + [layer_input],
        [jax.ShapeDtypeStruct((half // pieces, width), dtype)] * pieces,
        2 * depth(blocks) * half * width,
        tokens,
    )


def product_body(shape, here, *refs):
    groups = regroup(refs[: sum(shape)], shape)
    out = refs[-1]
    total = None
    for block, rows in zip(groups, refs[sum(shape) : -1]):
        pieces = [piece[...] for piece in block]
        left = pieces[0] if len(pieces) == 1 else jnp.concatenate(pieces, axis=0)
        term = lax.dot_general(left, rows[...], TRANSPOSED, preferred_element_type=jnp.float32)
        total = term if total is None else total + term
    out[...] = total


def row_blocks(blocks, width):
    def at(mask, i, here):
        return here[1] ^ mask, 0

    return [
        pl.BlockSpec((depth({mask: block}), width), functools.partial(at, mask))
        for mask, block in blocks.items()
    ]


def add_products(blocks, here, layer_input):
    kv = flat(blocks)[0].shape[1]
    width = layer_input.shape[1]
    tile = tile_of(kv)
    shape = [len(block) for block in blocks.values()]
    return pl.pallas_call(
        functools.partial(product_body, shape),
        grid_spec=pltpu.PrefetchScalarGridSpec(
            num_scalar_prefetch=1,
            grid=(kv // tile,),
            in_specs=[
                pl.BlockSpec((piece.shape[0], tile), lambda i, here: (0, i))
                for piece in flat(blocks)
            ]
            + row_blocks(blocks, width),
            out_specs=pl.BlockSpec((tile, width), lambda i, here: (i, 0)),
        ),
        out_shape=jax.ShapeDtypeStruct((kv, width), jnp.float32),
        compiler_params=pltpu.CompilerParams(vmem_limit_bytes=20 * MIB),
        cost_estimate=pl.CostEstimate(
            flops=2 * depth(blocks) * kv * width,
            bytes_accessed=2 * depth(blocks) * (kv + width) + 4 * kv * width,
            transcendentals=0,
        ),
    )(here, *flat(blocks), *([layer_input] * len(blocks)))


def project_body(masks, shape, scale, here, *refs):
    groups = regroup(refs[: sum(shape)], shape)
    rows, partial, projector, product = refs[sum(shape) : sum(shape) + 4]
    outs = refs[sum(shape) + 4 :]
    size = tile_of(product.shape[0])
    for at in range(0, product.shape[0], size):
        tile = pl.ds(at, size)
        total = partial[tile, :]
        for mask, block in zip(masks, groups):
            total += block_term(block, rows, here, mask, tile)
        product[tile, :] = total.astype(product.dtype)
    apply_body(0, scale, here, projector, product, *outs)


def apply_body(first, scale, here, projector, product, *outs):
    size = outs[0].shape[0] * len(outs)
    term = jnp.dot(
        projector[pl.ds(first, size), :], product[...], preferred_element_type=jnp.float32
    )
    for k, out in enumerate(outs):
        count = out.shape[0]
        out[...] = (term[k * count : (k + 1) * count] * scale).astype(out.dtype)


def project(blocks, here, layer_input, partial, projector, pieces, scale):
    kv, width = partial.shape
    half = projector.shape[0] // 2
    shape = [len(block) for block in blocks.values()]
    product, *sends = call_in_vmem(
        functools.partial(project_body, list(blocks), shape, scale),
        here,
        flat(blocks) + [layer_input, partial, projector],
        [jax.ShapeDtypeStruct((kv, width), jnp.bfloat16)]
        + [jax.ShapeDtypeStruct((half // pieces, width), jnp.bfloat16)] * pieces,
        2 * depth(blocks) * kv * width + 2 * half * kv * width,
    )
    return product, sends


def apply_rest(projector, product, here, pieces, scale):
    half = projector.shape[0] // 2
    kv, width = product.shape
    return call_in_vmem(
        functools.partial(apply_body, half, scale),
        here,
        [projector, product],
        [jax.ShapeDtypeStruct((half // pieces, width), jnp.float32)] * pieces,
        2 * half * kv * width,
    )


def on_device(layer_input, cotangent, candidates, moment_first, moment_second, owners):
    replicas = lax.axis_size("dp")
    members = lax.axis_size("fsdp")
    me_dp = lax.axis_index("dp")
    me_fsdp = lax.axis_index("fsdp")
    dp_bits = bits_of(replicas)
    far_bits = bits_of(members)[1:]
    scale = 1.0 / math.sqrt(layer_input.shape[0] * replicas)
    kv_share = candidates.shape[2] // replicas
    per = members // replicas

    order = [0]
    for bit in reversed(dp_bits):
        order = [mask ^ bit for mask in order] + order

    here = jnp.stack([me_dp, me_fsdp]).astype(jnp.int32)

    def owned(value, others, tokens):
        for at, bit in enumerate(dp_bits):
            if at == 1 and others:
                value = after(value, others, tokens)
            other = swap(value, "dp", bit)
            mine = (me_dp & bit) == (owners & bit)
            rows = jnp.repeat(mine, value.shape[0] // MATS)[:, None]
            value = jnp.where(rows, value, other)
        return value

    pieces = max(replicas // 2, 1)
    tokens = []

    near, far, arrived = spread_near(cotangent[0], far_bits, tokens)
    if arrived:
        near[0] = [after(cotangent, arrived, tokens)[0]]
    both = jnp.swapaxes(candidates[:, 0], 1, 2).reshape(-1, candidates.shape[2])
    both = owned(both, arrived, tokens)
    later = [piece for mask in far_bits for piece in near.get(mask, ())]
    later = [piece for piece in later if all(piece is not other for other in arrived)]
    blocks = spread(after(both, later + flat(far), tokens), far_bits)
    same = jnp.concatenate([blocks[mask] for mask in sorted(blocks)], axis=0)
    near_all = with_partner(near)
    partial = add_products(near_all, here, layer_input)
    far_all = with_partner(far)
    same = after(same, [partial], tokens)
    projectors = gather_projector(same, swap(same, "fsdp", 1), here, order, per, tokens)
    product, send_0 = project(far_all, here, layer_input, partial, projectors[0], pieces, scale)
    keep_0 = apply_rest(projectors[0], product, here, pieces, scale)
    arrived_0 = [swap(piece, "dp", dp_bits[0]) for piece in send_0]

    def reduced(arrived, keeps):
        for bit in dp_bits[1:]:
            totals = [keep + piece.astype(jnp.float32) for piece, keep in zip(arrived, keeps)]
            half = len(totals) // 2
            arrived = [swap(total.astype(jnp.bfloat16), "dp", bit) for total in totals[:half]]
            keeps = totals[half:]
        return keeps[0], arrived[0]

    heads = lax.dot_general(
        cotangent[1], projectors[1], (((1,), (1,)), ((), ())), preferred_element_type=jnp.float32
    ).astype(jnp.bfloat16)
    blocks = spread(heads, far_bits)
    open_0 = reduced(arrived_0, keep_0)
    blocks = with_partner({mask: [held] for mask, held in blocks.items()})
    send_1 = heads_product(blocks, here, layer_input, 0, pieces, jnp.bfloat16, scale)
    keep_1 = heads_product(
        blocks, here, layer_input, 1, pieces, jnp.float32, scale, arrived_0[pieces // 2 :]
    )
    arrived_1 = [swap(piece, "dp", dp_bits[0]) for piece in send_1]

    def moments(matrix, keep, received):
        projected = keep + received.astype(jnp.float32)
        return (
            beta_first * moment_first[matrix] + (1.0 - beta_first) * projected,
            beta_second * moment_second[matrix] + (1.0 - beta_second) * projected * projected,
        )

    updates, firsts, seconds, gathered = [], [], [], []
    for matrix, (keep, received) in enumerate((open_0, reduced(arrived_1, keep_1))):
        if gathered:
            received, *gathered[0][-3:-1] = lax.optimization_barrier(
                (received, *gathered[0][-3:-1])
            )
        first, second = moments(matrix, keep, received)
        direction = (
            first
            / (1.0 - beta_first**STEP)
            / (jnp.sqrt(second / (1.0 - beta_second**STEP)) + epsilon)
        ).astype(jnp.bfloat16)
        direction, keep, received = lax.optimization_barrier((direction, keep, received))
        first, second = moments(matrix, keep, received)
        parts = [direction]
        for bit in reversed(dp_bits):
            parts = [swap(piece, "dp", bit) for piece in parts] + parts
        gathered.append(parts)
        firsts.append(first)
        seconds.append(second)
    for parts, projector in zip(gathered, projectors):
        own = lax.dynamic_slice_in_dim(projector, me_dp * kv_share, kv_share, 1)
        update = lax.dot_general(
            own, jnp.concatenate(parts, axis=0), TRANSPOSED, preferred_element_type=jnp.float32
        )
        updates.append(update.astype(jnp.bfloat16))
    update = jnp.zeros((MATS,) + updates[0].shape, updates[0].dtype)
    for matrix in range(MATS):
        update = lax.dynamic_update_slice(update, updates[matrix][None], (matrix, 0, 0))
    return (update, jnp.stack(firsts), jnp.stack(seconds))


def solution(mesh):
    placed = (
        P("dp", "fsdp"),
        P(None, ("dp", "fsdp"), None),
        P(None, "dp", None, "fsdp"),
        P(None, "dp", "fsdp"),
        P(None, "dp", "fsdp"),
        P(),
    )
    return jax.shard_map(
        on_device,
        mesh=mesh,
        in_specs=placed,
        out_specs=(P(None, "dp", "fsdp"), P(None, "dp", "fsdp"), P(None, "dp", "fsdp")),
        check_vma=False,
    )
```

```python
import functools
import math

import jax
import jax.numpy as jnp
from jax import lax
from jax.experimental import pallas as pl
from jax.experimental.pallas import tpu as pltpu
from jax.sharding import PartitionSpec as P

MATS = 2
STEP = 10

beta_first = 0.9
beta_second = 0.999
epsilon = 1e-08

TRANSPOSED = (((0,), (0,)), ((), ()))
MIB = 1 << 20


def swap(value, axis, mask):
    size = lax.axis_size(axis)
    return lax.ppermute(value, axis, [(i, i ^ mask) for i in range(size)])


def bits_of(size):
    return [1 << k for k in range(size.bit_length() - 1)]


def after(value, others, tokens):
    corners = [other[:16, :128] for other in others]
    value, *held = lax.optimization_barrier((value, *corners))
    tokens.extend(held)
    return value


def spread(block, bits):
    if len(bits) == 2:
        low, high = bits
        masks = (0, low, high, low | high)
        return {mask: swap(block, "fsdp", mask) if mask else block for mask in masks}
    blocks = {0: block}
    for bit in bits:
        blocks.update({mask ^ bit: swap(held, "fsdp", bit) for mask, held in list(blocks.items())})
    return blocks


def spread_near(block, bits, tokens):
    if len(bits) == 2:
        low, high = bits
        half = block.shape[0] // 2
        top, bottom = block[:half], block[half:]
        low_top, high_bottom = swap(top, "fsdp", low), swap(bottom, "fsdp", high)
        far = [swap(low_top, "fsdp", high), swap(high_bottom, "fsdp", low)]
        by_low = [low_top, swap(after(bottom, [low_top], tokens), "fsdp", low)]
        by_high = [swap(after(top, [high_bottom], tokens), "fsdp", high), high_bottom]
        first = [low_top, high_bottom]
        return {0: [block], low: by_low, high: by_high}, {low | high: far}, first
    blocks = {mask: [held] for mask, held in spread(block, bits).items()}
    last = max(blocks)
    near = {mask: held for mask, held in blocks.items() if mask != last}
    return near, {last: blocks[last]}, []


def with_partner(blocks, own=None):
    other = {
        mask ^ 1: [own] if mask == 0 and own is not None else [swap(x, "fsdp", 1) for x in held]
        for mask, held in blocks.items()
    }
    return {**blocks, **other}


def tile_of(size):
    return min(size, 256)


def whole(shape):
    return pl.BlockSpec(shape, lambda *_: (0,) * len(shape))


def gather_body(order, per, count, here, same, other, *refs):
    for matrix, out in enumerate(refs[-MATS:]):
        spot = 0
        for mask in order:
            for sub in range(per):
                away = ((here[0] ^ mask) * per + sub) ^ here[1]
                at = pl.multiple_of(((away >> 1) * MATS + matrix) * count, count)
                out[pl.ds(spot * count, count), :] = jnp.where(
                    (away & 1) == 0, same[pl.ds(at, count), :], other[pl.ds(at, count), :]
                )
                spot += 1


def gather_projector(same, other, here, order, per, tokens):
    rows, kv = same.shape
    rank = 2 * rows // MATS
    return pl.pallas_call(
        functools.partial(gather_body, order, per, rank // (len(order) * per)),
        grid_spec=pltpu.PrefetchScalarGridSpec(
            num_scalar_prefetch=1,
            grid=(1,),
            in_specs=[whole((rows, kv))] * 2
            + [pl.BlockSpec(memory_space=pl.ANY)] * len(tokens),
            out_specs=[whole((rank, kv))] * MATS,
        ),
        out_shape=[jax.ShapeDtypeStruct((rank, kv), same.dtype)] * MATS,
        compiler_params=pltpu.CompilerParams(vmem_limit_bytes=16 * MIB),
        cost_estimate=pl.CostEstimate(flops=0, bytes_accessed=8 * rows * kv, transcendentals=0),
    )(here, same, other, *tokens)


def block_term(block, rows, here, mask, tile):
    pieces = [piece[:, tile] for piece in block]
    left = pieces[0] if len(pieces) == 1 else jnp.concatenate(pieces, axis=0)
    count = left.shape[0]
    start = pl.multiple_of((here[1] ^ mask) * count, count)
    return lax.dot_general(
        left, rows[pl.ds(start, count), :], TRANSPOSED, preferred_element_type=jnp.float32
    )


def regroup(refs, shape):
    refs = list(refs)
    return [[refs.pop(0) for _ in range(length)] for length in shape]


def call_in_vmem(body, here, operands, outputs, flops, tokens=()):
    moved = sum(x.size * x.dtype.itemsize for x in list(operands) + list(outputs))
    vmem = pl.BlockSpec(memory_space=pltpu.VMEM)
    return pl.pallas_call(
        body,
        grid_spec=pltpu.PrefetchScalarGridSpec(
            num_scalar_prefetch=1,
            grid=(),
            in_specs=[vmem] * len(operands) + [pl.BlockSpec(memory_space=pl.ANY)] * len(tokens),
            out_specs=[vmem] * len(outputs),
        ),
        out_shape=outputs,
        compiler_params=pltpu.CompilerParams(vmem_limit_bytes=20 * MIB),
        cost_estimate=pl.CostEstimate(
            flops=int(flops), bytes_accessed=int(moved), transcendentals=0
        ),
    )(here, *operands, *tokens)


def flat(blocks):
    return [piece for block in blocks.values() for piece in block]


def depth(blocks):
    return sum(piece.shape[0] for piece in flat(blocks))


def heads_body(masks, shape, part, pieces, scale, here, *refs):
    groups = regroup(refs[: sum(shape)], shape)
    rows, outs = refs[sum(shape)], refs[-pieces:]
    size = outs[0].shape[0] * len(outs)
    total = None
    for mask, block in zip(masks, groups):
        term = block_term(block, rows, here, mask, pl.ds(part * size, size))
        total = term if total is None else total + term
    for k, out in enumerate(outs):
        count = out.shape[0]
        out[...] = (total[k * count : (k + 1) * count] * scale).astype(out.dtype)


def heads_product(blocks, here, layer_input, part, pieces, dtype, scale, tokens=()):
    half = flat(blocks)[0].shape[1] // 2
    width = layer_input.shape[1]
    shape = [len(block) for block in blocks.values()]
    return call_in_vmem(
        functools.partial(heads_body, list(blocks), shape, part, pieces, scale),
        here,
        flat(blocks) + [layer_input],
        [jax.ShapeDtypeStruct((half // pieces, width), dtype)] * pieces,
        2 * depth(blocks) * half * width,
        tokens,
    )


def product_body(shape, here, *refs):
    groups = regroup(refs[: sum(shape)], shape)
    out = refs[-1]
    total = None
    for block, rows in zip(groups, refs[sum(shape) : -1]):
        pieces = [piece[...] for piece in block]
        left = pieces[0] if len(pieces) == 1 else jnp.concatenate(pieces, axis=0)
        term = lax.dot_general(left, rows[...], TRANSPOSED, preferred_element_type=jnp.float32)
        total = term if total is None else total + term
    out[...] = total


def row_blocks(blocks, width):
    def at(mask, i, here):
        return here[1] ^ mask, 0

    return [
        pl.BlockSpec((depth({mask: block}), width), functools.partial(at, mask))
        for mask, block in blocks.items()
    ]


def add_products(blocks, here, layer_input):
    kv = flat(blocks)[0].shape[1]
    width = layer_input.shape[1]
    tile = tile_of(kv)
    shape = [len(block) for block in blocks.values()]
    return pl.pallas_call(
        functools.partial(product_body, shape),
        grid_spec=pltpu.PrefetchScalarGridSpec(
            num_scalar_prefetch=1,
            grid=(kv // tile,),
            in_specs=[
                pl.BlockSpec((piece.shape[0], tile), lambda i, here: (0, i))
                for piece in flat(blocks)
            ]
            + row_blocks(blocks, width),
            out_specs=pl.BlockSpec((tile, width), lambda i, here: (i, 0)),
        ),
        out_shape=jax.ShapeDtypeStruct((kv, width), jnp.float32),
        compiler_params=pltpu.CompilerParams(vmem_limit_bytes=20 * MIB),
        cost_estimate=pl.CostEstimate(
            flops=2 * depth(blocks) * kv * width,
            bytes_accessed=2 * depth(blocks) * (kv + width) + 4 * kv * width,
            transcendentals=0,
        ),
    )(here, *flat(blocks), *([layer_input] * len(blocks)))


def project_body(masks, shape, scale, here, *refs):
    groups = regroup(refs[: sum(shape)], shape)
    rows, partial, projector, product = refs[sum(shape) : sum(shape) + 4]
    outs = refs[sum(shape) + 4 :]
    size = tile_of(product.shape[0])
    for at in range(0, product.shape[0], size):
        tile = pl.ds(at, size)
        total = partial[tile, :]
        for mask, block in zip(masks, groups):
            total += block_term(block, rows, here, mask, tile)
        product[tile, :] = total.astype(product.dtype)
    apply_body(0, scale, here, projector, product, *outs)


def apply_body(first, scale, here, projector, product, *outs):
    size = outs[0].shape[0] * len(outs)
    term = jnp.dot(
        projector[pl.ds(first, size), :], product[...], preferred_element_type=jnp.float32
    )
    for k, out in enumerate(outs):
        count = out.shape[0]
        out[...] = (term[k * count : (k + 1) * count] * scale).astype(out.dtype)


def project(blocks, here, layer_input, partial, projector, pieces, scale):
    kv, width = partial.shape
    half = projector.shape[0] // 2
    shape = [len(block) for block in blocks.values()]
    product, *sends = call_in_vmem(
        functools.partial(project_body, list(blocks), shape, scale),
        here,
        flat(blocks) + [layer_input, partial, projector],
        [jax.ShapeDtypeStruct((kv, width), jnp.bfloat16)]
        + [jax.ShapeDtypeStruct((half // pieces, width), jnp.bfloat16)] * pieces,
        2 * depth(blocks) * kv * width + 2 * half * kv * width,
    )
    return product, sends


def apply_rest(projector, product, here, pieces, scale):
    half = projector.shape[0] // 2
    kv, width = product.shape
    return call_in_vmem(
        functools.partial(apply_body, half, scale),
        here,
        [projector, product],
        [jax.ShapeDtypeStruct((half // pieces, width), jnp.float32)] * pieces,
        2 * half * kv * width,
    )


def on_device(layer_input, cotangent, candidates, moment_first, moment_second, owners):
    replicas = lax.axis_size("dp")
    members = lax.axis_size("fsdp")
    me_dp = lax.axis_index("dp")
    me_fsdp = lax.axis_index("fsdp")
    dp_bits = bits_of(replicas)
    far_bits = bits_of(members)[1:]
    scale = 1.0 / math.sqrt(layer_input.shape[0] * replicas)
    kv_share = candidates.shape[2] // replicas
    per = members // replicas

    order = [0]
    for bit in reversed(dp_bits):
        order = [mask ^ bit for mask in order] + order

    here = jnp.stack([me_dp, me_fsdp]).astype(jnp.int32)

    def owned(value, others, tokens):
        for at, bit in enumerate(dp_bits):
            if at == 1 and others:
                value = after(value, others, tokens)
            other = swap(value, "dp", bit)
            mine = (me_dp & bit) == (owners & bit)
            rows = jnp.repeat(mine, value.shape[0] // MATS)[:, None]
            value = jnp.where(rows, value, other)
        return value

    pieces = max(replicas // 2, 1)
    tokens = []

    near, far, arrived = spread_near(cotangent[0], far_bits, tokens)
    if arrived:
        near[0] = [after(cotangent, arrived, tokens)[0]]
    both = jnp.swapaxes(candidates[:, 0], 1, 2).reshape(-1, candidates.shape[2])
    both = owned(both, arrived, tokens)
    blocks = spread(after(both, flat(far), tokens), far_bits)
    same = jnp.concatenate([blocks[mask] for mask in sorted(blocks)], axis=0)
    near_all = with_partner(near)
    partial = add_products(near_all, here, layer_input)
    far_all = with_partner(far)
    same = after(same, [partial], tokens)
    projectors = gather_projector(same, swap(same, "fsdp", 1), here, order, per, tokens)
    product, send_0 = project(far_all, here, layer_input, partial, projectors[0], pieces, scale)
    keep_0 = apply_rest(projectors[0], product, here, pieces, scale)
    arrived_0 = [swap(piece, "dp", dp_bits[0]) for piece in send_0]

    def reduced(arrived, keeps):
        for bit in dp_bits[1:]:
            totals = [keep + piece.astype(jnp.float32) for piece, keep in zip(arrived, keeps)]
            half = len(totals) // 2
            arrived = [swap(total.astype(jnp.bfloat16), "dp", bit) for total in totals[:half]]
            keeps = totals[half:]
        return keeps[0], arrived[0]

    heads = lax.dot_general(
        cotangent[1], projectors[1], (((1,), (1,)), ((), ())), preferred_element_type=jnp.float32
    ).astype(jnp.bfloat16)
    blocks = spread(heads, far_bits)
    open_0 = reduced(arrived_0, keep_0)
    blocks = with_partner({mask: [held] for mask, held in blocks.items()})
    send_1 = heads_product(blocks, here, layer_input, 0, pieces, jnp.bfloat16, scale)
    keep_1 = heads_product(
        blocks, here, layer_input, 1, pieces, jnp.float32, scale, arrived_0[pieces // 2 :]
    )
    arrived_1 = [swap(piece, "dp", dp_bits[0]) for piece in send_1]

    def moments(matrix, keep, received):
        projected = keep + received.astype(jnp.float32)
        return (
            beta_first * moment_first[matrix] + (1.0 - beta_first) * projected,
            beta_second * moment_second[matrix] + (1.0 - beta_second) * projected * projected,
        )

    updates, firsts, seconds, gathered = [], [], [], []
    for matrix, (keep, received) in enumerate((open_0, reduced(arrived_1, keep_1))):
        if gathered:
            received, *gathered[0][-3:-1] = lax.optimization_barrier(
                (received, *gathered[0][-3:-1])
            )
        first, second = moments(matrix, keep, received)
        direction = (
            first
            / (1.0 - beta_first**STEP)
            / (jnp.sqrt(second / (1.0 - beta_second**STEP)) + epsilon)
        ).astype(jnp.bfloat16)
        direction, keep, received = lax.optimization_barrier((direction, keep, received))
        first, second = moments(matrix, keep, received)
        parts = [direction]
        for bit in reversed(dp_bits):
            parts = [swap(piece, "dp", bit) for piece in parts] + parts
        gathered.append(parts)
        firsts.append(first)
        seconds.append(second)
    for parts, projector in zip(gathered, projectors):
        own = lax.dynamic_slice_in_dim(projector, me_dp * kv_share, kv_share, 1)
        update = lax.dot_general(
            own, jnp.concatenate(parts, axis=0), TRANSPOSED, preferred_element_type=jnp.float32
        )
        updates.append(update.astype(jnp.bfloat16))
    update = jnp.zeros((MATS,) + updates[0].shape, updates[0].dtype)
    for matrix in range(MATS):
        update = lax.dynamic_update_slice(update, updates[matrix][None], (matrix, 0, 0))
    return (update, jnp.stack(firsts), jnp.stack(seconds))


def solution(mesh):
    placed = (
        P("dp", "fsdp"),
        P(None, ("dp", "fsdp"), None),
        P(None, "dp", None, "fsdp"),
        P(None, "dp", "fsdp"),
        P(None, "dp", "fsdp"),
        P(),
    )
    return jax.shard_map(
        on_device,
        mesh=mesh,
        in_specs=placed,
        out_specs=(P(None, "dp", "fsdp"), P(None, "dp", "fsdp"), P(None, "dp", "fsdp")),
        check_vma=False,
    )
```
